32 devices in a mesh: gy: 4 (over y, core), gz: 8 (over z, x).
Axes of the slice: x: 2, y: 2, z: 4, core: 2. Of those that a mesh axis runs over, the one named last changes fastest.
Arguments:
- fields: float32 [3, 132, 64, 1024], P(None, None, 'gy', 'gz'), may hold values from -25 to 25
Outputs:
- enstrophy: float32 [128, 64, 1024], P(None, 'gy', 'gz')
- strain_rate: float32 [128, 64, 1024], P(None, 'gy', 'gz')
- factor: float32 [128, 128], replicated
The draws below stay inside these ranges and needn't reach their ends.
All inputs are finite; a program needn't handle non-finite values.
Results may differ from the reference program's by a relative error of at most 0.0003.
Values sent between devices are 32-bit elements; how exact they have to be, the bound alone decides.
No kernel may reach another device: no remote copies, remote signals or barrier semaphores. Data moves between devices by JAX's collectives and lax.ppermute only.
A program may use at most 64 MiB of HBM per device.

```python
import jax
import jax.numpy as jnp
from jax import lax

X = 128
NY = 64
NZ = 1024


def draw_fields(key, part):
    key_base = jax.random.fold_in(key, 11)
    key_rough = jax.random.fold_in(key, 12)
    array_shape = (3, X + 4, NY, NZ)
    baseline = jax.random.truncated_normal(key_base, -4.0, 4.0, array_shape, jnp.float32)
    roughness = jnp.exp(jax.random.uniform(key_rough, array_shape, jnp.float32, -0.7, 0.7))
    y_position = jnp.arange(NY, dtype=jnp.float32) / max(NY - 1, 1)
    z_position = jnp.arange(NZ, dtype=jnp.float32) / max(NZ - 1, 1)
    envelope = jnp.sqrt((1.0 + 2.0 * y_position)[:, None] * (1.0 + 2.0 * z_position)[None, :])
    values = baseline * roughness * envelope
    return values


def setup_inputs(seed: int = 0) -> dict:
    seeds = jax.random.split(jax.random.key(seed), 2)
    return {
        "fields": draw_fields(jax.random.fold_in(seeds[1], 71), 0),
    }


def stencil(minus_two, minus_one, plus_one, plus_two):
    return (minus_two - 8.0 * minus_one + 8.0 * plus_one - plus_two) / 12.0

def periodic(values, axis_number):
    return stencil(jnp.roll(values, 2, axis_number), jnp.roll(values, 1, axis_number), jnp.roll(values, -1, axis_number), jnp.roll(values, -2, axis_number))

def invariants(along_x, along_y, along_z):
    gradient = (along_x, along_y, along_z)
    strain_rate = gradient[0][0] * gradient[0][0] + gradient[1][1] * gradient[1][1] + gradient[2][2] * gradient[2][2]
    enstrophy = jnp.zeros_like(strain_rate)
    for source_axis, target_axis in ((0, 1), (0, 2), (1, 2)):
        rotation = gradient[source_axis][target_axis] - gradient[target_axis][source_axis]
        shearing = gradient[source_axis][target_axis] + gradient[target_axis][source_axis]
        enstrophy = enstrophy + 0.5 * rotation * rotation
        strain_rate = strain_rate + 0.5 * shearing * shearing
    return (enstrophy, strain_rate)

def reference(fields):
    per_block = 8

    def one_block(block_index):
        first_plane = (block_index * per_block).astype(jnp.int32)
        slab_planes = lax.dynamic_slice_in_dim(fields, first_plane, per_block + 4, 1)
        centre = slab_planes[:, 2:per_block + 2]
        along_x = stencil(slab_planes[:, 0:per_block], slab_planes[:, 1:per_block + 1], slab_planes[:, 3:per_block + 3], slab_planes[:, 4:per_block + 4])
        along_y = periodic(centre, 2)
        along_z = periodic(centre, 3)
        return invariants(along_x, along_y, along_z)
    enstrophy, strain_rate = lax.map(one_block, jnp.arange(X // per_block, dtype=jnp.int32))
    enstrophy = enstrophy.reshape(X, NY, NZ)
    strain_rate = strain_rate.reshape(X, NY, NZ)
    cell_count = NY * NZ
    matrices = (fields[0, 2:X + 2].reshape(X, cell_count), fields[1, 2:X + 2].reshape(X, cell_count), fields[2, 2:X + 2].reshape(X, cell_count), enstrophy.reshape(X, cell_count), strain_rate.reshape(X, cell_count))
    cross = jnp.zeros((X, X), jnp.float32)
    for matrix in matrices:
        gram = jnp.dot(matrix.astype(jnp.float32), matrix.T.astype(jnp.float32), precision=lax.Precision.HIGHEST, preferred_element_type=jnp.float32)
        mean_square = jnp.sum(matrix * matrix) / (X * cell_count)
        cross = cross + gram / (5.0 * cell_count * (mean_square + 1e-06))
    factor = jnp.linalg.cholesky(cross)
    return (enstrophy, strain_rate, factor)
```

```python
import jax
import jax.numpy as jnp
from jax import lax
from jax.sharding import PartitionSpec as P


def with_halo(cells, sides, width):
    for axis, dim in sides:
        count = lax.axis_size(axis)
        head = lax.slice_in_dim(cells, 0, width, axis=dim)
        tail = lax.slice_in_dim(cells, cells.shape[dim] - width, cells.shape[dim], axis=dim)
        cells = jnp.concatenate(
            [
                lax.ppermute(tail, axis, [(i, (i + 1) % count) for i in range(count)]),
                cells,
                lax.ppermute(head, axis, [((i + 1) % count, i) for i in range(count)]),
            ],
            axis=dim,
        )
    return cells


def butterfly_sum(values, axes):
    for axis in axes:
        count = lax.axis_size(axis)
        if count & (count - 1):
            values = lax.psum(values, axis)
            continue
        step = 1
        while step < count:
            values = values + lax.ppermute(values, axis, [(i, i ^ step) for i in range(count)])
            step *= 2
    return values


def stencil(minus_two, minus_one, plus_one, plus_two):
    return (minus_two - 8.0 * minus_one + 8.0 * plus_one - plus_two) / 12.0


def invariants(along_x, along_y, along_z):
    gradient = (along_x, along_y, along_z)
    strain_rate = (
        gradient[0][0] * gradient[0][0]
        + gradient[1][1] * gradient[1][1]
        + gradient[2][2] * gradient[2][2]
    )
    enstrophy = jnp.zeros_like(strain_rate)
    for source_axis, target_axis in ((0, 1), (0, 2), (1, 2)):
        rotation = gradient[source_axis][target_axis] - gradient[target_axis][source_axis]
        shearing = gradient[source_axis][target_axis] + gradient[target_axis][source_axis]
        enstrophy = enstrophy + 0.5 * rotation * rotation
        strain_rate = strain_rate + 0.5 * shearing * shearing
    return (enstrophy, strain_rate)


def per_device(fields):
    planes = fields.shape[1] - 4
    rows_y = fields.shape[2]
    cols_z = fields.shape[3]
    padded = with_halo(fields, (("gy", 2), ("gz", 3)), 2)
    inner = padded[:, :, 2 : rows_y + 2, 2 : cols_z + 2]
    along_x = stencil(
        inner[:, 0:planes],
        inner[:, 1 : planes + 1],
        inner[:, 3 : planes + 3],
        inner[:, 4 : planes + 4],
    )
    middle = padded[:, 2 : planes + 2]
    along_y = stencil(
        middle[:, :, 0:rows_y, 2 : cols_z + 2],
        middle[:, :, 1 : rows_y + 1, 2 : cols_z + 2],
        middle[:, :, 3 : rows_y + 3, 2 : cols_z + 2],
        middle[:, :, 4 : rows_y + 4, 2 : cols_z + 2],
    )
    along_z = stencil(
        middle[:, :, 2 : rows_y + 2, 0:cols_z],
        middle[:, :, 2 : rows_y + 2, 1 : cols_z + 1],
        middle[:, :, 2 : rows_y + 2, 3 : cols_z + 3],
        middle[:, :, 2 : rows_y + 2, 4 : cols_z + 4],
    )
    enstrophy, strain_rate = invariants(along_x, along_y, along_z)
    cells = rows_y * cols_z
    stacked = jnp.concatenate(
        [
            fields[:, 2 : planes + 2].reshape(3, planes, cells),
            enstrophy.reshape(1, planes, cells),
            strain_rate.reshape(1, planes, cells),
        ],
        axis=0,
    )
    local_grams = jnp.einsum(
        "fxc,fyc->fxy",
        stacked,
        stacked,
        precision=lax.Precision.HIGHEST,
        preferred_element_type=jnp.float32,
    )
    total_cells = cells * lax.axis_size("gy") * lax.axis_size("gz")
    grams = butterfly_sum(local_grams, ("gy", "gz"))
    squares = jnp.trace(grams, axis1=1, axis2=2)
    denominators = 5.0 * total_cells * (squares / (planes * total_cells) + 1e-06)
    cross = jnp.sum(grams / denominators[:, None, None], axis=0)
    factor = jnp.linalg.cholesky(cross)
    return (enstrophy, strain_rate, factor)


def solution(mesh):
    return jax.shard_map(
        per_device,
        mesh=mesh,
        in_specs=(P(None, None, "gy", "gz"),),
        out_specs=(P(None, "gy", "gz"), P(None, "gy", "gz"), P()),
        check_vma=False,
    )
```

```python
import functools

import jax
import jax.numpy as jnp
from jax import lax
from jax.experimental import pallas as pl
from jax.experimental.pallas import tpu as pltpu
from jax.sharding import PartitionSpec as P

TILE = 16
VMEM = pl.BlockSpec(memory_space=pltpu.VMEM)
DIMS_NT = (((1,), (1,)), ((), ()))


def params(**more):
    return pltpu.CompilerParams(vmem_limit_bytes=32 * 1024 * 1024, **more)


def lanes(shape):
    return lax.broadcasted_iota(jnp.int32, shape, 1)


def split(values):
    high = values.astype(jnp.bfloat16)
    low = (values - high.astype(jnp.float32)).astype(jnp.bfloat16)
    return high, low


def gram_of(product):
    size = product.shape[0]
    mixed = product[:, size:]
    return product[:, :size] + (mixed + mixed.T)


def halves(size):
    row = lax.broadcasted_iota(jnp.int32, (size, size), 0)
    col = lax.broadcasted_iota(jnp.int32, (size, size), 1)
    return row, col


def pack_pair(first, second):
    row, col = halves(first.shape[0])
    return jnp.where(row >= col, first, second)


def diagonal(matrix):
    row, col = halves(matrix.shape[0])
    return jnp.sum(jnp.where(row == col, matrix, 0.0), axis=0, keepdims=True)


def faces_kernel(rows, planes, fields, near, far, behind, ahead):
    odd = lax.axis_index("gy") % 2
    size = fields.shape[2]
    near_row = (1 - odd) * (rows - 2)
    far_row = odd * (rows - 2)
    for c in range(3):
        for layer in range(2):
            near[c, layer] = fields[c, pl.ds(2 * rows + near_row + layer, planes, stride=rows), :]
            far[c, layer] = fields[c, pl.ds(2 * rows + far_row + layer, planes, stride=rows), :]
    lane = lanes((TILE, size))

    @pl.loop(0, planes // TILE)
    def _(t):
        tail = jnp.zeros((TILE, size), jnp.float32)
        head = jnp.zeros((TILE, size), jnp.float32)
        for c in range(3):
            for y in range(rows):
                k = c * rows + y
                cells = fields[c, pl.ds((2 + t * TILE) * rows + y, TILE, stride=rows), :]
                turned = pltpu.roll(cells, (2 * k + 2) % size, 1)
                tail = jnp.where((lane == 2 * k) | (lane == 2 * k + 1), turned, tail)
                head = jnp.where((lane == 2 * k + 2) | (lane == 2 * k + 3), turned, head)
        at = pl.ds(pl.multiple_of(t * TILE, TILE), TILE)
        ahead[at, :] = tail
        behind[at, :] = head


def invariants_of(fields, left, right, t, y, rows, row_at):
    size = fields.shape[2]
    lane = lanes((TILE, size))
    first = 2 + t * TILE
    at = pl.ds(t * TILE, TILE)

    def derivative(minus_two, minus_one, plus_one, plus_two):
        return minus_two - 8.0 * minus_one + 8.0 * plus_one - plus_two

    along_x, along_y, along_z = [], [], []
    halo_left = left[at, :]
    halo_right = right[at, :]
    for c in range(3):
        shifted = [fields[c, pl.ds((first + k) * rows + y, TILE, stride=rows), :] for k in (-2, -1, 1, 2)]
        along_x.append(derivative(*shifted))
        along_y.append(derivative(*[row_at(c, y, k, first, at) for k in (-2, -1, 1, 2)]))
        cells = fields[c, pl.ds(first * rows + y, TILE, stride=rows), :]
        k = c * rows + y
        halo = jnp.where((lane == 2 * k) | (lane == 2 * k + 1), halo_left, halo_right)
        halo = pltpu.roll(halo, (2 * size - 2 - 2 * k) % size, 1)
        along_z.append(
            derivative(
                pltpu.roll(jnp.where(lane >= size - 2, halo, cells), 2, 1),
                pltpu.roll(jnp.where(lane >= size - 1, halo, cells), 1, 1),
                pltpu.roll(jnp.where(lane < 1, halo, cells), size - 1, 1),
                pltpu.roll(jnp.where(lane < 2, halo, cells), size - 2, 1),
            )
        )
    gradient = (along_x, along_y, along_z)
    normal = [gradient[a][a] * gradient[a][a] for a in range(3)]
    rotation, shearing = [], []
    for a, b in ((0, 1), (0, 2), (1, 2)):
        turn = gradient[a][b] - gradient[b][a]
        shear = gradient[a][b] + gradient[b][a]
        rotation.append(turn * turn)
        shearing.append(shear * shear)
    enstrophy = (rotation[0] + rotation[1] + rotation[2]) * (1.0 / 288.0)
    strain = (normal[0] + normal[1] + normal[2]) * (1.0 / 144.0)
    strain = strain + (shearing[0] + shearing[1] + shearing[2]) * (1.0 / 288.0)
    return enstrophy, strain


def velocity_kernel(rows, planes, fields, message, pieces, total):
    size = fields.shape[2]
    for c in range(3):

        @pl.loop(0, rows // 2)
        def _(pair):
            for half in range(2):
                plane = fields[c, pl.ds(2 * rows + 2 * pair + half, planes, stride=rows), :]
                high, low = split(plane)
                pieces[0:planes, half * size : (half + 1) * size] = high
                pieces[planes : 2 * planes, half * size : (half + 1) * size] = low
            product = lax.dot_general(pieces[0:planes, :], pieces[...], DIMS_NT, preferred_element_type=jnp.float32)

            @pl.when(pair == 0)
            def _():
                total[c] = product

            @pl.when(pair > 0)
            def _():
                total[c] += product

    grams = [gram_of(total[c]) for c in range(3)]
    message[0:planes, :] = pack_pair(grams[0], grams[1])
    message[planes : 2 * planes, :] = grams[2]
    message[2 * planes : 2 * planes + 8, :] = jnp.broadcast_to(diagonal(grams[1]), (8, planes))


def interior_kernel(rows, planes, fields, left, right, out, total, pieces):
    size = fields.shape[2]

    def row_at(c, y, k, first, at):
        return fields[c, pl.ds(first * rows + y + k, TILE, stride=rows), :]

    @pl.loop(0, rows // 2 - 2)
    def _(pair):
        for half in range(2):
            index = 2 * pair + half
            for t in range(planes // TILE):
                results = invariants_of(fields, left, right, t, index + 2, rows, row_at)
                for f in range(2):
                    out[f, index, t * TILE : (t + 1) * TILE, :] = results[f]
                    high, low = split(results[f])
                    pieces[f, t * TILE : (t + 1) * TILE, half * size : (half + 1) * size] = high
                    pieces[f, planes + t * TILE : planes + (t + 1) * TILE, half * size : (half + 1) * size] = low
        for f in range(2):
            product = lax.dot_general(
                pieces[f, 0:planes, :], pieces[f], DIMS_NT, preferred_element_type=jnp.float32
            )

            @pl.when(pair == 0)
            def _():
                total[f] = product

            @pl.when(pair > 0)
            def _():
                total[f] += product


def border_kernel(rows, planes, fields, near, far, left, right, part, out, message, pieces, total):
    size = fields.shape[2]
    odd = lax.axis_index("gy") % 2 == 1

    def row_at(c, y, k, first, at):
        if 0 <= y + k < rows:
            return fields[c, pl.ds(first * rows + y + k, TILE, stride=rows), :]
        if y + k < 0:
            layer = y + k + 2
            return jnp.where(odd, near[c, layer, at, :], far[c, layer, at, :])
        layer = y + k - rows
        return jnp.where(odd, far[c, layer, at, :], near[c, layer, at, :])

    for index, y in enumerate((0, 1, rows - 2, rows - 1)):
        half = index % 2
        for t in range(planes // TILE):
            results = invariants_of(fields, left, right, t, y, rows, row_at)
            for f in range(2):
                out[f, index, t * TILE : (t + 1) * TILE, :] = results[f]
                high, low = split(results[f])
                pieces[f, t * TILE : (t + 1) * TILE, half * size : (half + 1) * size] = high
                pieces[f, planes + t * TILE : planes + (t + 1) * TILE, half * size : (half + 1) * size] = low
        if half == 1:
            for f in range(2):
                product = lax.dot_general(
                    pieces[f, 0:planes, :], pieces[f], DIMS_NT, preferred_element_type=jnp.float32
                )
                total[f] = (part[f] if index == 1 else total[f]) + product
    grams = [gram_of(total[f]) for f in range(2)]
    message[0:planes, :] = pack_pair(grams[0], grams[1])
    message[planes : planes + 8, :] = jnp.broadcast_to(diagonal(grams[1]), (8, planes))


def assemble_kernel(rows, planes, inner, border, enstrophy, strain):
    for f, out in enumerate((enstrophy, strain)):
        for y in range(rows):
            if 2 <= y < rows - 2:
                plane = inner[f, y - 2]
            else:
                plane = border[f, y if y < 2 else y - rows + 4]
            out[pl.ds(y, planes, stride=rows), :] = plane


def combine_kernel(cells, planes, velocity, derived, cross):
    row, col = halves(planes)
    eye = row == col

    def scale(squares):
        return 1.0 / (5.0 * cells * (squares / (planes * cells) + 1e-06))

    def unpack(packed, second_diagonal):
        first_scale = scale(jnp.sum(jnp.where(eye, packed, 0.0)))
        second_scale = scale(jnp.sum(second_diagonal))
        lower = jnp.where(row > col, packed * first_scale, jnp.where(row < col, packed * second_scale, 0.0))
        both = jnp.where(eye, packed * first_scale + second_diagonal * second_scale, 0.0)
        return lower, both

    low_a, both_a = unpack(velocity[0:planes, :], velocity[2 * planes : 2 * planes + 1, :])
    low_b, both_b = unpack(derived[0:planes, :], derived[planes : planes + 1, :])
    third = velocity[planes : 2 * planes, :]
    third = third * scale(jnp.sum(jnp.where(eye, third, 0.0)))
    triangles = low_a + low_b
    cross[...] = triangles + triangles.T + (both_a + both_b) + third


def butterfly_sum(values, axes):
    for axis in axes:
        count = lax.axis_size(axis)
        if count & (count - 1):
            values = lax.psum(values, axis)
            continue
        step = 1
        while step < count:
            values = values + lax.ppermute(values, axis, [(i, i ^ step) for i in range(count)])
            step *= 2
    return values


def f32(*shape):
    return jax.ShapeDtypeStruct(shape, jnp.float32)


def per_device(fields):
    planes = fields.shape[1] - 4
    rows, cols = fields.shape[2], fields.shape[3]
    count_y, count_z = lax.axis_size("gy"), lax.axis_size("gz")
    flat = fields.reshape(3, fields.shape[1] * rows, cols)

    near, far, behind, ahead = pl.pallas_call(
        functools.partial(faces_kernel, rows, planes),
        out_shape=(f32(3, 2, planes, cols), f32(3, 2, planes, cols), f32(planes, cols), f32(planes, cols)),
        in_specs=[VMEM],
        out_specs=(VMEM, VMEM, VMEM, VMEM),
        compiler_params=params(),
        name="faces",
    )(flat)
    far = lax.ppermute(far, "gy", [(i, (i + 1 if i % 2 else i - 1) % count_y) for i in range(count_y)])
    near = lax.ppermute(near, "gy", [(i, i ^ 1) for i in range(count_y)])
    left = lax.ppermute(ahead, "gz", [(i, (i + 1) % count_z) for i in range(count_z)])
    right = lax.ppermute(behind, "gz", [(i, (i - 1) % count_z) for i in range(count_z)])

    velocity = pl.pallas_call(
        functools.partial(velocity_kernel, rows, planes),
        out_shape=f32(2 * planes + 8, planes),
        in_specs=[VMEM],
        out_specs=VMEM,
        scratch_shapes=[pltpu.VMEM((2 * planes, 2 * cols), jnp.bfloat16), pltpu.VMEM((3, planes, 2 * planes), jnp.float32)],
        compiler_params=params(),
        name="velocity_grams",
    )(flat)
    pieces = pltpu.VMEM((2, 2 * planes, 2 * cols), jnp.bfloat16)
    inner, part = pl.pallas_call(
        functools.partial(interior_kernel, rows, planes),
        out_shape=(f32(2, rows - 4, planes, cols), f32(2, planes, 2 * planes)),
        in_specs=[VMEM] * 3,
        out_specs=(VMEM, VMEM),
        scratch_shapes=[pieces],
        compiler_params=params(),
        name="interior",
    )(flat, left, right)
    border, derived = pl.pallas_call(
        functools.partial(border_kernel, rows, planes),
        out_shape=(f32(2, 4, planes, cols), f32(planes + 8, planes)),
        in_specs=[VMEM] * 6,
        out_specs=(VMEM, VMEM),
        scratch_shapes=[pieces, pltpu.VMEM((2, planes, 2 * planes), jnp.float32)],
        compiler_params=params(),
        name="border",
    )(flat, near, far, left, right, part)
    enstrophy, strain_rate = pl.pallas_call(
        functools.partial(assemble_kernel, rows, planes),
        out_shape=(f32(planes * rows, cols), f32(planes * rows, cols)),
        in_specs=[VMEM] * 2,
        out_specs=(VMEM, VMEM),
        compiler_params=params(),
        name="assemble",
    )(inner, border)

    velocity = butterfly_sum(velocity, ("gy", "gz"))
    derived = butterfly_sum(derived, ("gy", "gz"))
    cells = rows * cols * count_y * count_z
    cross = pl.pallas_call(
        functools.partial(combine_kernel, float(cells), planes),
        out_shape=f32(planes, planes),
        in_specs=[VMEM] * 2,
        out_specs=VMEM,
        compiler_params=params(),
        name="combine",
    )(velocity, derived)
    factor = jnp.linalg.cholesky(cross)
    shape = (planes, rows, cols)
    return (enstrophy.reshape(shape), strain_rate.reshape(shape), factor)


def solution(mesh):
    return jax.shard_map(
        per_device,
        mesh=mesh,
        in_specs=(P(None, None, "gy", "gz"),),
        out_specs=(P(None, "gy", "gz"), P(None, "gy", "gz"), P()),
        check_vma=False,
    )
```

```python
import functools

import jax
import jax.numpy as jnp
from jax import lax
from jax.experimental import pallas as pl
from jax.experimental.pallas import tpu as pltpu
from jax.sharding import PartitionSpec as P

TILE = 16
BLOCK = 8
CHUNKS = 2
VMEM = pl.BlockSpec(memory_space=pltpu.VMEM)
DIMS_NT = (((1,), (1,)), ((), ()))


def params(mebibytes=20):
    return pltpu.CompilerParams(vmem_limit_bytes=mebibytes * 1024 * 1024)


def lanes(shape):
    return lax.broadcasted_iota(jnp.int32, shape, 1)


def split(values):
    high = values.astype(jnp.bfloat16)
    low = (values - high.astype(jnp.float32)).astype(jnp.bfloat16)
    return high, low


def gram_of(product):
    size = product.shape[0]
    mixed = product[:, size:]
    return product[:, :size] + (mixed + mixed.T)


def halves(size):
    row = lax.broadcasted_iota(jnp.int32, (size, size), 0)
    col = lax.broadcasted_iota(jnp.int32, (size, size), 1)
    return row, col


def pack_pair(first, second):
    row, col = halves(first.shape[0])
    return jnp.where(row >= col, first, second)


def diagonal(matrix):
    row, col = halves(matrix.shape[0])
    return jnp.sum(jnp.where(row == col, matrix, 0.0), axis=0, keepdims=True)


def faces_kernel(rows, planes, fields, turned_fields, near, far, behind, ahead, landed, tails, heads, arrived):
    odd = lax.axis_index("gy") % 2
    size = fields.shape[3]
    depth = planes + 4
    cuts = [depth * i // CHUNKS for i in range(CHUNKS + 1)]
    cuts = [cut - cut % 8 for cut in cuts[:-1]] + [depth]
    copies = []
    for c in range(3):
        for i in range(CHUNKS):
            part = pl.ds(cuts[i], cuts[i + 1] - cuts[i])
            copies.append(pltpu.make_async_copy(fields.at[c, part], landed.at[c, part], arrived.at[c, i]))
            copies[-1].start()
    lane = lanes((8, size))
    near_row = (1 - odd) * (rows - 2)
    far_row = odd * (rows - 2)

    def turn(c, first):
        at = pl.ds(first, 8)
        tail = tails[at, :]
        head = heads[at, :]
        for base in range(0, rows, 8):
            block = jnp.swapaxes(landed[c, at, base : base + 8, :], 0, 1)
            for j in range(8):
                y = base + j
                k = c * rows + y
                turned_fields[c, y, at, :] = block[j]
                moved = pltpu.roll(block[j], (2 * k + 2) % size, 1)
                tail = jnp.where(lane >= 2 * k, moved, tail)
                head = jnp.where(lane >= 2 * k + 2, moved, head)
        tails[at, :] = tail
        heads[at, :] = head

    for c in range(3):
        for i in range(CHUNKS):
            copies[c * CHUNKS + i].wait()

            @pl.loop(cuts[i] // 8, cuts[i + 1] // 8)
            def _(t):
                turn(c, pl.multiple_of(t * 8, 8))

        if depth % 8:
            turn(c, depth - 8)
        for layer in range(2):
            near[c, layer] = turned_fields[c, near_row + layer, 2 : planes + 2, :]
            far[c, layer] = turned_fields[c, far_row + layer, 2 : planes + 2, :]
    ahead[...] = tails[2 : planes + 2, :]
    behind[...] = heads[2 : planes + 2, :]


def derivative(minus_two, minus_one, plus_one, plus_two):
    return minus_two - 8.0 * minus_one + 8.0 * plus_one - plus_two


def velocity_kernel(rows, planes, fields, message, along_z, thirds, band):
    size = fields.shape[3]
    row = lax.broadcasted_iota(jnp.int32, (3 * size, size), 0) % size
    col = lax.broadcasted_iota(jnp.int32, (3 * size, size), 1)
    far_side = jnp.where(row == col - 2, 1.0, jnp.where(row == col + 2, -1.0, 0.0))
    near_side = jnp.where(row == col - 1, -8.0, jnp.where(row == col + 1, 8.0, 0.0))
    band[...] = (far_side + near_side).astype(jnp.bfloat16)
    grams = []
    for c in range(3):
        total = None
        for y in range(rows):
            for t in range(planes // TILE):
                cells = fields[c, y, 2 + t * TILE : 2 + (t + 1) * TILE, :]
                high = cells.astype(jnp.bfloat16)
                rest = cells - high.astype(jnp.float32)
                middle = rest.astype(jnp.bfloat16)
                low = (rest - middle.astype(jnp.float32)).astype(jnp.bfloat16)
                for part, piece in enumerate((high, middle, low)):
                    thirds[y, t * TILE : (t + 1) * TILE, part * size : (part + 1) * size] = piece
            high, middle = thirds[y, :, 0:size], thirds[y, :, size : 2 * size]
            product = lax.dot_general(
                high, jnp.concatenate([high, middle], axis=0), DIMS_NT, preferred_element_type=jnp.float32
            )
            total = product if y == 0 else total + product
        grams.append(gram_of(total))
        derivatives = jnp.dot(
            thirds[...].reshape(rows * planes, 3 * size), band[...], preferred_element_type=jnp.float32
        )
        along_z[c] = derivatives.reshape(rows, planes, size)
    message[0:planes, :] = pack_pair(grams[0], grams[1])
    message[planes : 2 * planes, :] = grams[2]
    message[2 * planes : 2 * planes + 8, :] = jnp.broadcast_to(diagonal(grams[1]), (8, planes))


def edge_terms(left, right):
    size = left.shape[1]
    even = lanes(left.shape) % 2 == 0
    left = pltpu.roll(left, 2, 1)
    right = pltpu.roll(right, size - 2, 1)
    to_last = jnp.where(even, -right, 8.0 * pltpu.roll(right, 1, 1) - right)
    to_first = jnp.where(even, left - 8.0 * pltpu.roll(left, size - 1, 1), left)
    return to_last, to_first


def invariants_of(fields, own_z, to_last, to_first, t, y, rows, row_at):
    size = fields.shape[3]
    lane = lanes((TILE, size))
    edge = (lane < 2) | (lane >= size - 2)
    at = pl.ds(t * TILE, TILE)
    along_x, along_y, along_z = [], [], []
    for c in range(3):
        along_x.append(derivative(*[fields[c, y, pl.ds(2 + t * TILE + k, TILE), :] for k in (-2, -1, 1, 2)]))
        along_y.append(derivative(*[row_at(c, y, k, t) for k in (-2, -1, 1, 2)]))
        k = c * rows + y
        terms = jnp.where(lane < 2 * k + 2, to_last[at, :], to_first[at, :])
        terms = pltpu.roll(terms, (2 * size - 2 - 2 * k) % size, 1)
        along_z.append(own_z[c, y, at, :] + jnp.where(edge, terms, 0.0))
    gradient = (along_x, along_y, along_z)
    normal = [gradient[a][a] * gradient[a][a] for a in range(3)]
    rotation, shearing = [], []
    for a, b in ((0, 1), (0, 2), (1, 2)):
        turn = gradient[a][b] - gradient[b][a]
        shear = gradient[a][b] + gradient[b][a]
        rotation.append(turn * turn)
        shearing.append(shear * shear)
    enstrophy = (rotation[0] + rotation[1] + rotation[2]) * (1.0 / 288.0)
    strain = (normal[0] + normal[1] + normal[2]) * (1.0 / 144.0)
    strain = strain + (shearing[0] + shearing[1] + shearing[2]) * (1.0 / 288.0)
    return enstrophy, strain


def store_results(results, out, index, pieces, half, t, planes, size):
    tile = slice(t * TILE, (t + 1) * TILE)
    lower = slice(planes + t * TILE, planes + (t + 1) * TILE)
    for f in range(2):
        out[f, index, tile, :] = results[f]
        high, low = split(results[f])
        pieces[f, tile, half * size : (half + 1) * size] = high
        pieces[f, lower, half * size : (half + 1) * size] = low


def interior_kernel(rows, planes, fields, own_z, left, right, out, total, pieces, to_last, to_first):
    size = fields.shape[3]
    to_last[...], to_first[...] = edge_terms(left[...], right[...])

    def row_at(c, y, k, t):
        return fields[c, y + k, pl.ds(2 + t * TILE, TILE), :]

    @pl.loop(0, rows // 2 - 2)
    def _(pair):
        for half in range(2):
            index = 2 * pair + half
            for t in range(planes // TILE):
                results = invariants_of(fields, own_z, to_last, to_first, t, index + 2, rows, row_at)
                store_results(results, out, index, pieces, half, t, planes, size)
        for f in range(2):
            product = lax.dot_general(
                pieces[f, 0:planes, :], pieces[f], DIMS_NT, preferred_element_type=jnp.float32
            )

            @pl.when(pair == 0)
            def _():
                total[f] = product

            @pl.when(pair > 0)
            def _():
                total[f] += product


def border_kernel(
    rows, planes, fields, own_z, near, far, left, right, part, out, message, pieces, total, to_last, to_first
):
    size = fields.shape[3]
    odd = lax.axis_index("gy") % 2 == 1
    to_last[...], to_first[...] = edge_terms(left[...], right[...])

    def row_at(c, y, k, t):
        at = pl.ds(t * TILE, TILE)
        if 0 <= y + k < rows:
            return fields[c, y + k, pl.ds(2 + t * TILE, TILE), :]
        if y + k < 0:
            layer = y + k + 2
            return jnp.where(odd, near[c, layer, at, :], far[c, layer, at, :])
        layer = y + k - rows
        return jnp.where(odd, far[c, layer, at, :], near[c, layer, at, :])

    for index, y in enumerate((0, 1, rows - 2, rows - 1)):
        half = index % 2
        for t in range(planes // TILE):
            results = invariants_of(fields, own_z, to_last, to_first, t, y, rows, row_at)
            store_results(results, out, index, pieces, half, t, planes, size)
        if half == 1:
            for f in range(2):
                product = lax.dot_general(
                    pieces[f, 0:planes, :], pieces[f], DIMS_NT, preferred_element_type=jnp.float32
                )
                total[f] = (part[f] if index == 1 else total[f]) + product
    grams = [gram_of(total[f]) for f in range(2)]
    message[0:planes, :] = pack_pair(grams[0], grams[1])
    message[planes : planes + 8, :] = jnp.broadcast_to(diagonal(grams[1]), (8, planes))


def assemble_kernel(rows, planes, inner, border, enstrophy, strain):
    def plane_of(f, y):
        if 2 <= y < rows - 2:
            return inner.at[f, y - 2]
        return border.at[f, y if y < 2 else y - rows + 4]

    for f, out in enumerate((enstrophy, strain)):

        @pl.loop(0, planes // 8)
        def _(t):
            at = pl.ds(pl.multiple_of(t * 8, 8), 8)
            for base in range(0, rows, 8):
                block = jnp.stack([plane_of(f, y)[at, :] for y in range(base, base + 8)], axis=0)
                out[at, base : base + 8, :] = jnp.swapaxes(block, 0, 1)


def thirds_of(values):
    high = values.astype(jnp.bfloat16).astype(jnp.float32)
    rest = values - high
    middle = rest.astype(jnp.bfloat16).astype(jnp.float32)
    return high, middle, rest - middle

def splat_row(block, j):
    return jnp.broadcast_to(block[j : j + 1, :], block.shape)

def eliminate(rows, first):
    count, size = rows.shape
    columns = [jnp.broadcast_to(rows[:, first + j : first + j + 1], rows.shape) for j in range(count)]
    entry = {(i, j): splat_row(columns[j], i) for j in range(count) for i in range(j, count)}
    row = [splat_row(rows, j) for j in range(count)]
    sub = lax.broadcasted_iota(jnp.int32, rows.shape, 0)
    lane = lax.broadcasted_iota(jnp.int32, rows.shape, 1)
    out = jnp.zeros_like(rows)
    for j in range(count):
        root = lax.rsqrt(entry[j, j])
        lower = {i: entry[i, j] * root for i in range(j + 1, count)}
        row[j] = row[j] * root
        for i in range(j + 1, count):
            for m in range(i, count):
                entry[m, i] = entry[m, i] - lower[m] * lower[i]
            row[i] = row[i] - lower[i] * row[j]
        out = jnp.where(sub == j, row[j], out)
    return jnp.where(lane >= first + sub, out, 0.0)


def factor_kernel(cells, planes, velocity, derived, factor, work, upper):
    row, col = halves(planes)
    eye = row == col

    def scale(squares):
        return 1.0 / (5.0 * cells * (squares / (planes * cells) + 1e-06))

    def unpack(packed, second_diagonal):
        first_scale = scale(jnp.sum(jnp.where(eye, packed, 0.0)))
        second_scale = scale(jnp.sum(second_diagonal))
        lower = jnp.where(row > col, packed * first_scale, jnp.where(row < col, packed * second_scale, 0.0))
        both = jnp.where(eye, packed * first_scale + second_diagonal * second_scale, 0.0)
        return lower, both

    low_a, both_a = unpack(velocity[0:planes, :], velocity[2 * planes : 2 * planes + 1, :])
    low_b, both_b = unpack(derived[0:planes, :], derived[planes : planes + 1, :])
    third = velocity[planes : 2 * planes, :]
    third = third * scale(jnp.sum(jnp.where(eye, third, 0.0)))
    triangles = low_a + low_b
    work[...] = triangles + triangles.T + (both_a + both_b) + third
    for first in range(0, planes, BLOCK):
        rows = eliminate(work[first : first + BLOCK, :], first)
        upper[first : first + BLOCK, :] = rows
        if first + BLOCK < planes:
            high, middle, low = thirds_of(rows)
            one = jnp.concatenate([high, high, middle, high, low, middle], axis=0).astype(jnp.bfloat16)
            two = jnp.concatenate([high, middle, high, low, high, middle], axis=0).astype(jnp.bfloat16)
            update = lax.dot_general(one, two, (((0,), (0,)), ((), ())), preferred_element_type=jnp.float32)
            work[first + BLOCK :, :] -= update[first + BLOCK :, :]
    factor[...] = upper[...].T


def butterfly_sum(values, axes):
    for axis in axes:
        count = lax.axis_size(axis)
        if count & (count - 1):
            values = lax.psum(values, axis)
            continue
        step = 1
        while step < count:
            values = values + lax.ppermute(values, axis, [(i, i ^ step) for i in range(count)])
            step *= 2
    return values


def f32(*shape):
    return jax.ShapeDtypeStruct(shape, jnp.float32)


def per_device(fields):
    planes = fields.shape[1] - 4
    rows, cols = fields.shape[2], fields.shape[3]
    count_y, count_z = lax.axis_size("gy"), lax.axis_size("gz")

    turned, near, far, behind, ahead = pl.pallas_call(
        functools.partial(faces_kernel, rows, planes),
        out_shape=(
            pltpu.VMEM((3, rows, planes + 4, cols), jnp.float32),
            f32(3, 2, planes, cols),
            f32(3, 2, planes, cols),
            f32(planes, cols),
            f32(planes, cols),
        ),
        in_specs=[pl.BlockSpec(memory_space=pl.ANY)],
        out_specs=(VMEM, VMEM, VMEM, VMEM, VMEM),
        scratch_shapes=[
            pltpu.VMEM(fields.shape, jnp.float32),
            pltpu.VMEM((planes + 4, cols), jnp.float32),
            pltpu.VMEM((planes + 4, cols), jnp.float32),
            pltpu.SemaphoreType.DMA((3, CHUNKS)),
        ],
        compiler_params=params(),
        name="faces",
    )(pltpu.with_memory_space_constraint(fields, pltpu.HBM))
    far = lax.ppermute(far, "gy", [(i, (i + 1 if i % 2 else i - 1) % count_y) for i in range(count_y)])
    near = lax.ppermute(near, "gy", [(i, i ^ 1) for i in range(count_y)])
    left = lax.ppermute(ahead, "gz", [(i, (i + 1) % count_z) for i in range(count_z)])
    right = lax.ppermute(behind, "gz", [(i, (i - 1) % count_z) for i in range(count_z)])

    velocity, own_z = pl.pallas_call(
        functools.partial(velocity_kernel, rows, planes),
        out_shape=(f32(2 * planes + 8, planes), pltpu.VMEM((3, rows, planes, cols), jnp.float32)),
        in_specs=[VMEM],
        out_specs=(VMEM, VMEM),
        scratch_shapes=[
            pltpu.VMEM((rows, planes, 3 * cols), jnp.bfloat16),
            pltpu.VMEM((3 * cols, cols), jnp.bfloat16),
        ],
        compiler_params=params(),
        name="velocity_grams",
    )(turned)
    pieces = pltpu.VMEM((2, 2 * planes, 2 * cols), jnp.bfloat16)
    edges = [pltpu.VMEM((planes, cols), jnp.float32)] * 2
    inner, part = pl.pallas_call(
        functools.partial(interior_kernel, rows, planes),
        out_shape=(f32(2, rows - 4, planes, cols), f32(2, planes, 2 * planes)),
        in_specs=[VMEM] * 4,
        out_specs=(VMEM, VMEM),
        scratch_shapes=[pieces, *edges],
        compiler_params=params(),
        name="interior",
    )(turned, own_z, left, right)
    border, derived = pl.pallas_call(
        functools.partial(border_kernel, rows, planes),
        out_shape=(f32(2, 4, planes, cols), f32(planes + 8, planes)),
        in_specs=[VMEM] * 7,
        out_specs=(VMEM, VMEM),
        scratch_shapes=[pieces, pltpu.VMEM((2, planes, 2 * planes), jnp.float32), *edges],
        compiler_params=params(),
        name="border",
    )(turned, own_z, near, far, left, right, part)
    enstrophy, strain_rate = pl.pallas_call(
        functools.partial(assemble_kernel, rows, planes),
        out_shape=(f32(planes, rows, cols), f32(planes, rows, cols)),
        in_specs=[VMEM] * 2,
        out_specs=(VMEM, VMEM),
        compiler_params=params(),
        name="assemble",
    )(inner, border)

    velocity = butterfly_sum(velocity, ("gy", "gz"))
    derived = butterfly_sum(derived, ("gy", "gz"))
    cells = rows * cols * count_y * count_z
    factor = pl.pallas_call(
        functools.partial(factor_kernel, float(cells), planes),
        out_shape=f32(planes, planes),
        in_specs=[VMEM] * 2,
        out_specs=VMEM,
        scratch_shapes=[pltpu.VMEM((planes, planes), jnp.float32)] * 2,
        compiler_params=params(),
        name="factor",
    )(velocity, derived)
    return (enstrophy, strain_rate, factor)


def solution(mesh):
    return jax.shard_map(
        per_device,
        mesh=mesh,
        in_specs=(P(None, None, "gy", "gz"),),
        out_specs=(P(None, "gy", "gz"), P(None, "gy", "gz"), P()),
        check_vma=False,
    )
```

```python
import functools

import jax
import jax.numpy as jnp
from jax import lax
from jax.experimental import pallas as pl
from jax.experimental.pallas import tpu as pltpu
from jax.sharding import PartitionSpec as P

TILE = 16
BLOCK = 8
CHUNKS = 2
VMEM = pl.BlockSpec(memory_space=pltpu.VMEM)
DIMS_NT = (((1,), (1,)), ((), ()))


def params(mebibytes=20):
    return pltpu.CompilerParams(vmem_limit_bytes=mebibytes * 1024 * 1024)


def lanes(shape):
    return lax.broadcasted_iota(jnp.int32, shape, 1)


def split(values):
    high = values.astype(jnp.bfloat16)
    low = (values - high.astype(jnp.float32)).astype(jnp.bfloat16)
    return high, low


def gram_of(product):
    size = product.shape[0]
    mixed = product[:, size:]
    return product[:, :size] + (mixed + mixed.T)


def halves(size):
    row = lax.broadcasted_iota(jnp.int32, (size, size), 0)
    col = lax.broadcasted_iota(jnp.int32, (size, size), 1)
    return row, col


def pack_pair(first, second):
    row, col = halves(first.shape[0])
    return jnp.where(row >= col, first, second)


def half_starts(length):
    core = lax.axis_index("gy") % 2
    return pl.multiple_of(core * length, 8), pl.multiple_of((1 - core) * length, 8)


def diagonal(matrix):
    row, col = halves(matrix.shape[0])
    return jnp.sum(jnp.where(row == col, matrix, 0.0), axis=0, keepdims=True)


def faces_kernel(rows, planes, fields, turned_fields, near, far, behind, ahead, landed, tails, heads, arrived):
    odd = lax.axis_index("gy") % 2
    size = fields.shape[3]
    depth = planes + 4
    cuts = [depth * i // CHUNKS for i in range(CHUNKS + 1)]
    cuts = [cut - cut % 8 for cut in cuts[:-1]] + [depth]
    copies = []
    for c in range(3):
        for i in range(CHUNKS):
            part = pl.ds(cuts[i], cuts[i + 1] - cuts[i])
            copies.append(pltpu.make_async_copy(fields.at[c, part], landed.at[c, part], arrived.at[c, i]))
            copies[-1].start()
    lane = lanes((8, size))
    near_row = (1 - odd) * (rows - 2)
    far_row = odd * (rows - 2)

    def turn(c, first):
        at = pl.ds(first, 8)
        tail = tails[at, :]
        head = heads[at, :]
        for base in range(0, rows, 8):
            block = jnp.swapaxes(landed[c, at, base : base + 8, :], 0, 1)
            for j in range(8):
                y = base + j
                k = c * rows + y
                turned_fields[c, y, at, :] = block[j]
                moved = pltpu.roll(block[j], (2 * k + 2) % size, 1)
                tail = jnp.where(lane >= 2 * k, moved, tail)
                head = jnp.where(lane >= 2 * k + 2, moved, head)
        tails[at, :] = tail
        heads[at, :] = head

    for c in range(3):
        for i in range(CHUNKS):
            copies[c * CHUNKS + i].wait()

            @pl.loop(cuts[i] // 8, cuts[i + 1] // 8, unroll=8)
            def _(t):
                turn(c, pl.multiple_of(t * 8, 8))

        if depth % 8:
            turn(c, depth - 8)
        for layer in range(2):
            near[c, layer] = turned_fields[c, near_row + layer, 2 : planes + 2, :]
            far[c, layer] = turned_fields[c, far_row + layer, 2 : planes + 2, :]
    ahead[...] = tails[2 : planes + 2, :]
    behind[...] = heads[2 : planes + 2, :]


def derivative(minus_two, minus_one, plus_one, plus_two):
    return minus_two - 8.0 * minus_one + 8.0 * plus_one - plus_two


def velocity_kernel(rows, planes, fields, grams, along_z, thirds, band):
    size = fields.shape[3]
    row = lax.broadcasted_iota(jnp.int32, (3 * size, size), 0) % size
    col = lax.broadcasted_iota(jnp.int32, (3 * size, size), 1)
    far_side = jnp.where(row == col - 2, 1.0, jnp.where(row == col + 2, -1.0, 0.0))
    near_side = jnp.where(row == col - 1, -8.0, jnp.where(row == col + 1, 8.0, 0.0))
    band[...] = (far_side + near_side).astype(jnp.bfloat16)
    for c in range(3):
        total = None
        for y in range(rows):
            for t in range(planes // TILE):
                cells = fields[c, y, 2 + t * TILE : 2 + (t + 1) * TILE, :]
                high = cells.astype(jnp.bfloat16)
                rest = cells - high.astype(jnp.float32)
                middle = rest.astype(jnp.bfloat16)
                low = (rest - middle.astype(jnp.float32)).astype(jnp.bfloat16)
                for part, piece in enumerate((high, middle, low)):
                    thirds[y, t * TILE : (t + 1) * TILE, part * size : (part + 1) * size] = piece
            high, middle = thirds[y, :, 0:size], thirds[y, :, size : 2 * size]
            product = lax.dot_general(
                high, jnp.concatenate([high, middle], axis=0), DIMS_NT, preferred_element_type=jnp.float32
            )
            total = product if y == 0 else total + product
        grams[c] = gram_of(total)
        derivatives = jnp.dot(
            thirds[...].reshape(rows * planes, 3 * size), band[...], preferred_element_type=jnp.float32
        )
        along_z[c] = derivatives.reshape(rows, planes, size)


def edge_terms(left, right):
    size = left.shape[1]
    even = lanes(left.shape) % 2 == 0
    left = pltpu.roll(left, 2, 1)
    right = pltpu.roll(right, size - 2, 1)
    to_last = jnp.where(even, -right, 8.0 * pltpu.roll(right, 1, 1) - right)
    to_first = jnp.where(even, left - 8.0 * pltpu.roll(left, size - 1, 1), left)
    return to_last, to_first


def invariants_of(fields, own_z, to_last, to_first, t, y, rows, row_at):
    size = fields.shape[3]
    lane = lanes((TILE, size))
    edge = (lane < 2) | (lane >= size - 2)
    at = pl.ds(t * TILE, TILE)
    along_x, along_y, along_z = [], [], []
    for c in range(3):
        along_x.append(derivative(*[fields[c, y, pl.ds(2 + t * TILE + k, TILE), :] for k in (-2, -1, 1, 2)]))
        along_y.append(derivative(*[row_at(c, y, k, t) for k in (-2, -1, 1, 2)]))
        k = c * rows + y
        terms = jnp.where(lane < 2 * k + 2, to_last[at, :], to_first[at, :])
        terms = pltpu.roll(terms, (2 * size - 2 - 2 * k) % size, 1)
        along_z.append(own_z[c, y, at, :] + jnp.where(edge, terms, 0.0))
    gradient = (along_x, along_y, along_z)
    normal = [gradient[a][a] * gradient[a][a] for a in range(3)]
    rotation, shearing = [], []
    for a, b in ((0, 1), (0, 2), (1, 2)):
        turn = gradient[a][b] - gradient[b][a]
        shear = gradient[a][b] + gradient[b][a]
        rotation.append(turn * turn)
        shearing.append(shear * shear)
    enstrophy = (rotation[0] + rotation[1] + rotation[2]) * (1.0 / 288.0)
    strain = (normal[0] + normal[1] + normal[2]) * (1.0 / 144.0)
    strain = strain + (shearing[0] + shearing[1] + shearing[2]) * (1.0 / 288.0)
    return enstrophy, strain


def store_results(results, out, index, pieces, half, t, planes, size):
    tile = slice(t * TILE, (t + 1) * TILE)
    lower = slice(planes + t * TILE, planes + (t + 1) * TILE)
    for f in range(2):
        out[f, index, tile, :] = results[f]
        high, low = split(results[f])
        pieces[f, tile, half * size : (half + 1) * size] = high
        pieces[f, lower, half * size : (half + 1) * size] = low


def interior_kernel(rows, planes, fields, own_z, left, right, out, total, pieces, to_last, to_first):
    size = fields.shape[3]
    to_last[...], to_first[...] = edge_terms(left[...], right[...])

    def row_at(c, y, k, t):
        return fields[c, y + k, pl.ds(2 + t * TILE, TILE), :]

    @pl.loop(0, rows // 2 - 2)
    def _(pair):
        for half in range(2):
            index = 2 * pair + half
            for t in range(planes // TILE):
                results = invariants_of(fields, own_z, to_last, to_first, t, index + 2, rows, row_at)
                store_results(results, out, index, pieces, half, t, planes, size)
        for f in range(2):
            product = lax.dot_general(
                pieces[f, 0:planes, :], pieces[f], DIMS_NT, preferred_element_type=jnp.float32
            )

            @pl.when(pair == 0)
            def _():
                total[f] = product

            @pl.when(pair > 0)
            def _():
                total[f] += product


def border_kernel(
    rows, planes, fields, own_z, near, far, left, right, part, velocity, out, keep, give, message, pieces, total, to_last, to_first
):
    size = fields.shape[3]
    odd = lax.axis_index("gy") % 2 == 1
    to_last[...], to_first[...] = edge_terms(left[...], right[...])

    def row_at(c, y, k, t):
        at = pl.ds(t * TILE, TILE)
        if 0 <= y + k < rows:
            return fields[c, y + k, pl.ds(2 + t * TILE, TILE), :]
        if y + k < 0:
            layer = y + k + 2
            return jnp.where(odd, near[c, layer, at, :], far[c, layer, at, :])
        layer = y + k - rows
        return jnp.where(odd, far[c, layer, at, :], near[c, layer, at, :])

    for index, y in enumerate((0, 1, rows - 2, rows - 1)):
        half = index % 2
        for t in range(planes // TILE):
            results = invariants_of(fields, own_z, to_last, to_first, t, y, rows, row_at)
            store_results(results, out, index, pieces, half, t, planes, size)
        if half == 1:
            for f in range(2):
                product = lax.dot_general(
                    pieces[f, 0:planes, :], pieces[f], DIMS_NT, preferred_element_type=jnp.float32
                )
                total[f] = (part[f] if index == 1 else total[f]) + product
    grams = [gram_of(total[f]) for f in range(2)] + [velocity[c] for c in range(3)]
    message[0:planes, :] = pack_pair(grams[0], grams[1])
    message[planes : 2 * planes, :] = pack_pair(grams[2], grams[3])
    message[2 * planes : 3 * planes, :] = grams[4]
    message[3 * planes : 3 * planes + 8, :] = jnp.broadcast_to(diagonal(grams[1]), (8, planes))
    message[3 * planes + 8 : 3 * planes + 16, :] = jnp.broadcast_to(diagonal(grams[3]), (8, planes))
    mine, other = half_starts(keep.shape[0])
    keep[...] = message[pl.ds(mine, keep.shape[0]), :]
    give[...] = message[pl.ds(other, keep.shape[0]), :]


def assemble_kernel(rows, planes, inner, border, enstrophy, strain):
    def plane_of(f, y):
        if 2 <= y < rows - 2:
            return inner.at[f, y - 2]
        return border.at[f, y if y < 2 else y - rows + 4]

    for f, out in enumerate((enstrophy, strain)):

        @pl.loop(0, planes // 8)
        def _(t):
            at = pl.ds(pl.multiple_of(t * 8, 8), 8)
            for base in range(0, rows, 8):
                block = jnp.stack([plane_of(f, y)[at, :] for y in range(base, base + 8)], axis=0)
                out[at, base : base + 8, :] = jnp.swapaxes(block, 0, 1)


def thirds_of(values):
    high = values.astype(jnp.bfloat16).astype(jnp.float32)
    rest = values - high
    middle = rest.astype(jnp.bfloat16).astype(jnp.float32)
    return high, middle, rest - middle

def splat_row(block, j):
    return jnp.broadcast_to(block[j : j + 1, :], block.shape)

def eliminate(rows, first):
    count, size = rows.shape
    columns = [jnp.broadcast_to(rows[:, first + j : first + j + 1], rows.shape) for j in range(count)]
    entry = {(i, j): splat_row(columns[j], i) for j in range(count) for i in range(j, count)}
    row = [splat_row(rows, j) for j in range(count)]
    sub = lax.broadcasted_iota(jnp.int32, rows.shape, 0)
    lane = lax.broadcasted_iota(jnp.int32, rows.shape, 1)
    out = jnp.zeros_like(rows)
    for j in range(count):
        root = lax.rsqrt(entry[j, j])
        lower = {i: entry[i, j] * root for i in range(j + 1, count)}
        row[j] = row[j] * root
        for i in range(j + 1, count):
            for m in range(i, count):
                entry[m, i] = entry[m, i] - lower[m] * lower[i]
            row[i] = row[i] - lower[i] * row[j]
        out = jnp.where(sub == j, row[j], out)
    return jnp.where(lane >= first + sub, out, 0.0)


def factor_kernel(cells, planes, kept, given, factor, message, work, upper):
    mine, other = half_starts(kept.shape[0])
    message[pl.ds(mine, kept.shape[0]), :] = kept[...]
    message[pl.ds(other, kept.shape[0]), :] = given[...]
    row, col = halves(planes)
    eye = row == col

    def scale(squares):
        return 1.0 / (5.0 * cells * (squares / (planes * cells) + 1e-06))

    def unpack(packed, second_diagonal):
        first_scale = scale(jnp.sum(jnp.where(eye, packed, 0.0)))
        second_scale = scale(jnp.sum(second_diagonal))
        lower = jnp.where(row > col, packed * first_scale, jnp.where(row < col, packed * second_scale, 0.0))
        both = jnp.where(eye, packed * first_scale + second_diagonal * second_scale, 0.0)
        return lower, both

    low_a, both_a = unpack(message[0:planes, :], message[3 * planes : 3 * planes + 1, :])
    low_b, both_b = unpack(message[planes : 2 * planes, :], message[3 * planes + 8 : 3 * planes + 9, :])
    third = message[2 * planes : 3 * planes, :]
    third = third * scale(jnp.sum(jnp.where(eye, third, 0.0)))
    triangles = low_a + low_b
    work[...] = triangles + triangles.T + (both_a + both_b) + third
    for first in range(0, planes, BLOCK):
        rows = eliminate(work[first : first + BLOCK, :], first)
        upper[first : first + BLOCK, :] = rows
        if first + BLOCK < planes:
            high, middle, low = thirds_of(rows)
            one = jnp.concatenate([high, high, middle, high, low, middle], axis=0).astype(jnp.bfloat16)
            two = jnp.concatenate([high, middle, high, low, high, middle], axis=0).astype(jnp.bfloat16)
            update = lax.dot_general(one, two, (((0,), (0,)), ((), ())), preferred_element_type=jnp.float32)
            work[first + BLOCK :, :] -= update[first + BLOCK :, :]
    factor[...] = upper[...].T


def cost(microseconds):
    return pl.CostEstimate(flops=0, bytes_accessed=int(microseconds * 3.69e6), transcendentals=0)


AXES = ("gy", "gz")


def exchange(values, even, odd):
    count_z = lax.axis_size("gz")
    count = lax.axis_size("gy") * count_z
    return lax.ppermute(values, AXES, [(i, i ^ (odd if i // count_z % 2 else even)) for i in range(count)])


def rounds():
    count_y, count_z = lax.axis_size("gy"), lax.axis_size("gz")
    assert count_y & (count_y - 1) == 0 and count_z & (count_z - 1) == 0
    bits = [count_z << i for i in range(1, count_y.bit_length() - 1)] + [1 << i for i in range(count_z.bit_length() - 1)]
    groups = [bits[i : i + 2] for i in range(0, len(bits), 2)]
    return [[group[0]] if len(group) == 1 else [group[0], group[1], group[0] ^ group[1]] for group in groups]


def add_terms(terms):
    while len(terms) > 1:
        terms = [terms[i] + terms[i + 1] for i in range(0, len(terms), 2)]
    return terms[0]


def f32(*shape):
    return jax.ShapeDtypeStruct(shape, jnp.float32)


def per_device(fields):
    planes = fields.shape[1] - 4
    rows, cols = fields.shape[2], fields.shape[3]
    count_y, count_z = lax.axis_size("gy"), lax.axis_size("gz")

    turned, near, far, behind, ahead = pl.pallas_call(
        functools.partial(faces_kernel, rows, planes),
        out_shape=(
            pltpu.VMEM((3, rows, planes + 4, cols), jnp.float32),
            f32(3, 2, planes, cols),
            f32(3, 2, planes, cols),
            f32(planes, cols),
            f32(planes, cols),
        ),
        in_specs=[pl.BlockSpec(memory_space=pl.ANY)],
        out_specs=(VMEM, VMEM, VMEM, VMEM, VMEM),
        scratch_shapes=[
            pltpu.VMEM(fields.shape, jnp.float32),
            pltpu.VMEM((planes + 4, cols), jnp.float32),
            pltpu.VMEM((planes + 4, cols), jnp.float32),
            pltpu.SemaphoreType.DMA((3, CHUNKS)),
        ],
        compiler_params=params(),
        cost_estimate=cost(5),
        name="faces",
    )(pltpu.with_memory_space_constraint(fields, pltpu.HBM))
    far = lax.ppermute(far, "gy", [(i, (i + 1 if i % 2 else i - 1) % count_y) for i in range(count_y)])
    near = lax.ppermute(near, "gy", [(i, i ^ 1) for i in range(count_y)])
    left = lax.ppermute(ahead, "gz", [(i, (i + 1) % count_z) for i in range(count_z)])
    right = lax.ppermute(behind, "gz", [(i, (i - 1) % count_z) for i in range(count_z)])

    velocity, own_z = pl.pallas_call(
        functools.partial(velocity_kernel, rows, planes),
        out_shape=(f32(3, planes, planes), pltpu.VMEM((3, rows, planes, cols), jnp.float32)),
        in_specs=[VMEM],
        out_specs=(VMEM, VMEM),
        scratch_shapes=[
            pltpu.VMEM((rows, planes, 3 * cols), jnp.bfloat16),
            pltpu.VMEM((3 * cols, cols), jnp.bfloat16),
        ],
        compiler_params=params(),
        cost_estimate=cost(2.5),
        name="velocity_grams",
    )(turned)
    pieces = pltpu.VMEM((2, 2 * planes, 2 * cols), jnp.bfloat16)
    edges = [pltpu.VMEM((planes, cols), jnp.float32)] * 2
    inner, part = pl.pallas_call(
        functools.partial(interior_kernel, rows, planes),
        out_shape=(f32(2, rows - 4, planes, cols), f32(2, planes, 2 * planes)),
        in_specs=[VMEM] * 4,
        out_specs=(VMEM, VMEM),
        scratch_shapes=[pieces, *edges],
        compiler_params=params(),
        cost_estimate=cost(4),
        name="interior",
    )(turned, own_z, left, right)
    half = 3 * planes // 2 + 8
    message = pltpu.VMEM((2 * half, planes), jnp.float32)
    border, keep, give = pl.pallas_call(
        functools.partial(border_kernel, rows, planes),
        out_shape=(f32(2, 4, planes, cols), f32(half, planes), f32(half, planes)),
        in_specs=[VMEM] * 8,
        out_specs=(VMEM, VMEM, VMEM),
        scratch_shapes=[message, pieces, pltpu.VMEM((2, planes, 2 * planes), jnp.float32), *edges],
        compiler_params=params(),
        cost_estimate=cost(1),
        name="border",
    )(turned, own_z, near, far, left, right, part, velocity)
    enstrophy, strain_rate = pl.pallas_call(
        functools.partial(assemble_kernel, rows, planes),
        out_shape=(f32(planes, rows, cols), f32(planes, rows, cols)),
        in_specs=[VMEM] * 2,
        out_specs=(VMEM, VMEM),
        compiler_params=params(),
        cost_estimate=cost(2),
        name="assemble",
    )(inner, border)

    core = count_z
    kept = keep + exchange(give, core, core)
    masks = rounds()
    for even, odd in zip(masks, masks[::-1]):
        kept = add_terms([kept] + [exchange(kept, *pair) for pair in zip(even, odd)])
    given = exchange(kept, core, core)
    cells = rows * cols * count_y * count_z
    factor = pl.pallas_call(
        functools.partial(factor_kernel, float(cells), planes),
        out_shape=f32(planes, planes),
        in_specs=[VMEM] * 2,
        out_specs=VMEM,
        scratch_shapes=[message] + [pltpu.VMEM((planes, planes), jnp.float32)] * 2,
        compiler_params=params(),
        cost_estimate=cost(6),
        name="factor",
    )(kept, given)
    return (enstrophy, strain_rate, factor)


def solution(mesh):
    return jax.shard_map(
        per_device,
        mesh=mesh,
        in_specs=(P(None, None, "gy", "gz"),),
        out_specs=(P(None, "gy", "gz"), P(None, "gy", "gz"), P()),
        check_vma=False,
    )
```

```python
import functools

import jax
import jax.numpy as jnp
from jax import lax
from jax.experimental import pallas as pl
from jax.experimental.pallas import tpu as pltpu
from jax.sharding import PartitionSpec as P

TILE = 16
CHUNKS = 2
VMEM = pl.BlockSpec(memory_space=pltpu.VMEM)
DIMS_NT = (((1,), (1,)), ((), ()))


def params(mebibytes=20):
    return pltpu.CompilerParams(vmem_limit_bytes=mebibytes * 1024 * 1024)


def lanes(shape):
    return lax.broadcasted_iota(jnp.int32, shape, 1)


def split(values):
    high = values.astype(jnp.bfloat16)
    low = (values - high.astype(jnp.float32)).astype(jnp.bfloat16)
    return high, low


def gram_of(product):
    size = product.shape[0] // 2
    same = product[:size, :size] + product[size:, size:]
    return same + (product[:size, size:] + product[size:, :size])


def square(pieces):
    return lax.dot_general(pieces, pieces, DIMS_NT, preferred_element_type=jnp.float32)


def halves(size):
    row = lax.broadcasted_iota(jnp.int32, (size, size), 0)
    col = lax.broadcasted_iota(jnp.int32, (size, size), 1)
    return row, col


def pack_pair(first, second):
    row, col = halves(first.shape[0])
    return jnp.where(row >= col, first, second)


def half_starts(length):
    core = lax.axis_index("gy") % 2
    return pl.multiple_of(core * length, 8), pl.multiple_of((1 - core) * length, 8)


def diagonal(matrix):
    row, col = halves(matrix.shape[0])
    return jnp.sum(jnp.where(row == col, matrix, 0.0), axis=0, keepdims=True)


def faces_kernel(rows, planes, fields, turned_fields, near, far, behind, ahead, landed, tails, heads, arrived):
    odd = lax.axis_index("gy") % 2
    size = fields.shape[3]
    depth = planes + 4
    cuts = [depth * i // CHUNKS for i in range(CHUNKS + 1)]
    cuts = [cut - cut % 8 for cut in cuts[:-1]] + [depth]
    copies = []
    for c in range(3):
        for i in range(CHUNKS):
            part = pl.ds(cuts[i], cuts[i + 1] - cuts[i])
            copies.append(pltpu.make_async_copy(fields.at[c, part], landed.at[c, part], arrived.at[c, i]))
            copies[-1].start()
    lane = lanes((8, size))
    near_row = (1 - odd) * (rows - 2)
    far_row = odd * (rows - 2)

    def turn(c, first):
        at = pl.ds(first, 8)
        tail = tails[at, :]
        head = heads[at, :]
        for base in range(0, rows, 8):
            block = jnp.swapaxes(landed[c, at, base : base + 8, :], 0, 1)
            for j in range(8):
                y = base + j
                k = c * rows + y
                turned_fields[c, y, at, :] = block[j]
                moved = pltpu.roll(block[j], (2 * k + 2) % size, 1)
                tail = jnp.where(lane >= 2 * k, moved, tail)
                head = jnp.where(lane >= 2 * k + 2, moved, head)
        tails[at, :] = tail
        heads[at, :] = head

    for c in range(3):
        for i in range(CHUNKS):
            copies[c * CHUNKS + i].wait()

            @pl.loop(cuts[i] // 8, cuts[i + 1] // 8, unroll=8)
            def _(t):
                turn(c, pl.multiple_of(t * 8, 8))

        if depth % 8:
            turn(c, depth - 8)
        for layer in range(2):
            near[c, layer] = turned_fields[c, near_row + layer, 2 : planes + 2, :]
            far[c, layer] = turned_fields[c, far_row + layer, 2 : planes + 2, :]
    ahead[...] = tails[2 : planes + 2, :]
    behind[...] = heads[2 : planes + 2, :]


def derivative(minus_two, minus_one, plus_one, plus_two):
    return 8.0 * (plus_one - minus_one) - (plus_two - minus_two)


def velocity_kernel(rows, planes, fields, grams, along_z, thirds, band):
    size = fields.shape[3]
    row = lax.broadcasted_iota(jnp.int32, (3 * size, size), 0) % size
    col = lax.broadcasted_iota(jnp.int32, (3 * size, size), 1)
    far_side = jnp.where(row == col - 2, 1.0, jnp.where(row == col + 2, -1.0, 0.0))
    near_side = jnp.where(row == col - 1, -8.0, jnp.where(row == col + 1, 8.0, 0.0))
    band[...] = (far_side + near_side).astype(jnp.bfloat16)
    for c in range(3):
        total = None
        for y in range(rows):
            for t in range(planes // TILE):
                cells = fields[c, y, 2 + t * TILE : 2 + (t + 1) * TILE, :]
                high = cells.astype(jnp.bfloat16)
                rest = cells - high.astype(jnp.float32)
                middle = rest.astype(jnp.bfloat16)
                low = (rest - middle.astype(jnp.float32)).astype(jnp.bfloat16)
                for part, piece in enumerate((high, middle, low)):
                    thirds[y, t * TILE : (t + 1) * TILE, part * size : (part + 1) * size] = piece
            if y % 2 == 1:
                parts = [
                    jnp.concatenate([thirds[y - 1, :, at : at + size], thirds[y, :, at : at + size]], axis=1)
                    for at in (0, size)
                ]
                product = square(jnp.concatenate(parts, axis=0))
                total = product if y == 1 else total + product
        grams[c] = gram_of(total)
        derivatives = jnp.dot(
            thirds[...].reshape(rows * planes, 3 * size), band[...], preferred_element_type=jnp.float32
        )
        along_z[c] = derivatives.reshape(rows, planes, size)


def edge_terms(left, right):
    size = left.shape[1]
    even = lanes(left.shape) % 2 == 0
    left = pltpu.roll(left, 2, 1)
    right = pltpu.roll(right, size - 2, 1)
    to_last = jnp.where(even, -right, 8.0 * pltpu.roll(right, 1, 1) - right)
    to_first = jnp.where(even, left - 8.0 * pltpu.roll(left, size - 1, 1), left)
    return to_last, to_first


def invariants_of(fields, own_z, to_last, to_first, t, y, rows, row_at):
    size = fields.shape[3]
    lane = lanes((TILE, size))
    edge = (lane < 2) | (lane >= size - 2)
    at = pl.ds(t * TILE, TILE)
    along_x, along_y, along_z = [], [], []
    for c in range(3):
        along_x.append(derivative(*[fields[c, y, pl.ds(2 + t * TILE + k, TILE), :] for k in (-2, -1, 1, 2)]))
        along_y.append(derivative(*[row_at(c, y, k, t) for k in (-2, -1, 1, 2)]))
        k = c * rows + y
        terms = jnp.where(lane < 2 * k + 2, to_last[at, :], to_first[at, :])
        terms = pltpu.roll(terms, (2 * size - 2 - 2 * k) % size, 1)
        along_z.append(own_z[c, y, at, :] + jnp.where(edge, terms, 0.0))
    gradient = (along_x, along_y, along_z)
    normal = [gradient[a][a] * gradient[a][a] for a in range(3)]
    rotation, shearing = [], []
    for a, b in ((0, 1), (0, 2), (1, 2)):
        turn = gradient[a][b] - gradient[b][a]
        shear = gradient[a][b] + gradient[b][a]
        rotation.append(turn * turn)
        shearing.append(shear * shear)
    enstrophy = (rotation[0] + rotation[1] + rotation[2]) * (1.0 / 288.0)
    strain = (normal[0] + normal[1] + normal[2]) * (1.0 / 144.0)
    strain = strain + (shearing[0] + shearing[1] + shearing[2]) * (1.0 / 288.0)
    return enstrophy, strain


def store_results(results, out, index, pieces, half, t, planes, size):
    tile = slice(t * TILE, (t + 1) * TILE)
    lower = slice(planes + t * TILE, planes + (t + 1) * TILE)
    for f in range(2):
        out[f, index, tile, :] = results[f]
        high, low = split(results[f])
        pieces[f, tile, half * size : (half + 1) * size] = high
        pieces[f, lower, half * size : (half + 1) * size] = low


def interior_kernel(rows, planes, fields, own_z, left, right, out, total, pieces, to_last, to_first):
    size = fields.shape[3]
    to_last[...], to_first[...] = edge_terms(left[...], right[...])

    def row_at(c, y, k, t):
        return fields[c, y + k, pl.ds(2 + t * TILE, TILE), :]

    for pair in range(rows // 2 - 2):
        buffer = pieces.at[pair % 2]
        for half in range(2):
            index = 2 * pair + half
            for t in range(planes // TILE):
                results = invariants_of(fields, own_z, to_last, to_first, t, index + 2, rows, row_at)
                store_results(results, out, index, buffer, half, t, planes, size)
        for f in range(2):
            product = square(buffer[f])
            total[f] = product if pair == 0 else total[f] + product


def border_kernel(
    rows, planes, fields, own_z, near, far, left, right, part, velocity, out, keep, give, message, pieces, total, to_last, to_first
):
    size = fields.shape[3]
    odd = lax.axis_index("gy") % 2 == 1
    to_last[...], to_first[...] = edge_terms(left[...], right[...])

    def row_at(c, y, k, t):
        at = pl.ds(t * TILE, TILE)
        if 0 <= y + k < rows:
            return fields[c, y + k, pl.ds(2 + t * TILE, TILE), :]
        if y + k < 0:
            layer = y + k + 2
            return jnp.where(odd, near[c, layer, at, :], far[c, layer, at, :])
        layer = y + k - rows
        return jnp.where(odd, far[c, layer, at, :], near[c, layer, at, :])

    for index, y in enumerate((0, 1, rows - 2, rows - 1)):
        half = index % 2
        buffer = pieces.at[index // 2]
        for t in range(planes // TILE):
            results = invariants_of(fields, own_z, to_last, to_first, t, y, rows, row_at)
            store_results(results, out, index, buffer, half, t, planes, size)
        if half == 1:
            for f in range(2):
                product = square(buffer[f])
                total[f] = (part[f] if index == 1 else total[f]) + product
    grams = [gram_of(total[f]) for f in range(2)] + [velocity[c] for c in range(3)]
    message[0:planes, :] = pack_pair(grams[0], grams[1])
    message[planes : 2 * planes, :] = pack_pair(grams[2], grams[3])
    message[2 * planes : 3 * planes, :] = grams[4]
    message[3 * planes : 3 * planes + 8, :] = jnp.broadcast_to(diagonal(grams[1]), (8, planes))
    message[3 * planes + 8 : 3 * planes + 16, :] = jnp.broadcast_to(diagonal(grams[3]), (8, planes))
    mine, other = half_starts(keep.shape[0])
    keep[...] = message[pl.ds(mine, keep.shape[0]), :]
    give[...] = message[pl.ds(other, keep.shape[0]), :]


def assemble_kernel(rows, planes, f, inner, border, out):
    def plane_of(y):
        if 2 <= y < rows - 2:
            return inner.at[f, y - 2]
        return border.at[f, y if y < 2 else y - rows + 4]

    @pl.loop(0, planes // 8)
    def _(t):
        at = pl.ds(pl.multiple_of(t * 8, 8), 8)
        for base in range(0, rows, 8):
            block = jnp.stack([plane_of(y)[at, :] for y in range(base, base + 8)], axis=0)
            out[at, base : base + 8, :] = jnp.swapaxes(block, 0, 1)


def splat(tile, j):
    return jnp.broadcast_to(tile[j : j + 1, :], tile.shape)

def spread_column(tile, at):
    return jnp.broadcast_to(tile[:, at : at + 1], tile.shape)


def factor_tiles(tiles, widths):
    count, size = tiles[0].shape
    sub = lax.broadcasted_iota(jnp.int32, (count, size), 0)
    lane = lax.broadcasted_iota(jnp.int32, (count, size), 1)
    tiles = list(tiles)
    out = []
    first = 0
    for width in widths:
        top = first // count
        head = width // count
        spread = [[spread_column(tiles[top + t], first + j) for t in range(head)] for j in range(width)]
        rows = tiles[top : top + head]
        results = [jnp.zeros((count, size), jnp.float32)] * head
        inverses, entries, pivots = [], {}, []
        pivot = splat(spread[0][0], 0)
        for j in range(width):
            t0, s0 = divmod(j, count)
            inverse = 1.0 / pivot
            inverses.append(inverse)
            for m in range(j + 1, width):
                entries[j, m] = splat(spread[j][m // count], m % count)
            if j + 1 < width:
                t1, s1 = divmod(j + 1, count)
                following = splat(spread[j + 1][t1], s1) - (entries[j, j + 1] * entries[j, j + 1]) * inverse
            row = splat(rows[t0], s0)
            pivots.append(row)
            results[t0] = jnp.where(sub == s0, row * lax.rsqrt(pivot), results[t0])
            for t in range(t0, head):
                scaled = spread[j][t] * inverse
                for m in range(j + 1, width):
                    spread[m][t] = spread[m][t] - scaled * entries[j, m]
                rows[t] = rows[t] - scaled * row
            if j + 1 < width:
                pivot = following
        for t in range(head):
            out.append(jnp.where(lane >= first + t * count + sub, results[t], 0.0))
        for t in range(top + head, len(tiles)):
            tile = tiles[t]
            columns = [spread_column(tile, first + j) for j in range(width)]
            for j in range(width):
                scaled = columns[j] * inverses[j]
                for m in range(j + 1, width):
                    columns[m] = columns[m] - scaled * entries[j, m]
                tile = tile - scaled * pivots[j]
            tiles[t] = tile
        first += width
    return out


def factor_kernel(cells, planes, kept, given, factor, message):
    mine, other = half_starts(kept.shape[0])
    message[pl.ds(mine, kept.shape[0]), :] = kept[...]
    message[pl.ds(other, kept.shape[0]), :] = given[...]
    row, col = halves(planes)
    eye = row == col

    def scale(squares):
        return 1.0 / (5.0 * cells * (squares / (planes * cells) + 1e-06))

    def unpack(packed, second_diagonal):
        first_scale = scale(jnp.sum(jnp.where(eye, packed, 0.0)))
        second_scale = scale(jnp.sum(second_diagonal))
        lower = jnp.where(row > col, packed * first_scale, jnp.where(row < col, packed * second_scale, 0.0))
        both = jnp.where(eye, packed * first_scale + second_diagonal * second_scale, 0.0)
        return lower, both

    low_a, both_a = unpack(message[0:planes, :], message[3 * planes : 3 * planes + 1, :])
    low_b, both_b = unpack(message[planes : 2 * planes, :], message[3 * planes + 8 : 3 * planes + 9, :])
    third = message[2 * planes : 3 * planes, :]
    third = third * scale(jnp.sum(jnp.where(eye, third, 0.0)))
    triangles = low_a + low_b
    cross = triangles + triangles.T + (both_a + both_b) + third
    wide = 16 if planes % 32 == 0 else 8
    widths = [8] * (planes // 16) + [wide] * (planes // 2 // wide)
    upper = factor_tiles([cross[t : t + 8, :] for t in range(0, planes, 8)], widths)
    factor[...] = jnp.concatenate(upper, axis=0).T


def cost(microseconds):
    return pl.CostEstimate(flops=0, bytes_accessed=int(microseconds * 3.69e6), transcendentals=0)


AXES = ("gy", "gz")


def exchange(values, even, odd):
    count_z = lax.axis_size("gz")
    count = lax.axis_size("gy") * count_z
    return lax.ppermute(values, AXES, [(i, i ^ (odd if i // count_z % 2 else even)) for i in range(count)])


def rounds():
    count_y, count_z = lax.axis_size("gy"), lax.axis_size("gz")
    assert count_y & (count_y - 1) == 0 and count_z & (count_z - 1) == 0
    bits = [count_z << i for i in range(1, count_y.bit_length() - 1)] + [1 << i for i in range(count_z.bit_length() - 1)]
    groups = [bits[i : i + 2] for i in range(0, len(bits), 2)]
    return [[group[0]] if len(group) == 1 else [group[0] ^ group[1], group[0], group[1]] for group in groups]


def add_terms(terms):
    while len(terms) > 1:
        terms = [terms[i] + terms[i + 1] for i in range(0, len(terms), 2)]
    return terms[0]


def f32(*shape):
    return jax.ShapeDtypeStruct(shape, jnp.float32)


def per_device(fields):
    planes = fields.shape[1] - 4
    rows, cols = fields.shape[2], fields.shape[3]
    count_y, count_z = lax.axis_size("gy"), lax.axis_size("gz")

    turned, near, far, behind, ahead = pl.pallas_call(
        functools.partial(faces_kernel, rows, planes),
        out_shape=(
            pltpu.VMEM((3, rows, planes + 4, cols), jnp.float32),
            f32(3, 2, planes, cols),
            f32(3, 2, planes, cols),
            f32(planes, cols),
            f32(planes, cols),
        ),
        in_specs=[pl.BlockSpec(memory_space=pl.ANY)],
        out_specs=(VMEM, VMEM, VMEM, VMEM, VMEM),
        scratch_shapes=[
            pltpu.VMEM(fields.shape, jnp.float32),
            pltpu.VMEM((planes + 4, cols), jnp.float32),
            pltpu.VMEM((planes + 4, cols), jnp.float32),
            pltpu.SemaphoreType.DMA((3, CHUNKS)),
        ],
        compiler_params=params(),
        cost_estimate=cost(5),
        name="faces",
    )(pltpu.with_memory_space_constraint(fields, pltpu.HBM))
    far = lax.ppermute(far, "gy", [(i, (i + 1 if i % 2 else i - 1) % count_y) for i in range(count_y)])
    near = lax.ppermute(near, "gy", [(i, i ^ 1) for i in range(count_y)])
    left = lax.ppermute(ahead, "gz", [(i, (i + 1) % count_z) for i in range(count_z)])
    right = lax.ppermute(behind, "gz", [(i, (i - 1) % count_z) for i in range(count_z)])

    velocity, own_z = pl.pallas_call(
        functools.partial(velocity_kernel, rows, planes),
        out_shape=(f32(3, planes, planes), pltpu.VMEM((3, rows, planes, cols), jnp.float32)),
        in_specs=[VMEM],
        out_specs=(VMEM, VMEM),
        scratch_shapes=[
            pltpu.VMEM((rows, planes, 3 * cols), jnp.bfloat16),
            pltpu.VMEM((3 * cols, cols), jnp.bfloat16),
        ],
        compiler_params=params(),
        cost_estimate=cost(2.5),
        name="velocity_grams",
    )(turned)
    pieces = pltpu.VMEM((2, 2, 2 * planes, 2 * cols), jnp.bfloat16)
    edges = [pltpu.VMEM((planes, cols), jnp.float32)] * 2
    inner, part = pl.pallas_call(
        functools.partial(interior_kernel, rows, planes),
        out_shape=(f32(2, rows - 4, planes, cols), f32(2, 2 * planes, 2 * planes)),
        in_specs=[VMEM] * 4,
        out_specs=(VMEM, VMEM),
        scratch_shapes=[pieces, *edges],
        compiler_params=params(),
        cost_estimate=cost(4),
        name="interior",
    )(turned, own_z, left, right)
    half = 3 * planes // 2 + 8
    message = pltpu.VMEM((2 * half, planes), jnp.float32)
    border, keep, give = pl.pallas_call(
        functools.partial(border_kernel, rows, planes),
        out_shape=(f32(2, 4, planes, cols), f32(half, planes), f32(half, planes)),
        in_specs=[VMEM] * 8,
        out_specs=(VMEM, VMEM, VMEM),
        scratch_shapes=[message, pieces, pltpu.VMEM((2, 2 * planes, 2 * planes), jnp.float32), *edges],
        compiler_params=params(),
        cost_estimate=cost(1),
        name="border",
    )(turned, own_z, near, far, left, right, part, velocity)
    enstrophy, strain_rate = [
        pl.pallas_call(
            functools.partial(assemble_kernel, rows, planes, f),
            out_shape=f32(planes, rows, cols),
            in_specs=[VMEM] * 2,
            out_specs=VMEM,
            compiler_params=params(),
            cost_estimate=cost(1),
            name="assemble",
        )(inner, border)
        for f in range(2)
    ]
    core = count_z
    kept = keep + exchange(give, core, core)
    masks = rounds()
    for even, odd in zip(masks, masks[::-1]):
        kept = add_terms([kept] + [exchange(kept, *pair) for pair in zip(even, odd)])
    kept, enstrophy, strain_rate = lax.optimization_barrier((kept, enstrophy, strain_rate))
    given = exchange(kept, core, core)
    cells = rows * cols * count_y * count_z
    factor = pl.pallas_call(
        functools.partial(factor_kernel, float(cells), planes),
        out_shape=f32(planes, planes),
        in_specs=[VMEM] * 2,
        out_specs=VMEM,
        scratch_shapes=[message],
        compiler_params=params(),
        cost_estimate=cost(6),
        name="factor",
    )(kept, given)
    return (enstrophy, strain_rate, factor)


def solution(mesh):
    return jax.shard_map(
        per_device,
        mesh=mesh,
        in_specs=(P(None, None, "gy", "gz"),),
        out_specs=(P(None, "gy", "gz"), P(None, "gy", "gz"), P()),
        check_vma=False,
    )
```

```python
import functools

import jax
import jax.numpy as jnp
from jax import lax
from jax.experimental import pallas as pl
from jax.experimental.pallas import tpu as pltpu
from jax.sharding import PartitionSpec as P

TILE = 16
VMEM = pl.BlockSpec(memory_space=pltpu.VMEM)
DIMS_NT = (((1,), (1,)), ((), ()))


def params(mebibytes=20):
    return pltpu.CompilerParams(vmem_limit_bytes=mebibytes * 1024 * 1024)


def lanes(shape):
    return lax.broadcasted_iota(jnp.int32, shape, 1)


def split(values):
    high = values.astype(jnp.bfloat16)
    low = (values - high.astype(jnp.float32)).astype(jnp.bfloat16)
    return high, low


def gram_of(product):
    size = product.shape[0] // 2
    same = product[:size, :size] + product[size:, size:]
    return same + (product[:size, size:] + product[size:, :size])


def square(pieces):
    return lax.dot_general(pieces, pieces, DIMS_NT, preferred_element_type=jnp.float32)


def halves(size):
    row = lax.broadcasted_iota(jnp.int32, (size, size), 0)
    col = lax.broadcasted_iota(jnp.int32, (size, size), 1)
    return row, col


def pack_pair(first, second):
    row, col = halves(first.shape[0])
    return jnp.where(row >= col, first, second)


def half_starts(length):
    core = lax.axis_index("gy") % 2
    return pl.multiple_of(core * length, 8), pl.multiple_of((1 - core) * length, 8)


def diagonal(matrix):
    row, col = halves(matrix.shape[0])
    return jnp.sum(jnp.where(row == col, matrix, 0.0), axis=0, keepdims=True)


def far_kernel(rows, planes, fields, far, arrived):
    first = lax.axis_index("gy") % 2 * (rows - 2)
    copies = []
    for layer in range(2):
        for c in range(3):
            source = fields.at[c, pl.ds(2, planes), first + layer, :]
            copies.append(pltpu.make_async_copy(source, far.at[c, layer], arrived.at[layer, c]))
            copies[-1].start()
    for copy in copies:
        copy.wait()


def faces_kernel(rows, planes, fields, turned_fields, near_0, near_1, behind, ahead, tails, heads):
    odd = lax.axis_index("gy") % 2
    size = fields.shape[3]
    depth = planes + 4
    lane = lanes((8, size))
    near_row = (1 - odd) * (rows - 2)

    def turn(c, first):
        at = pl.ds(first, 8)
        tail = tails[at, :]
        head = heads[at, :]
        for base in range(0, rows, 8):
            block = jnp.swapaxes(fields[c, at, base : base + 8, :], 0, 1)
            for j in range(8):
                y = base + j
                k = c * rows + y
                turned_fields[c, y, at, :] = block[j]
                moved = pltpu.roll(block[j], (2 * k + 2) % size, 1)
                tail = jnp.where(lane >= 2 * k, moved, tail)
                head = jnp.where(lane >= 2 * k + 2, moved, head)
        tails[at, :] = tail
        heads[at, :] = head

    for c in range(3):

        @pl.loop(0, depth // 8, unroll=8)
        def _(t):
            turn(c, pl.multiple_of(t * 8, 8))

        if depth % 8:
            turn(c, depth - 8)
        for layer, near in enumerate((near_0, near_1)):
            near[c] = turned_fields[c, near_row + layer, 2 : planes + 2, :]
    ahead[...] = tails[2 : planes + 2, :]
    behind[...] = heads[2 : planes + 2, :]


def derivative(minus_two, minus_one, plus_one, plus_two):
    return 8.0 * (plus_one - minus_one) - (plus_two - minus_two)


def inner_kernel(rows, planes, fields, grams, along_z, spin, stretch, bend_x, bend_y, thirds, band):
    size = fields.shape[3]
    row = lax.broadcasted_iota(jnp.int32, (3 * size, size), 0) % size
    col = lax.broadcasted_iota(jnp.int32, (3 * size, size), 1)
    far_side = jnp.where(row == col - 2, 1.0, jnp.where(row == col + 2, -1.0, 0.0))
    near_side = jnp.where(row == col - 1, -8.0, jnp.where(row == col + 1, 8.0, 0.0))
    band[...] = (far_side + near_side).astype(jnp.bfloat16)

    def planar(index, t):
        y = index + 2
        at = pl.ds(t * TILE, TILE)
        x, y = [
            [
                derivative(*[fields[c, y + k * step, pl.ds(2 + t * TILE + k * (1 - step), TILE), :] for k in (-2, -1, 1, 2)])
                for c in range(3)
            ]
            for step in (0, 1)
        ]
        turn = x[1] - y[0]
        shear = x[1] + y[0]
        spin[index, at, :] = turn * turn
        stretch[index, at, :] = 2.0 * (x[0] * x[0] + y[1] * y[1]) + shear * shear
        bend_x[index, at, :] = x[2]
        bend_y[index, at, :] = y[2]

    tiles = [(index, t) for index in range(rows - 4) for t in range(planes // TILE)]
    done = 0
    for c in range(3):
        total = None
        for y in range(rows):
            for t in range(planes // TILE):
                cells = fields[c, y, 2 + t * TILE : 2 + (t + 1) * TILE, :]
                high = cells.astype(jnp.bfloat16)
                rest = cells - high.astype(jnp.float32)
                middle = rest.astype(jnp.bfloat16)
                low = (rest - middle.astype(jnp.float32)).astype(jnp.bfloat16)
                for part, piece in enumerate((high, middle, low)):
                    thirds[y, t * TILE : (t + 1) * TILE, part * size : (part + 1) * size] = piece
            if y % 2 == 1:
                parts = [
                    jnp.concatenate([thirds[y - 1, :, at : at + size], thirds[y, :, at : at + size]], axis=1)
                    for at in (0, size)
                ]
                product = square(jnp.concatenate(parts, axis=0))
                total = product if y == 1 else total + product
            upto = len(tiles) * (c * rows + y + 1) // (3 * rows)
            for tile in tiles[done:upto]:
                planar(*tile)
            done = upto
        grams[c] = gram_of(total)
        derivatives = jnp.dot(
            thirds[...].reshape(rows * planes, 3 * size), band[...], preferred_element_type=jnp.float32
        )
        along_z[c] = derivatives.reshape(rows, planes, size)


def edge_terms(left, right):
    size = left.shape[1]
    even = lanes(left.shape) % 2 == 0
    left = pltpu.roll(left, 2, 1)
    right = pltpu.roll(right, size - 2, 1)
    to_last = jnp.where(even, -right, 8.0 * pltpu.roll(right, 1, 1) - right)
    to_first = jnp.where(even, left - 8.0 * pltpu.roll(left, size - 1, 1), left)
    return to_last, to_first


def z_derivatives(own_z, to_last, to_first, t, y, rows):
    size = own_z.shape[3]
    lane = lanes((TILE, size))
    edge = (lane < 2) | (lane >= size - 2)
    at = pl.ds(t * TILE, TILE)
    along_z = []
    for c in range(3):
        k = c * rows + y
        terms = jnp.where(lane < 2 * k + 2, to_last[at, :], to_first[at, :])
        terms = pltpu.roll(terms, (2 * size - 2 - 2 * k) % size, 1)
        along_z.append(own_z[c, y, at, :] + jnp.where(edge, terms, 0.0))
    return along_z


def finish(spin, stretch, bend_x, bend_y, z):
    turn_x, turn_y = bend_x - z[0], bend_y - z[1]
    shear_x, shear_y = bend_x + z[0], bend_y + z[1]
    enstrophy = spin + turn_x * turn_x + turn_y * turn_y
    strain = stretch + 2.0 * (z[2] * z[2]) + (shear_x * shear_x + shear_y * shear_y)
    return enstrophy * (1.0 / 288.0), strain * (1.0 / 288.0)


def store_results(results, out, index, pieces, half, t, planes, size):
    tile = slice(t * TILE, (t + 1) * TILE)
    lower = slice(planes + t * TILE, planes + (t + 1) * TILE)
    for f in range(2):
        out[f, index, tile, :] = results[f]
        high, low = split(results[f])
        pieces[f, tile, half * size : (half + 1) * size] = high
        pieces[f, lower, half * size : (half + 1) * size] = low


def beside_face(rows, planes, fields, own_z, halo, lower, to_last, to_first, t):
    at = pl.ds(t * TILE, TILE)
    within = pl.ds(2 + t * TILE, TILE)
    first = jnp.where(lower, 0, rows - 2)

    def window(c):
        own = [fields[c, jnp.where(lower, 0, rows - 4) + i, within, :] for i in range(4)]
        ends = [halo[i][c, at, :] for i in range(2)]
        before = [jnp.where(lower, ends[i], own[i]) for i in range(2)]
        centre = [jnp.where(lower, own[i], own[i + 2]) for i in range(2)]
        after = [jnp.where(lower, own[i + 2], ends[i]) for i in range(2)]
        return before + centre + after

    windows = [window(c) for c in range(3)]
    for i in range(2):
        y = first + i
        z = z_derivatives(own_z, to_last, to_first, t, y, rows)
        along_x = [derivative(*[fields[c, y, pl.ds(2 + t * TILE + k, TILE), :] for k in (-2, -1, 1, 2)]) for c in range(3)]
        along_y = [derivative(*[windows[c][2 + i + k] for k in (-2, -1, 1, 2)]) for c in range(3)]
        turn = along_x[1] - along_y[0]
        shear = along_x[1] + along_y[0]
        stretch = 2.0 * (along_x[0] * along_x[0] + along_y[1] * along_y[1]) + shear * shear
        yield i, finish(turn * turn, stretch, along_x[2], along_y[2], z)


def interior_kernel(
    rows, planes, fields, own_z, spin, stretch, bend_x, bend_y, near_0, near_1, left, right, out, total, pieces, to_last, to_first
):
    size = own_z.shape[3]
    odd = lax.axis_index("gy") % 2 == 1
    to_last[...], to_first[...] = edge_terms(left[...], right[...])
    for pair in range(rows // 2 - 1):
        buffer = pieces.at[pair % 2]
        for t in range(planes // TILE):
            if pair < rows // 2 - 2:
                for half in range(2):
                    index = 2 * pair + half
                    z = z_derivatives(own_z, to_last, to_first, t, index + 2, rows)
                    planar = [ref[index, t * TILE : (t + 1) * TILE, :] for ref in (spin, stretch, bend_x, bend_y)]
                    store_results(finish(*planar, z), out, index, buffer, half, t, planes, size)
            else:
                for half, results in beside_face(rows, planes, fields, own_z, [near_0, near_1], odd, to_last, to_first, t):
                    store_results(results, out, 2 * pair + half, buffer, half, t, planes, size)
        for f in range(2):
            product = square(buffer[f])
            total[f] = product if pair == 0 else total[f] + product


def border_kernel(
    rows, planes, fields, own_z, far, left, right, part, velocity, out, keep, give, message, pieces, to_last, to_first
):
    size = fields.shape[3]
    odd = lax.axis_index("gy") % 2 == 1
    to_last[...], to_first[...] = edge_terms(left[...], right[...])
    for t in range(planes // TILE):
        for half, results in beside_face(rows, planes, fields, own_z, [far.at[:, i] for i in range(2)], ~odd, to_last, to_first, t):
            store_results(results, out, half, pieces, half, t, planes, size)
    grams = [gram_of(part[f] + square(pieces[f])) for f in range(2)] + [velocity[c] for c in range(3)]
    message[0:planes, :] = pack_pair(grams[0], grams[1])
    message[planes : 2 * planes, :] = pack_pair(grams[2], grams[3])
    message[2 * planes : 3 * planes, :] = grams[4]
    message[3 * planes : 3 * planes + 8, :] = jnp.broadcast_to(diagonal(grams[1]), (8, planes))
    message[3 * planes + 8 : 3 * planes + 16, :] = jnp.broadcast_to(diagonal(grams[3]), (8, planes))
    mine, other = half_starts(keep.shape[0])
    keep[...] = message[pl.ds(mine, keep.shape[0]), :]
    give[...] = message[pl.ds(other, keep.shape[0]), :]


def assemble_kernel(rows, planes, f, inner, border, out):
    odd = lax.axis_index("gy") % 2 == 1

    def plane_of(y, at):
        if 2 <= y < rows - 2:
            return inner[f, y - 2, at, :]
        layer = y % (rows - 2)
        beside_near = odd if y < 2 else ~odd
        return jnp.where(beside_near, inner[f, rows - 4 + layer, at, :], border[f, layer, at, :])

    @pl.loop(0, planes // 8)
    def _(t):
        at = pl.ds(pl.multiple_of(t * 8, 8), 8)
        for base in range(0, rows, 8):
            block = jnp.stack([plane_of(y, at) for y in range(base, base + 8)], axis=0)
            out[at, base : base + 8, :] = jnp.swapaxes(block, 0, 1)


def splat(tile, j):
    return jnp.broadcast_to(tile[j : j + 1, :], tile.shape)

def spread_column(tile, at):
    return jnp.broadcast_to(tile[:, at : at + 1], tile.shape)


def factor_tiles(tiles, widths):
    count, size = tiles[0].shape
    sub = lax.broadcasted_iota(jnp.int32, (count, size), 0)
    lane = lax.broadcasted_iota(jnp.int32, (count, size), 1)
    tiles = list(tiles)
    out = []
    first = 0
    for width in widths:
        top = first // count
        head = width // count
        spread = [[spread_column(tiles[top + t], first + j) for t in range(head)] for j in range(width)]
        rows = tiles[top : top + head]
        results = [jnp.zeros((count, size), jnp.float32)] * head
        inverses, entries, pivots = [], {}, []
        pivot = splat(spread[0][0], 0)
        for j in range(width):
            t0, s0 = divmod(j, count)
            inverse = 1.0 / pivot
            inverses.append(inverse)
            for m in range(j + 1, width):
                entries[j, m] = splat(spread[j][m // count], m % count)
            if j + 1 < width:
                t1, s1 = divmod(j + 1, count)
                following = splat(spread[j + 1][t1], s1) - (entries[j, j + 1] * entries[j, j + 1]) * inverse
            row = splat(rows[t0], s0)
            pivots.append(row)
            results[t0] = jnp.where(sub == s0, row * lax.rsqrt(pivot), results[t0])
            for t in range(t0, head):
                scaled = spread[j][t] * inverse
                for m in range(j + 1, width):
                    spread[m][t] = spread[m][t] - scaled * entries[j, m]
                rows[t] = rows[t] - scaled * row
            if j + 1 < width:
                pivot = following
        for t in range(head):
            out.append(jnp.where(lane >= first + t * count + sub, results[t], 0.0))
        for t in range(top + head, len(tiles)):
            tile = tiles[t]
            columns = [spread_column(tile, first + j) for j in range(width)]
            for j in range(width):
                scaled = columns[j] * inverses[j]
                for m in range(j + 1, width):
                    columns[m] = columns[m] - scaled * entries[j, m]
                tile = tile - scaled * pivots[j]
            tiles[t] = tile
        first += width
    return out


def factor_kernel(cells, planes, kept, given, factor, message):
    mine, other = half_starts(kept.shape[0])
    message[pl.ds(mine, kept.shape[0]), :] = kept[...]
    message[pl.ds(other, kept.shape[0]), :] = given[...]
    row, col = halves(planes)
    eye = row == col

    def scale(squares):
        return 1.0 / (5.0 * cells * (squares / (planes * cells) + 1e-06))

    def unpack(packed, second_diagonal):
        first_scale = scale(jnp.sum(jnp.where(eye, packed, 0.0)))
        second_scale = scale(jnp.sum(second_diagonal))
        lower = jnp.where(row > col, packed * first_scale, jnp.where(row < col, packed * second_scale, 0.0))
        both = jnp.where(eye, packed * first_scale + second_diagonal * second_scale, 0.0)
        return lower, both

    low_a, both_a = unpack(message[0:planes, :], message[3 * planes : 3 * planes + 1, :])
    low_b, both_b = unpack(message[planes : 2 * planes, :], message[3 * planes + 8 : 3 * planes + 9, :])
    third = message[2 * planes : 3 * planes, :]
    third = third * scale(jnp.sum(jnp.where(eye, third, 0.0)))
    triangles = low_a + low_b
    cross = triangles + triangles.T + (both_a + both_b) + third
    wide = 16 if planes % 32 == 0 else 8
    widths = [8] * (planes // 16) + [wide] * (planes // 2 // wide)
    upper = factor_tiles([cross[t : t + 8, :] for t in range(0, planes, 8)], widths)
    factor[...] = jnp.concatenate(upper, axis=0).T


def cost(microseconds):
    return pl.CostEstimate(flops=0, bytes_accessed=int(microseconds * 3.69e6), transcendentals=0)


AXES = ("gy", "gz")


def exchange(values, even, odd):
    count_z = lax.axis_size("gz")
    count = lax.axis_size("gy") * count_z
    return lax.ppermute(values, AXES, [(i, i ^ (odd if i // count_z % 2 else even)) for i in range(count)])


def rounds():
    count_y, count_z = lax.axis_size("gy"), lax.axis_size("gz")
    assert count_y & (count_y - 1) == 0 and count_z & (count_z - 1) == 0
    bits = [count_z << i for i in range(1, count_y.bit_length() - 1)] + [1 << i for i in range(count_z.bit_length() - 1)]
    groups = [bits[i : i + 2] for i in range(0, len(bits), 2)]
    return [[group[0]] if len(group) == 1 else [group[0], group[1], group[0] ^ group[1]] for group in groups]


def add_terms(terms):
    while len(terms) > 1:
        terms = [terms[i] + terms[i + 1] for i in range(0, len(terms), 2)]
    return terms[0]


def f32(*shape):
    return jax.ShapeDtypeStruct(shape, jnp.float32)


def per_device(fields):
    planes = fields.shape[1] - 4
    rows, cols = fields.shape[2], fields.shape[3]
    count_y, count_z = lax.axis_size("gy"), lax.axis_size("gz")

    far = pl.pallas_call(
        functools.partial(far_kernel, rows, planes),
        out_shape=f32(3, 2, planes, cols),
        in_specs=[pl.BlockSpec(memory_space=pl.ANY)],
        out_specs=VMEM,
        scratch_shapes=[pltpu.SemaphoreType.DMA((2, 3))],
        compiler_params=params(),
        cost_estimate=cost(1),
        name="far_face",
    )(pltpu.with_memory_space_constraint(fields, pltpu.HBM))
    fields, far = lax.optimization_barrier((fields, far))
    far = lax.ppermute(far, "gy", [(i, (i + 1 if i % 2 else i - 1) % count_y) for i in range(count_y)])
    turned, near_0, near_1, behind, ahead = pl.pallas_call(
        functools.partial(faces_kernel, rows, planes),
        out_shape=(
            pltpu.VMEM((3, rows, planes + 4, cols), jnp.float32),
            f32(3, planes, cols),
            f32(3, planes, cols),
            f32(planes, cols),
            f32(planes, cols),
        ),
        in_specs=[VMEM],
        out_specs=(VMEM,) * 5,
        scratch_shapes=[pltpu.VMEM((planes + 4, cols), jnp.float32)] * 2,
        compiler_params=params(),
        cost_estimate=cost(2.5),
        name="faces",
    )(pltpu.with_memory_space_constraint(fields, pltpu.VMEM))
    near = [lax.ppermute(layer, "gy", [(i, i ^ 1) for i in range(count_y)]) for layer in (near_0, near_1)]
    left = lax.ppermute(ahead, "gz", [(i, (i + 1) % count_z) for i in range(count_z)])
    right = lax.ppermute(behind, "gz", [(i, (i - 1) % count_z) for i in range(count_z)])

    inner_rows = [pltpu.VMEM((rows - 4, planes, cols), jnp.float32)] * 4
    velocity, own_z, *planar = pl.pallas_call(
        functools.partial(inner_kernel, rows, planes),
        out_shape=(f32(3, planes, planes), pltpu.VMEM((3, rows, planes, cols), jnp.float32), *inner_rows),
        in_specs=[VMEM],
        out_specs=(VMEM,) * 6,
        scratch_shapes=[
            pltpu.VMEM((rows, planes, 3 * cols), jnp.bfloat16),
            pltpu.VMEM((3 * cols, cols), jnp.bfloat16),
        ],
        compiler_params=params(),
        cost_estimate=cost(3),
        name="inner",
    )(turned)
    pieces = pltpu.VMEM((2, 2, 2 * planes, 2 * cols), jnp.bfloat16)
    edges = [pltpu.VMEM((planes, cols), jnp.float32)] * 2
    inner, part = pl.pallas_call(
        functools.partial(interior_kernel, rows, planes),
        out_shape=(f32(2, rows - 2, planes, cols), f32(2, 2 * planes, 2 * planes)),
        in_specs=[VMEM] * 10,
        out_specs=(VMEM, VMEM),
        scratch_shapes=[pieces, *edges],
        compiler_params=params(),
        cost_estimate=cost(1.9),
        name="interior",
    )(turned, own_z, *planar, *near, left, right)
    half = 3 * planes // 2 + 8
    message = pltpu.VMEM((2 * half, planes), jnp.float32)
    border, keep, give = pl.pallas_call(
        functools.partial(border_kernel, rows, planes),
        out_shape=(f32(2, 2, planes, cols), f32(half, planes), f32(half, planes)),
        in_specs=[VMEM] * 7,
        out_specs=(VMEM, VMEM, VMEM),
        scratch_shapes=[message, pltpu.VMEM((2, 2 * planes, 2 * cols), jnp.bfloat16), *edges],
        compiler_params=params(),
        cost_estimate=cost(0.7),
        name="border",
    )(turned, own_z, far, left, right, part, velocity)
    enstrophy, strain_rate = [
        pl.pallas_call(
            functools.partial(assemble_kernel, rows, planes, f),
            out_shape=f32(planes, rows, cols),
            in_specs=[VMEM] * 2,
            out_specs=VMEM,
            compiler_params=params(),
            cost_estimate=cost(1),
            name="assemble",
        )(inner, border)
        for f in range(2)
    ]
    core = count_z
    kept = keep + exchange(give, core, core)
    masks = rounds()
    for even, odd in zip(masks, masks[::-1]):
        kept = add_terms([kept] + [exchange(kept, *pair) for pair in zip(even, odd)])
    kept, enstrophy, strain_rate = lax.optimization_barrier((kept, enstrophy, strain_rate))
    given = exchange(kept, core, core)
    cells = rows * cols * count_y * count_z
    factor = pl.pallas_call(
        functools.partial(factor_kernel, float(cells), planes),
        out_shape=f32(planes, planes),
        in_specs=[VMEM] * 2,
        out_specs=VMEM,
        scratch_shapes=[message],
        compiler_params=params(),
        cost_estimate=cost(6),
        name="factor",
    )(kept, given)
    return (enstrophy, strain_rate, factor)


def solution(mesh):
    return jax.shard_map(
        per_device,
        mesh=mesh,
        in_specs=(P(None, None, "gy", "gz"),),
        out_specs=(P(None, "gy", "gz"), P(None, "gy", "gz"), P()),
        check_vma=False,
    )
```

```python
import functools

import jax
import jax.numpy as jnp
from jax import lax
from jax.experimental import pallas as pl
from jax.experimental.pallas import tpu as pltpu
from jax.sharding import PartitionSpec as P

TILE = 16
VMEM = pl.BlockSpec(memory_space=pltpu.VMEM)
DIMS_NT = (((1,), (1,)), ((), ()))


def params(mebibytes=20):
    return pltpu.CompilerParams(vmem_limit_bytes=mebibytes * 1024 * 1024)


def lanes(shape):
    return lax.broadcasted_iota(jnp.int32, shape, 1)


def split(values):
    high = values.astype(jnp.bfloat16)
    low = (values - high.astype(jnp.float32)).astype(jnp.bfloat16)
    return high, low


def gram_of(product):
    size = product.shape[0] // 2
    same = product[:size, :size] + product[size:, size:]
    return same + (product[:size, size:] + product[size:, :size])


def square(pieces):
    return lax.dot_general(pieces, pieces, DIMS_NT, preferred_element_type=jnp.float32)


def halves(size):
    row = lax.broadcasted_iota(jnp.int32, (size, size), 0)
    col = lax.broadcasted_iota(jnp.int32, (size, size), 1)
    return row, col


def pack_pair(first, second):
    row, col = halves(first.shape[0])
    return jnp.where(row >= col, first, second)


def fold(matrix):
    half = matrix.shape[0] // 2
    row = lax.broadcasted_iota(jnp.int32, (half, 2 * half), 0)
    col = lax.broadcasted_iota(jnp.int32, (half, 2 * half), 1)
    first = pltpu.roll(matrix[:half, :], half, 1)
    last = matrix[half:, :]
    return jnp.where((col >= half) & (row >= col - half), first, last)


def unfold(folded, last_diagonal):
    half = folded.shape[0]
    row = lax.broadcasted_iota(jnp.int32, folded.shape, 0)
    col = lax.broadcasted_iota(jnp.int32, folded.shape, 1)
    first = pltpu.roll(folded, half, 1)
    off_first = jnp.where(row > col, first, 0.0)
    off_last = jnp.where((col < half) | (col - half > row), folded, 0.0)
    on_first = jnp.where(row == col, first, 0.0)
    on_last = jnp.where(row == col - half, last_diagonal, 0.0)
    return jnp.concatenate([off_first, off_last], axis=0), jnp.concatenate([on_first, on_last], axis=0)


def half_starts(length):
    core = lax.axis_index("gy") % 2
    return pl.multiple_of(core * length, 8), pl.multiple_of((1 - core) * length, 8)


def diagonal(matrix):
    row, col = halves(matrix.shape[0])
    return jnp.sum(jnp.where(row == col, matrix, 0.0), axis=0, keepdims=True)


def far_kernel(rows, planes, fields, far, arrived):
    first = lax.axis_index("gy") % 2 * (rows - 2)
    copies = []
    for layer in range(2):
        for c in range(3):
            source = fields.at[c, pl.ds(2, planes), first + layer, :]
            copies.append(pltpu.make_async_copy(source, far.at[c, layer], arrived.at[layer, c]))
            copies[-1].start()
    for copy in copies:
        copy.wait()


def faces_kernel(rows, planes, fields, turned_fields, near_0, near_1, behind, ahead, tails, heads):
    odd = lax.axis_index("gy") % 2
    size = fields.shape[3]
    depth = planes + 4
    lane = lanes((8, size))
    near_row = (1 - odd) * (rows - 2)

    def turn(c, first):
        at = pl.ds(first, 8)
        tail = tails[at, :]
        head = heads[at, :]
        for base in range(0, rows, 8):
            block = jnp.swapaxes(fields[c, at, base : base + 8, :], 0, 1)
            for j in range(8):
                y = base + j
                k = c * rows + y
                turned_fields[c, y, at, :] = block[j]
                moved = pltpu.roll(block[j], (2 * k + 2) % size, 1)
                tail = jnp.where(lane >= 2 * k, moved, tail)
                head = jnp.where(lane >= 2 * k + 2, moved, head)
        tails[at, :] = tail
        heads[at, :] = head

    for c in range(3):

        @pl.loop(0, depth // 8, unroll=8)
        def _(t):
            turn(c, pl.multiple_of(t * 8, 8))

        if depth % 8:
            turn(c, depth - 8)
        for layer, near in enumerate((near_0, near_1)):
            near[c] = turned_fields[c, near_row + layer, 2 : planes + 2, :]
    ahead[...] = tails[2 : planes + 2, :]
    behind[...] = heads[2 : planes + 2, :]


def derivative(minus_two, minus_one, plus_one, plus_two):
    return 8.0 * (plus_one - minus_one) - (plus_two - minus_two)


def inner_kernel(rows, planes, fields, grams, along_z, spin, stretch, bend_x, bend_y, thirds, band):
    size = fields.shape[3]
    row = lax.broadcasted_iota(jnp.int32, (3 * size, size), 0) % size
    col = lax.broadcasted_iota(jnp.int32, (3 * size, size), 1)
    far_side = jnp.where(row == col - 2, 1.0, jnp.where(row == col + 2, -1.0, 0.0))
    near_side = jnp.where(row == col - 1, -8.0, jnp.where(row == col + 1, 8.0, 0.0))
    band[...] = (far_side + near_side).astype(jnp.bfloat16)

    def planar(index, t):
        y = index + 2
        at = pl.ds(t * TILE, TILE)
        x, y = [
            [
                derivative(*[fields[c, y + k * step, pl.ds(2 + t * TILE + k * (1 - step), TILE), :] for k in (-2, -1, 1, 2)])
                for c in range(3)
            ]
            for step in (0, 1)
        ]
        turn = x[1] - y[0]
        shear = x[1] + y[0]
        spin[index, at, :] = turn * turn
        stretch[index, at, :] = 2.0 * (x[0] * x[0] + y[1] * y[1]) + shear * shear
        bend_x[index, at, :] = x[2]
        bend_y[index, at, :] = y[2]

    tiles = [(index, t) for index in range(rows - 4) for t in range(planes // TILE)]
    done = 0
    for c in range(3):
        total = None
        for y in range(rows):
            for t in range(planes // TILE):
                cells = fields[c, y, 2 + t * TILE : 2 + (t + 1) * TILE, :]
                high = cells.astype(jnp.bfloat16)
                rest = cells - high.astype(jnp.float32)
                middle = rest.astype(jnp.bfloat16)
                low = (rest - middle.astype(jnp.float32)).astype(jnp.bfloat16)
                for part, piece in enumerate((high, middle, low)):
                    thirds[y, t * TILE : (t + 1) * TILE, part * size : (part + 1) * size] = piece
            if y % 2 == 1:
                parts = [
                    jnp.concatenate([thirds[y - 1, :, at : at + size], thirds[y, :, at : at + size]], axis=1)
                    for at in (0, size)
                ]
                product = square(jnp.concatenate(parts, axis=0))
                total = product if y == 1 else total + product
            upto = len(tiles) * (c * rows + y + 1) // (3 * rows)
            for tile in tiles[done:upto]:
                planar(*tile)
            done = upto
        grams[c] = gram_of(total)
        derivatives = jnp.dot(
            thirds[...].reshape(rows * planes, 3 * size), band[...], preferred_element_type=jnp.float32
        )
        along_z[c] = derivatives.reshape(rows, planes, size)


def edge_terms(left, right):
    size = left.shape[1]
    even = lanes(left.shape) % 2 == 0
    left = pltpu.roll(left, 2, 1)
    right = pltpu.roll(right, size - 2, 1)
    to_last = jnp.where(even, -right, 8.0 * pltpu.roll(right, 1, 1) - right)
    to_first = jnp.where(even, left - 8.0 * pltpu.roll(left, size - 1, 1), left)
    return to_last, to_first


def z_derivatives(own_z, to_last, to_first, t, y, rows):
    size = own_z.shape[3]
    lane = lanes((TILE, size))
    edge = (lane < 2) | (lane >= size - 2)
    at = pl.ds(t * TILE, TILE)
    along_z = []
    for c in range(3):
        k = c * rows + y
        terms = jnp.where(lane < 2 * k + 2, to_last[at, :], to_first[at, :])
        terms = pltpu.roll(terms, (2 * size - 2 - 2 * k) % size, 1)
        along_z.append(own_z[c, y, at, :] + jnp.where(edge, terms, 0.0))
    return along_z


def finish(spin, stretch, bend_x, bend_y, z):
    turn_x, turn_y = bend_x - z[0], bend_y - z[1]
    shear_x, shear_y = bend_x + z[0], bend_y + z[1]
    enstrophy = spin + turn_x * turn_x + turn_y * turn_y
    strain = stretch + 2.0 * (z[2] * z[2]) + (shear_x * shear_x + shear_y * shear_y)
    return enstrophy * (1.0 / 288.0), strain * (1.0 / 288.0)


def store_results(results, out, index, pieces, half, t, planes, size):
    tile = slice(t * TILE, (t + 1) * TILE)
    lower = slice(planes + t * TILE, planes + (t + 1) * TILE)
    for f in range(2):
        out[f, index, tile, :] = results[f]
        high, low = split(results[f])
        pieces[f, tile, half * size : (half + 1) * size] = high
        pieces[f, lower, half * size : (half + 1) * size] = low


def beside_face(rows, planes, fields, own_z, halo, lower, to_last, to_first, t):
    at = pl.ds(t * TILE, TILE)
    within = pl.ds(2 + t * TILE, TILE)
    first = jnp.where(lower, 0, rows - 2)

    def window(c):
        own = [fields[c, jnp.where(lower, 0, rows - 4) + i, within, :] for i in range(4)]
        ends = [halo[i][c, at, :] for i in range(2)]
        before = [jnp.where(lower, ends[i], own[i]) for i in range(2)]
        centre = [jnp.where(lower, own[i], own[i + 2]) for i in range(2)]
        after = [jnp.where(lower, own[i + 2], ends[i]) for i in range(2)]
        return before + centre + after

    windows = [window(c) for c in range(3)]
    for i in range(2):
        y = first + i
        z = z_derivatives(own_z, to_last, to_first, t, y, rows)
        along_x = [derivative(*[fields[c, y, pl.ds(2 + t * TILE + k, TILE), :] for k in (-2, -1, 1, 2)]) for c in range(3)]
        along_y = [derivative(*[windows[c][2 + i + k] for k in (-2, -1, 1, 2)]) for c in range(3)]
        turn = along_x[1] - along_y[0]
        shear = along_x[1] + along_y[0]
        stretch = 2.0 * (along_x[0] * along_x[0] + along_y[1] * along_y[1]) + shear * shear
        yield i, finish(turn * turn, stretch, along_x[2], along_y[2], z)


def interior_kernel(
    rows, planes, fields, own_z, spin, stretch, bend_x, bend_y, near_0, near_1, left, right, out, total, pieces, to_last, to_first
):
    size = own_z.shape[3]
    odd = lax.axis_index("gy") % 2 == 1
    to_last[...], to_first[...] = edge_terms(left[...], right[...])
    for pair in range(rows // 2 - 1):
        buffer = pieces.at[pair % 2]
        for t in range(planes // TILE):
            if pair < rows // 2 - 2:
                for half in range(2):
                    index = 2 * pair + half
                    z = z_derivatives(own_z, to_last, to_first, t, index + 2, rows)
                    planar = [ref[index, t * TILE : (t + 1) * TILE, :] for ref in (spin, stretch, bend_x, bend_y)]
                    store_results(finish(*planar, z), out, index, buffer, half, t, planes, size)
            else:
                for half, results in beside_face(rows, planes, fields, own_z, [near_0, near_1], odd, to_last, to_first, t):
                    store_results(results, out, 2 * pair + half, buffer, half, t, planes, size)
        for f in range(2):
            product = square(buffer[f])
            total[f] = product if pair == 0 else total[f] + product


def border_kernel(
    rows, planes, fields, own_z, far, left, right, part, velocity, out, keep, give, message, pieces, to_last, to_first
):
    size = fields.shape[3]
    odd = lax.axis_index("gy") % 2 == 1
    to_last[...], to_first[...] = edge_terms(left[...], right[...])
    for t in range(planes // TILE):
        for half, results in beside_face(rows, planes, fields, own_z, [far.at[:, i] for i in range(2)], ~odd, to_last, to_first, t):
            store_results(results, out, half, pieces, half, t, planes, size)
    grams = [gram_of(part[f] + square(pieces[f])) for f in range(2)] + [velocity[c] for c in range(3)]
    message[0:planes, :] = pack_pair(grams[0], grams[1])
    message[planes : 2 * planes, :] = pack_pair(grams[2], grams[3])
    message[2 * planes : 5 * planes // 2, :] = fold(grams[4])
    for i, f in enumerate((1, 3, 4)):
        message[5 * planes // 2 + i : 5 * planes // 2 + i + 1, :] = diagonal(grams[f])
    used = 5 * planes // 2 + 3
    message[used:, :] = jnp.zeros((message.shape[0] - used, planes), jnp.float32)
    mine, other = half_starts(keep.shape[0])
    keep[...] = message[pl.ds(mine, keep.shape[0]), :]
    give[...] = message[pl.ds(other, keep.shape[0]), :]


def assemble_kernel(rows, planes, f, inner, border, out):
    odd = lax.axis_index("gy") % 2 == 1

    def plane_of(y, at):
        if 2 <= y < rows - 2:
            return inner[f, y - 2, at, :]
        layer = y % (rows - 2)
        beside_near = odd if y < 2 else ~odd
        return jnp.where(beside_near, inner[f, rows - 4 + layer, at, :], border[f, layer, at, :])

    @pl.loop(0, planes // 8)
    def _(t):
        at = pl.ds(pl.multiple_of(t * 8, 8), 8)
        for base in range(0, rows, 8):
            block = jnp.stack([plane_of(y, at) for y in range(base, base + 8)], axis=0)
            out[at, base : base + 8, :] = jnp.swapaxes(block, 0, 1)


def splat(tile, j):
    return jnp.broadcast_to(tile[j : j + 1, :], tile.shape)

def spread_column(tile, at):
    return jnp.broadcast_to(tile[:, at : at + 1], tile.shape)


def factor_tiles(tiles, widths):
    count, size = tiles[0].shape
    sub = lax.broadcasted_iota(jnp.int32, (count, size), 0)
    lane = lax.broadcasted_iota(jnp.int32, (count, size), 1)
    tiles = list(tiles)
    out = []
    first = 0
    for width in widths:
        top = first // count
        head = width // count
        spread = [[spread_column(tiles[top + t], first + j) for t in range(head)] for j in range(width)]
        rows = tiles[top : top + head]
        results = [jnp.zeros((count, size), jnp.float32)] * head
        inverses, entries, pivots = [], {}, []
        pivot = splat(spread[0][0], 0)
        for j in range(width):
            t0, s0 = divmod(j, count)
            inverse = 1.0 / pivot
            inverses.append(inverse)
            for m in range(j + 1, width):
                entries[j, m] = splat(spread[j][m // count], m % count)
            if j + 1 < width:
                t1, s1 = divmod(j + 1, count)
                following = splat(spread[j + 1][t1], s1) - (entries[j, j + 1] * entries[j, j + 1]) * inverse
            row = splat(rows[t0], s0)
            pivots.append(row)
            results[t0] = jnp.where(sub == s0, row * lax.rsqrt(pivot), results[t0])
            for t in range(t0, head):
                scaled = spread[j][t] * inverse
                for m in range(j + 1, width):
                    spread[m][t] = spread[m][t] - scaled * entries[j, m]
                rows[t] = rows[t] - scaled * row
            if j + 1 < width:
                pivot = following
        for t in range(head):
            out.append(jnp.where(lane >= first + t * count + sub, results[t], 0.0))
        for t in range(top + head, len(tiles)):
            tile = tiles[t]
            columns = [spread_column(tile, first + j) for j in range(width)]
            for j in range(width):
                scaled = columns[j] * inverses[j]
                for m in range(j + 1, width):
                    columns[m] = columns[m] - scaled * entries[j, m]
                tile = tile - scaled * pivots[j]
            tiles[t] = tile
        first += width
    return out


def factor_kernel(cells, planes, kept, given, factor, message):
    mine, other = half_starts(kept.shape[0])
    message[pl.ds(mine, kept.shape[0]), :] = kept[...]
    message[pl.ds(other, kept.shape[0]), :] = given[...]
    row, col = halves(planes)
    eye = row == col

    def scale(squares):
        return 1.0 / (5.0 * cells * (squares / (planes * cells) + 1e-06))

    def unpack(packed, second_diagonal):
        first_scale = scale(jnp.sum(jnp.where(eye, packed, 0.0)))
        second_scale = scale(jnp.sum(second_diagonal))
        lower = jnp.where(row > col, packed * first_scale, jnp.where(row < col, packed * second_scale, 0.0))
        both = jnp.where(eye, packed * first_scale + second_diagonal * second_scale, 0.0)
        return lower, both

    diagonals = [message[5 * planes // 2 + i : 5 * planes // 2 + i + 1, :] for i in range(3)]
    low_a, both_a = unpack(message[0:planes, :], diagonals[0])
    low_b, both_b = unpack(message[planes : 2 * planes, :], diagonals[1])
    low_c, both_c = unfold(message[2 * planes : 5 * planes // 2, :], diagonals[2])
    third = scale(jnp.sum(both_c))
    triangles = low_a + low_b + low_c * third
    cross = triangles + triangles.T + (both_a + both_b + both_c * third)
    wide = 16 if planes % 32 == 0 else 8
    widths = [8] * (planes // 16) + [wide] * (planes // 2 // wide)
    upper = factor_tiles([cross[t : t + 8, :] for t in range(0, planes, 8)], widths)
    factor[...] = jnp.concatenate(upper, axis=0).T


def cost(microseconds):
    return pl.CostEstimate(flops=0, bytes_accessed=int(microseconds * 3.69e6), transcendentals=0)


AXES = ("gy", "gz")


def exchange(values, even, odd):
    count_z = lax.axis_size("gz")
    count = lax.axis_size("gy") * count_z
    return lax.ppermute(values, AXES, [(i, i ^ (odd if i // count_z % 2 else even)) for i in range(count)])


def rounds():
    count_y, count_z = lax.axis_size("gy"), lax.axis_size("gz")
    assert count_y & (count_y - 1) == 0 and count_z & (count_z - 1) == 0
    bits = [count_z << i for i in range(1, count_y.bit_length() - 1)] + [1 << i for i in range(count_z.bit_length() - 1)]
    groups = [bits[i : i + 2] for i in range(0, len(bits), 2)]
    return [[group[0]] if len(group) == 1 else [group[0], group[1], group[0] ^ group[1]] for group in groups]


def add_terms(terms):
    while len(terms) > 1:
        terms = [terms[i] + terms[i + 1] for i in range(0, len(terms), 2)]
    return terms[0]


def f32(*shape):
    return jax.ShapeDtypeStruct(shape, jnp.float32)


def per_device(fields):
    planes = fields.shape[1] - 4
    rows, cols = fields.shape[2], fields.shape[3]
    count_y, count_z = lax.axis_size("gy"), lax.axis_size("gz")

    far = pl.pallas_call(
        functools.partial(far_kernel, rows, planes),
        out_shape=f32(3, 2, planes, cols),
        in_specs=[pl.BlockSpec(memory_space=pl.ANY)],
        out_specs=VMEM,
        scratch_shapes=[pltpu.SemaphoreType.DMA((2, 3))],
        compiler_params=params(),
        cost_estimate=cost(1),
        name="far_face",
    )(pltpu.with_memory_space_constraint(fields, pltpu.HBM))
    fields, far = lax.optimization_barrier((fields, far))
    far = lax.ppermute(far, "gy", [(i, (i + 1 if i % 2 else i - 1) % count_y) for i in range(count_y)])
    turned, near_0, near_1, behind, ahead = pl.pallas_call(
        functools.partial(faces_kernel, rows, planes),
        out_shape=(
            pltpu.VMEM((3, rows, planes + 4, cols), jnp.float32),
            f32(3, planes, cols),
            f32(3, planes, cols),
            f32(planes, cols),
            f32(planes, cols),
        ),
        in_specs=[VMEM],
        out_specs=(VMEM,) * 5,
        scratch_shapes=[pltpu.VMEM((planes + 4, cols), jnp.float32)] * 2,
        compiler_params=params(),
        cost_estimate=cost(2.5),
        name="faces",
    )(pltpu.with_memory_space_constraint(fields, pltpu.VMEM))
    near = [lax.ppermute(layer, "gy", [(i, i ^ 1) for i in range(count_y)]) for layer in (near_0, near_1)]
    left = lax.ppermute(ahead, "gz", [(i, (i + 1) % count_z) for i in range(count_z)])
    right = lax.ppermute(behind, "gz", [(i, (i - 1) % count_z) for i in range(count_z)])

    inner_rows = [pltpu.VMEM((rows - 4, planes, cols), jnp.float32)] * 4
    velocity, own_z, *planar = pl.pallas_call(
        functools.partial(inner_kernel, rows, planes),
        out_shape=(f32(3, planes, planes), pltpu.VMEM((3, rows, planes, cols), jnp.float32), *inner_rows),
        in_specs=[VMEM],
        out_specs=(VMEM,) * 6,
        scratch_shapes=[
            pltpu.VMEM((rows, planes, 3 * cols), jnp.bfloat16),
            pltpu.VMEM((3 * cols, cols), jnp.bfloat16),
        ],
        compiler_params=params(),
        cost_estimate=cost(3),
        name="inner",
    )(turned)
    pieces = pltpu.VMEM((2, 2, 2 * planes, 2 * cols), jnp.bfloat16)
    edges = [pltpu.VMEM((planes, cols), jnp.float32)] * 2
    inner, part = pl.pallas_call(
        functools.partial(interior_kernel, rows, planes),
        out_shape=(f32(2, rows - 2, planes, cols), f32(2, 2 * planes, 2 * planes)),
        in_specs=[VMEM] * 10,
        out_specs=(VMEM, VMEM),
        scratch_shapes=[pieces, *edges],
        compiler_params=params(),
        cost_estimate=cost(1.9),
        name="interior",
    )(turned, own_z, *planar, *near, left, right)
    half = -(-(5 * planes // 2 + 3) // 16) * 8
    message = pltpu.VMEM((2 * half, planes), jnp.float32)
    border, keep, give = pl.pallas_call(
        functools.partial(border_kernel, rows, planes),
        out_shape=(f32(2, 2, planes, cols), f32(half, planes), f32(half, planes)),
        in_specs=[VMEM] * 7,
        out_specs=(VMEM, VMEM, VMEM),
        scratch_shapes=[message, pltpu.VMEM((2, 2 * planes, 2 * cols), jnp.bfloat16), *edges],
        compiler_params=params(),
        cost_estimate=cost(0.7),
        name="border",
    )(turned, own_z, far, left, right, part, velocity)
    enstrophy, strain_rate = [
        pl.pallas_call(
            functools.partial(assemble_kernel, rows, planes, f),
            out_shape=f32(planes, rows, cols),
            in_specs=[VMEM] * 2,
            out_specs=VMEM,
            compiler_params=params(),
            cost_estimate=cost(1),
            name="assemble",
        )(inner, border)
        for f in range(2)
    ]
    core = count_z
    kept = keep + exchange(give, core, core)
    masks = rounds()
    outputs = [enstrophy, strain_rate]
    for i, (even, odd) in enumerate(zip(masks, masks[::-1])):
        kept = add_terms([kept] + [exchange(kept, *pair) for pair in zip(even, odd)])
        if i < len(outputs):
            kept, outputs[i] = lax.optimization_barrier((kept, outputs[i]))
    enstrophy, strain_rate = outputs
    given = exchange(kept, core, core)
    cells = rows * cols * count_y * count_z
    factor = pl.pallas_call(
        functools.partial(factor_kernel, float(cells), planes),
        out_shape=f32(planes, planes),
        in_specs=[VMEM] * 2,
        out_specs=VMEM,
        scratch_shapes=[message],
        compiler_params=params(),
        cost_estimate=cost(6),
        name="factor",
    )(kept, given)
    return (enstrophy, strain_rate, factor)


def solution(mesh):
    return jax.shard_map(
        per_device,
        mesh=mesh,
        in_specs=(P(None, None, "gy", "gz"),),
        out_specs=(P(None, "gy", "gz"), P(None, "gy", "gz"), P()),
        check_vma=False,
    )
```

```python
import functools

import jax
import jax.numpy as jnp
from jax import lax
from jax.experimental import pallas as pl
from jax.experimental.pallas import tpu as pltpu
from jax.sharding import PartitionSpec as P

TILE = 16
VMEM = pl.BlockSpec(memory_space=pltpu.VMEM)
DIMS_NT = (((1,), (1,)), ((), ()))


def params(mebibytes=20):
    return pltpu.CompilerParams(vmem_limit_bytes=mebibytes * 1024 * 1024)


def lanes(shape):
    return lax.broadcasted_iota(jnp.int32, shape, 1)


def split(values):
    high = values.astype(jnp.bfloat16)
    low = (values - high.astype(jnp.float32)).astype(jnp.bfloat16)
    return high, low


def gram_of(product):
    size = product.shape[0] // 2
    same = product[:size, :size] + product[size:, size:]
    return same + (product[:size, size:] + product[size:, :size])


def square(pieces):
    return lax.dot_general(pieces, pieces, DIMS_NT, preferred_element_type=jnp.float32)


def halves(size):
    row = lax.broadcasted_iota(jnp.int32, (size, size), 0)
    col = lax.broadcasted_iota(jnp.int32, (size, size), 1)
    return row, col


def pack_pair(first, second):
    row, col = halves(first.shape[0])
    return jnp.where(row >= col, first, second)


def fold(matrix):
    half = matrix.shape[0] // 2
    row = lax.broadcasted_iota(jnp.int32, (half, 2 * half), 0)
    col = lax.broadcasted_iota(jnp.int32, (half, 2 * half), 1)
    first = pltpu.roll(matrix[:half, :], half, 1)
    last = matrix[half:, :]
    return jnp.where((col >= half) & (row >= col - half), first, last)


def unfold(folded):
    half = folded.shape[0]
    row = lax.broadcasted_iota(jnp.int32, folded.shape, 0)
    col = lax.broadcasted_iota(jnp.int32, folded.shape, 1)
    first = jnp.where(row > col, pltpu.roll(folded, half, 1), 0.0)
    last = jnp.where((col < half) | (col - half > row), folded, 0.0)
    return jnp.concatenate([first, last], axis=0)


def half_starts(length):
    core = lax.axis_index("gy") % 2
    return pl.multiple_of(core * length, 8), pl.multiple_of((1 - core) * length, 8)


def diagonal(matrix):
    row, col = halves(matrix.shape[0])
    return jnp.sum(jnp.where(row == col, matrix, 0.0), axis=0, keepdims=True)


def far_kernel(rows, planes, fields, far, arrived):
    first = lax.axis_index("gy") % 2 * (rows - 2)
    copies = []
    for layer in range(2):
        for c in range(3):
            source = fields.at[c, pl.ds(2, planes), first + layer, :]
            copies.append(pltpu.make_async_copy(source, far.at[c, layer], arrived.at[layer, c]))
            copies[-1].start()
    for copy in copies:
        copy.wait()


def faces_kernel(rows, planes, fields, turned_fields, near_0, near_1, behind, ahead, tails, heads):
    odd = lax.axis_index("gy") % 2
    size = fields.shape[3]
    depth = planes + 4
    lane = lanes((8, size))
    near_row = (1 - odd) * (rows - 2)

    def turn(c, first):
        at = pl.ds(first, 8)
        tail = tails[at, :]
        head = heads[at, :]
        for base in range(0, rows, 8):
            block = jnp.swapaxes(fields[c, at, base : base + 8, :], 0, 1)
            for j in range(8):
                y = base + j
                k = c * rows + y
                turned_fields[c, y, at, :] = block[j]
                moved = pltpu.roll(block[j], (2 * k + 2) % size, 1)
                tail = jnp.where(lane >= 2 * k, moved, tail)
                head = jnp.where(lane >= 2 * k + 2, moved, head)
        tails[at, :] = tail
        heads[at, :] = head

    for c in range(3):

        @pl.loop(0, depth // 8, unroll=8)
        def _(t):
            turn(c, pl.multiple_of(t * 8, 8))

        if depth % 8:
            turn(c, depth - 8)
        for layer, near in enumerate((near_0, near_1)):
            near[c] = turned_fields[c, near_row + layer, 2 : planes + 2, :]
    ahead[...] = tails[2 : planes + 2, :]
    behind[...] = heads[2 : planes + 2, :]


def derivative(minus_two, minus_one, plus_one, plus_two):
    return 8.0 * (plus_one - minus_one) - (plus_two - minus_two)


def inner_kernel(rows, planes, fields, grams, along_z, spin, stretch, bend_x, bend_y, thirds, band):
    size = fields.shape[3]
    row = lax.broadcasted_iota(jnp.int32, (3 * size, size), 0) % size
    col = lax.broadcasted_iota(jnp.int32, (3 * size, size), 1)
    far_side = jnp.where(row == col - 2, 1.0, jnp.where(row == col + 2, -1.0, 0.0))
    near_side = jnp.where(row == col - 1, -8.0, jnp.where(row == col + 1, 8.0, 0.0))
    band[...] = (far_side + near_side).astype(jnp.bfloat16)

    def planar(index, t):
        y = index + 2
        at = pl.ds(t * TILE, TILE)
        x, y = [
            [
                derivative(*[fields[c, y + k * step, pl.ds(2 + t * TILE + k * (1 - step), TILE), :] for k in (-2, -1, 1, 2)])
                for c in range(3)
            ]
            for step in (0, 1)
        ]
        turn = x[1] - y[0]
        shear = x[1] + y[0]
        spin[index, at, :] = turn * turn
        stretch[index, at, :] = 2.0 * (x[0] * x[0] + y[1] * y[1]) + shear * shear
        bend_x[index, at, :] = x[2]
        bend_y[index, at, :] = y[2]

    tiles = [(index, t) for index in range(rows - 4) for t in range(planes // TILE)]
    done = 0
    for c in range(3):
        total = None
        for y in range(rows):
            for t in range(planes // TILE):
                cells = fields[c, y, 2 + t * TILE : 2 + (t + 1) * TILE, :]
                high = cells.astype(jnp.bfloat16)
                rest = cells - high.astype(jnp.float32)
                middle = rest.astype(jnp.bfloat16)
                low = (rest - middle.astype(jnp.float32)).astype(jnp.bfloat16)
                for part, piece in enumerate((high, middle, low)):
                    thirds[y, t * TILE : (t + 1) * TILE, part * size : (part + 1) * size] = piece
            if y % 2 == 1:
                parts = [
                    jnp.concatenate([thirds[y - 1, :, at : at + size], thirds[y, :, at : at + size]], axis=1)
                    for at in (0, size)
                ]
                product = square(jnp.concatenate(parts, axis=0))
                total = product if y == 1 else total + product
            upto = len(tiles) * (c * rows + y + 1) // (3 * rows)
            for tile in tiles[done:upto]:
                planar(*tile)
            done = upto
        grams[c] = gram_of(total)
        derivatives = jnp.dot(
            thirds[...].reshape(rows * planes, 3 * size), band[...], preferred_element_type=jnp.float32
        )
        along_z[c] = derivatives.reshape(rows, planes, size)


def edge_terms(left, right):
    size = left.shape[1]
    even = lanes(left.shape) % 2 == 0
    left = pltpu.roll(left, 2, 1)
    right = pltpu.roll(right, size - 2, 1)
    to_last = jnp.where(even, -right, 8.0 * pltpu.roll(right, 1, 1) - right)
    to_first = jnp.where(even, left - 8.0 * pltpu.roll(left, size - 1, 1), left)
    return to_last, to_first


def z_derivatives(own_z, to_last, to_first, t, y, rows):
    size = own_z.shape[3]
    lane = lanes((TILE, size))
    edge = (lane < 2) | (lane >= size - 2)
    at = pl.ds(t * TILE, TILE)
    along_z = []
    for c in range(3):
        k = c * rows + y
        terms = jnp.where(lane < 2 * k + 2, to_last[at, :], to_first[at, :])
        terms = pltpu.roll(terms, (2 * size - 2 - 2 * k) % size, 1)
        along_z.append(own_z[c, y, at, :] + jnp.where(edge, terms, 0.0))
    return along_z


def finish(spin, stretch, bend_x, bend_y, z):
    turn_x, turn_y = bend_x - z[0], bend_y - z[1]
    shear_x, shear_y = bend_x + z[0], bend_y + z[1]
    enstrophy = spin + turn_x * turn_x + turn_y * turn_y
    strain = stretch + 2.0 * (z[2] * z[2]) + (shear_x * shear_x + shear_y * shear_y)
    return enstrophy * (1.0 / 288.0), strain * (1.0 / 288.0)


def store_results(results, out, index, pieces, half, t, planes, size):
    tile = slice(t * TILE, (t + 1) * TILE)
    lower = slice(planes + t * TILE, planes + (t + 1) * TILE)
    for f in range(2):
        out[f, index, tile, :] = results[f]
        high, low = split(results[f])
        pieces[f, tile, half * size : (half + 1) * size] = high
        pieces[f, lower, half * size : (half + 1) * size] = low


def beside_face(rows, planes, fields, own_z, halo, lower, to_last, to_first, t):
    at = pl.ds(t * TILE, TILE)
    within = pl.ds(2 + t * TILE, TILE)
    first = jnp.where(lower, 0, rows - 2)

    def window(c):
        own = [fields[c, jnp.where(lower, 0, rows - 4) + i, within, :] for i in range(4)]
        ends = [halo[i][c, at, :] for i in range(2)]
        before = [jnp.where(lower, ends[i], own[i]) for i in range(2)]
        centre = [jnp.where(lower, own[i], own[i + 2]) for i in range(2)]
        after = [jnp.where(lower, own[i + 2], ends[i]) for i in range(2)]
        return before + centre + after

    windows = [window(c) for c in range(3)]
    for i in range(2):
        y = first + i
        z = z_derivatives(own_z, to_last, to_first, t, y, rows)
        along_x = [derivative(*[fields[c, y, pl.ds(2 + t * TILE + k, TILE), :] for k in (-2, -1, 1, 2)]) for c in range(3)]
        along_y = [derivative(*[windows[c][2 + i + k] for k in (-2, -1, 1, 2)]) for c in range(3)]
        turn = along_x[1] - along_y[0]
        shear = along_x[1] + along_y[0]
        stretch = 2.0 * (along_x[0] * along_x[0] + along_y[1] * along_y[1]) + shear * shear
        yield i, finish(turn * turn, stretch, along_x[2], along_y[2], z)


def interior_kernel(
    rows, planes, fields, own_z, spin, stretch, bend_x, bend_y, near_0, near_1, left, right, out, total, to_last, to_first, pieces
):
    size = own_z.shape[3]
    odd = lax.axis_index("gy") % 2 == 1
    to_last[...], to_first[...] = edge_terms(left[...], right[...])
    for pair in range(rows // 2 - 1):
        buffer = pieces.at[pair % 2]
        for t in range(planes // TILE):
            if pair < rows // 2 - 2:
                for half in range(2):
                    index = 2 * pair + half
                    z = z_derivatives(own_z, to_last, to_first, t, index + 2, rows)
                    planar = [ref[index, t * TILE : (t + 1) * TILE, :] for ref in (spin, stretch, bend_x, bend_y)]
                    store_results(finish(*planar, z), out, index, buffer, half, t, planes, size)
            else:
                for half, results in beside_face(rows, planes, fields, own_z, [near_0, near_1], odd, to_last, to_first, t):
                    store_results(results, out, 2 * pair + half, buffer, half, t, planes, size)
        for f in range(2):
            product = square(buffer[f])
            total[f] = product if pair == 0 else total[f] + product


def border_kernel(
    rows, planes, fields, own_z, far, to_last, to_first, part, velocity, out, keep, give, message, pieces
):
    size = fields.shape[3]
    odd = lax.axis_index("gy") % 2 == 1
    for t in range(planes // TILE):
        for half, results in beside_face(rows, planes, fields, own_z, [far.at[:, i] for i in range(2)], ~odd, to_last, to_first, t):
            store_results(results, out, half, pieces, half, t, planes, size)
    grams = [gram_of(part[f] + square(pieces[f])) for f in range(2)] + [velocity[c] for c in range(3)]
    message[0:planes, :] = pack_pair(grams[0], grams[1])
    message[planes : 2 * planes, :] = pack_pair(grams[2], grams[3])
    message[2 * planes : 5 * planes // 2, :] = fold(grams[4])
    for i, gram in enumerate(grams):
        message[5 * planes // 2 + i : 5 * planes // 2 + i + 1, :] = diagonal(gram)
    used = 5 * planes // 2 + 5
    message[used:, :] = jnp.zeros((message.shape[0] - used, planes), jnp.float32)
    mine, other = half_starts(keep.shape[0])
    keep[...] = message[pl.ds(mine, keep.shape[0]), :]
    give[...] = message[pl.ds(other, keep.shape[0]), :]


def assemble_kernel(rows, planes, f, inner, border, out):
    odd = lax.axis_index("gy") % 2 == 1

    def plane_of(y, at):
        if 2 <= y < rows - 2:
            return inner[f, y - 2, at, :]
        layer = y % (rows - 2)
        beside_near = odd if y < 2 else ~odd
        return jnp.where(beside_near, inner[f, rows - 4 + layer, at, :], border[f, layer, at, :])

    @pl.loop(0, planes // 8)
    def _(t):
        at = pl.ds(pl.multiple_of(t * 8, 8), 8)
        for base in range(0, rows, 8):
            block = jnp.stack([plane_of(y, at) for y in range(base, base + 8)], axis=0)
            out[at, base : base + 8, :] = jnp.swapaxes(block, 0, 1)


def splat(tile, j):
    return jnp.broadcast_to(tile[j : j + 1, :], tile.shape)

def spread_column(tile, at):
    return jnp.broadcast_to(tile[:, at : at + 1], tile.shape)


def thirds_of(values):
    high = values.astype(jnp.bfloat16).astype(jnp.float32)
    rest = values - high
    middle = rest.astype(jnp.bfloat16).astype(jnp.float32)
    return high, middle, rest - middle


def eliminate(rows, first, width):
    count, size = rows[0].shape
    sub = lax.broadcasted_iota(jnp.int32, (count, size), 0)
    lane = lax.broadcasted_iota(jnp.int32, (count, size), 1)
    head = width // count
    tall = len(rows)
    made = [[spread_column(rows[t], first + j) for j in range(width)] for t in range(tall)]
    spread = [[made[t][j] for t in range(tall)] for j in range(width)]
    rows = list(rows)
    results = [jnp.zeros((count, size), jnp.float32)] * head
    entries = {}
    pivot = splat(spread[0][0], 0)
    for j in range(width):
        t0, s0 = divmod(j, count)
        inverse = 1.0 / pivot
        for m in range(j + 1, width):
            entries[j, m] = splat(spread[j][m // count], m % count)
        if j + 1 < width:
            t1, s1 = divmod(j + 1, count)
            following = splat(spread[j + 1][t1], s1) - (entries[j, j + 1] * entries[j, j + 1]) * inverse
        row = splat(rows[t0], s0)
        results[t0] = jnp.where(sub == s0, row * lax.rsqrt(pivot), results[t0])
        for t in range(t0, tall):
            scaled = spread[j][t] * inverse
            for m in range(j + 1, width):
                spread[m][t] = spread[m][t] - scaled * entries[j, m]
            rows[t] = rows[t] - scaled * row
        if j + 1 < width:
            pivot = following
    results = [jnp.where(lane >= first + t * count + sub, results[t], 0.0) for t in range(head)]
    return results, rows[head:]


def factor_tiles(tiles, widths):
    count = tiles[0].shape[0]
    tiles = list(tiles)
    out = []
    first = 0
    for i, width in enumerate(widths):
        top, after = first // count, (first + width) // count
        end = after + sum(widths[i + 1 : i + 3]) // count
        results, tiles[after:end] = eliminate(tiles[top:end], first, width)
        out += results
        if end < len(tiles):
            high, middle, low = thirds_of(jnp.concatenate(results, axis=0))
            one = jnp.concatenate([high, high, middle, high, low, middle], axis=0).astype(jnp.bfloat16)
            two = jnp.concatenate([high, middle, high, low, high, middle], axis=0).astype(jnp.bfloat16)
            update = lax.dot_general(one, two, (((0,), (0,)), ((), ())), preferred_element_type=jnp.float32)
            for t in range(end, len(tiles)):
                tiles[t] = tiles[t] - update[t * count : (t + 1) * count, :]
        first += width
    return out


def factor_kernel(cells, planes, kept, given, factor, message):
    mine, other = half_starts(kept.shape[0])
    message[pl.ds(mine, kept.shape[0]), :] = kept[...]
    message[pl.ds(other, kept.shape[0]), :] = given[...]
    row, col = halves(planes)
    eye = row == col
    diagonals = message[5 * planes // 2 : 5 * planes // 2 + 8, :]
    squares = jnp.broadcast_to(jnp.sum(diagonals, axis=1, keepdims=True), diagonals.shape)
    scales = 1.0 / (5.0 * cells * (squares / (planes * cells) + 1e-06))
    scaled = diagonals * scales
    scale = [scales[i : i + 1, :] for i in range(5)]

    def pair(packed, first):
        return jnp.where(row > col, packed * scale[first], packed * scale[first + 1])

    folded = unfold(message[2 * planes : 5 * planes // 2, :])
    triangles = jnp.where(eye, 0.0, pair(message[0:planes, :], 0) + pair(message[planes : 2 * planes, :], 2))
    triangles = triangles + folded * scale[4]
    cross = triangles + triangles.T + jnp.where(eye, jnp.sum(scaled[0:5], axis=0, keepdims=True), 0.0)
    narrow = planes // 64 * 2
    widths = [8] * narrow + [16] * (planes // 16 - narrow // 2)
    upper = factor_tiles([cross[t : t + 8, :] for t in range(0, planes, 8)], widths)
    factor[...] = jnp.concatenate(upper, axis=0).T


def cost(microseconds):
    return pl.CostEstimate(flops=0, bytes_accessed=int(microseconds * 3.69e6), transcendentals=0)


AXES = ("gy", "gz")


def exchange(values, even, odd):
    count_z = lax.axis_size("gz")
    count = lax.axis_size("gy") * count_z
    return lax.ppermute(values, AXES, [(i, i ^ (odd if i // count_z % 2 else even)) for i in range(count)])


def rounds():
    count_y, count_z = lax.axis_size("gy"), lax.axis_size("gz")
    assert count_y & (count_y - 1) == 0 and count_z & (count_z - 1) == 0
    bits = [count_z << i for i in range(1, count_y.bit_length() - 1)] + [1 << i for i in range(count_z.bit_length() - 1)]
    groups = [bits[i : i + 2] for i in range(0, len(bits), 2)]
    return [[group[0]] if len(group) == 1 else [group[0], group[1], group[0] ^ group[1]] for group in groups]


def add_terms(terms):
    while len(terms) > 1:
        terms = [terms[i] + terms[i + 1] for i in range(0, len(terms), 2)]
    return terms[0]


def f32(*shape):
    return jax.ShapeDtypeStruct(shape, jnp.float32)


def per_device(fields):
    planes = fields.shape[1] - 4
    rows, cols = fields.shape[2], fields.shape[3]
    count_y, count_z = lax.axis_size("gy"), lax.axis_size("gz")

    far = pl.pallas_call(
        functools.partial(far_kernel, rows, planes),
        out_shape=f32(3, 2, planes, cols),
        in_specs=[pl.BlockSpec(memory_space=pl.ANY)],
        out_specs=VMEM,
        scratch_shapes=[pltpu.SemaphoreType.DMA((2, 3))],
        compiler_params=params(),
        cost_estimate=cost(1),
        name="far_face",
    )(pltpu.with_memory_space_constraint(fields, pltpu.HBM))
    fields, far = lax.optimization_barrier((fields, far))
    far = lax.ppermute(far, "gy", [(i, (i + 1 if i % 2 else i - 1) % count_y) for i in range(count_y)])
    turned, near_0, near_1, behind, ahead = pl.pallas_call(
        functools.partial(faces_kernel, rows, planes),
        out_shape=(
            pltpu.VMEM((3, rows, planes + 4, cols), jnp.float32),
            f32(3, planes, cols),
            f32(3, planes, cols),
            f32(planes, cols),
            f32(planes, cols),
        ),
        in_specs=[VMEM],
        out_specs=(VMEM,) * 5,
        scratch_shapes=[pltpu.VMEM((planes + 4, cols), jnp.float32)] * 2,
        compiler_params=params(),
        cost_estimate=cost(2.5),
        name="faces",
    )(pltpu.with_memory_space_constraint(fields, pltpu.VMEM))
    near = [lax.ppermute(layer, "gy", [(i, i ^ 1) for i in range(count_y)]) for layer in (near_0, near_1)]
    left = lax.ppermute(ahead, "gz", [(i, (i + 1) % count_z) for i in range(count_z)])
    right = lax.ppermute(behind, "gz", [(i, (i - 1) % count_z) for i in range(count_z)])

    inner_rows = [pltpu.VMEM((rows - 4, planes, cols), jnp.float32)] * 4
    velocity, own_z, *planar = pl.pallas_call(
        functools.partial(inner_kernel, rows, planes),
        out_shape=(f32(3, planes, planes), pltpu.VMEM((3, rows, planes, cols), jnp.float32), *inner_rows),
        in_specs=[VMEM],
        out_specs=(VMEM,) * 6,
        scratch_shapes=[
            pltpu.VMEM((rows, planes, 3 * cols), jnp.bfloat16),
            pltpu.VMEM((3 * cols, cols), jnp.bfloat16),
        ],
        compiler_params=params(),
        cost_estimate=cost(3),
        name="inner",
    )(turned)
    pieces = pltpu.VMEM((2, 2, 2 * planes, 2 * cols), jnp.bfloat16)
    inner, part, to_last, to_first = pl.pallas_call(
        functools.partial(interior_kernel, rows, planes),
        out_shape=(
            f32(2, rows - 2, planes, cols),
            f32(2, 2 * planes, 2 * planes),
            f32(planes, cols),
            f32(planes, cols),
        ),
        in_specs=[VMEM] * 10,
        out_specs=(VMEM,) * 4,
        scratch_shapes=[pieces],
        compiler_params=params(),
        cost_estimate=cost(1.9),
        name="interior",
    )(turned, own_z, *planar, *near, left, right)
    half = -(-(5 * planes // 2 + 8) // 16) * 8
    message = pltpu.VMEM((2 * half, planes), jnp.float32)
    border, keep, give = pl.pallas_call(
        functools.partial(border_kernel, rows, planes),
        out_shape=(f32(2, 2, planes, cols), f32(half, planes), f32(half, planes)),
        in_specs=[VMEM] * 7,
        out_specs=(VMEM, VMEM, VMEM),
        scratch_shapes=[message, pltpu.VMEM((2, 2 * planes, 2 * cols), jnp.bfloat16)],
        compiler_params=params(),
        cost_estimate=cost(0.7),
        name="border",
    )(turned, own_z, far, to_last, to_first, part, velocity)
    enstrophy, strain_rate = [
        pl.pallas_call(
            functools.partial(assemble_kernel, rows, planes, f),
            out_shape=f32(planes, rows, cols),
            in_specs=[VMEM] * 2,
            out_specs=VMEM,
            compiler_params=params(),
            cost_estimate=cost(1),
            name="assemble",
        )(inner, border)
        for f in range(2)
    ]
    core = count_z
    kept = keep + exchange(give, core, core)
    masks = rounds()
    outputs = [enstrophy, strain_rate]
    for i, (even, odd) in enumerate(zip(masks, masks[::-1])):
        kept = add_terms([kept] + [exchange(kept, *pair) for pair in zip(even, odd)])
        if i < len(outputs):
            kept, outputs[i] = lax.optimization_barrier((kept, outputs[i]))
    enstrophy, strain_rate = outputs
    given = exchange(kept, core, core)
    cells = rows * cols * count_y * count_z
    factor = pl.pallas_call(
        functools.partial(factor_kernel, float(cells), planes),
        out_shape=f32(planes, planes),
        in_specs=[VMEM] * 2,
        out_specs=VMEM,
        scratch_shapes=[message],
        compiler_params=params(),
        cost_estimate=cost(6),
        name="factor",
    )(kept, given)
    return (enstrophy, strain_rate, factor)


def solution(mesh):
    return jax.shard_map(
        per_device,
        mesh=mesh,
        in_specs=(P(None, None, "gy", "gz"),),
        out_specs=(P(None, "gy", "gz"), P(None, "gy", "gz"), P()),
        check_vma=False,
    )
```

```python
import functools

import jax
import jax.numpy as jnp
from jax import lax
from jax.experimental import pallas as pl
from jax.experimental.pallas import tpu as pltpu
from jax.sharding import PartitionSpec as P

TILE = 16
VMEM = pl.BlockSpec(memory_space=pltpu.VMEM)
DIMS_NT = (((1,), (1,)), ((), ()))


def params(mebibytes=20):
    return pltpu.CompilerParams(vmem_limit_bytes=mebibytes * 1024 * 1024)


def lanes(shape):
    return lax.broadcasted_iota(jnp.int32, shape, 1)


def split(values):
    high = values.astype(jnp.bfloat16)
    low = (values - high.astype(jnp.float32)).astype(jnp.bfloat16)
    return high, low


def gram_of(product):
    size = product.shape[0] // 2
    same = product[:size, :size] + product[size:, size:]
    return same + (product[:size, size:] + product[size:, :size])


def square(pieces):
    return lax.dot_general(pieces, pieces, DIMS_NT, preferred_element_type=jnp.float32)


def halves(size):
    row = lax.broadcasted_iota(jnp.int32, (size, size), 0)
    col = lax.broadcasted_iota(jnp.int32, (size, size), 1)
    return row, col


def pack_pair(first, second):
    row, col = halves(first.shape[0])
    return jnp.where(row >= col, first, second)


def fold(matrix):
    half = matrix.shape[0] // 2
    row = lax.broadcasted_iota(jnp.int32, (half, 2 * half), 0)
    col = lax.broadcasted_iota(jnp.int32, (half, 2 * half), 1)
    first = pltpu.roll(matrix[:half, :], half, 1)
    last = matrix[half:, :]
    return jnp.where((col >= half) & (row >= col - half), first, last)


def unfold(folded):
    half = folded.shape[0]
    row = lax.broadcasted_iota(jnp.int32, folded.shape, 0)
    col = lax.broadcasted_iota(jnp.int32, folded.shape, 1)
    first = jnp.where(row > col, pltpu.roll(folded, half, 1), 0.0)
    last = jnp.where((col < half) | (col - half > row), folded, 0.0)
    return jnp.concatenate([first, last], axis=0)


def half_starts(length):
    core = lax.axis_index("gy") % 2
    return pl.multiple_of(core * length, 8), pl.multiple_of((1 - core) * length, 8)


def diagonal(matrix):
    row, col = halves(matrix.shape[0])
    return jnp.sum(jnp.where(row == col, matrix, 0.0), axis=0, keepdims=True)


def far_kernel(rows, planes, fields, far, arrived):
    first = lax.axis_index("gy") % 2 * (rows - 2)
    copies = []
    for layer in range(2):
        for c in range(3):
            source = fields.at[c, pl.ds(2, planes), first + layer, :]
            copies.append(pltpu.make_async_copy(source, far.at[pl.ds((3 * layer + c) * planes, planes)], arrived.at[layer, c]))
            copies[-1].start()
    far[6 * planes :, :] = jnp.zeros((far.shape[0] - 6 * planes, far.shape[1]), jnp.float32)
    for copy in copies:
        copy.wait()


def faces_kernel(rows, planes, fields, turned_fields, near, behind, ahead, tails, heads):
    odd = lax.axis_index("gy") % 2
    size = fields.shape[3]
    depth = planes + 4
    lane = lanes((8, size))
    near_row = (1 - odd) * (rows - 2)

    def turn(c, first):
        at = pl.ds(first, 8)
        tail = tails[at, :]
        head = heads[at, :]
        for base in range(0, rows, 8):
            block = jnp.swapaxes(fields[c, at, base : base + 8, :], 0, 1)
            for j in range(8):
                y = base + j
                k = c * rows + y
                turned_fields[c, y, at, :] = block[j]
                moved = pltpu.roll(block[j], (2 * k + 2) % size, 1)
                tail = jnp.where(lane >= 2 * k, moved, tail)
                head = jnp.where(lane >= 2 * k + 2, moved, head)
        tails[at, :] = tail
        heads[at, :] = head

    for c in range(3):

        @pl.loop(0, depth // 8, unroll=8)
        def _(t):
            turn(c, pl.multiple_of(t * 8, 8))

        if depth % 8:
            turn(c, depth - 8)
        for layer in range(2):
            near[layer, c] = turned_fields[c, near_row + layer, 2 : planes + 2, :]
    ahead[...] = tails[2 : planes + 2, :]
    behind[...] = heads[2 : planes + 2, :]


def derivative(minus_two, minus_one, plus_one, plus_two):
    return 8.0 * (plus_one - minus_one) - (plus_two - minus_two)


def inner_kernel(rows, planes, fields, grams, along_z, spin, stretch, bend_x, bend_y, thirds, band):
    size = fields.shape[3]
    row = lax.broadcasted_iota(jnp.int32, (3 * size, size), 0) % size
    col = lax.broadcasted_iota(jnp.int32, (3 * size, size), 1)
    far_side = jnp.where(row == col - 2, 1.0, jnp.where(row == col + 2, -1.0, 0.0))
    near_side = jnp.where(row == col - 1, -8.0, jnp.where(row == col + 1, 8.0, 0.0))
    band[...] = (far_side + near_side).astype(jnp.bfloat16)

    def planar(index, t):
        y = index + 2
        at = pl.ds(t * TILE, TILE)
        x, y = [
            [
                derivative(*[fields[c, y + k * step, pl.ds(2 + t * TILE + k * (1 - step), TILE), :] for k in (-2, -1, 1, 2)])
                for c in range(3)
            ]
            for step in (0, 1)
        ]
        turn = x[1] - y[0]
        shear = x[1] + y[0]
        spin[index, at, :] = turn * turn
        stretch[index, at, :] = 2.0 * (x[0] * x[0] + y[1] * y[1]) + shear * shear
        bend_x[index, at, :] = x[2]
        bend_y[index, at, :] = y[2]

    tiles = [(index, t) for index in range(rows - 4) for t in range(planes // TILE)]
    done = 0
    for c in range(3):
        total = None
        for y in range(rows):
            for t in range(planes // TILE):
                cells = fields[c, y, 2 + t * TILE : 2 + (t + 1) * TILE, :]
                high = cells.astype(jnp.bfloat16)
                rest = cells - high.astype(jnp.float32)
                middle = rest.astype(jnp.bfloat16)
                low = (rest - middle.astype(jnp.float32)).astype(jnp.bfloat16)
                for part, piece in enumerate((high, middle, low)):
                    thirds[y, t * TILE : (t + 1) * TILE, part * size : (part + 1) * size] = piece
            if y % 2 == 1:
                parts = [
                    jnp.concatenate([thirds[y - 1, :, at : at + size], thirds[y, :, at : at + size]], axis=1)
                    for at in (0, size)
                ]
                product = square(jnp.concatenate(parts, axis=0))
                total = product if y == 1 else total + product
            upto = len(tiles) * (c * rows + y + 1) // (3 * rows)
            for tile in tiles[done:upto]:
                planar(*tile)
            done = upto
        grams[c] = gram_of(total)
        derivatives = jnp.dot(
            thirds[...].reshape(rows * planes, 3 * size), band[...], preferred_element_type=jnp.float32
        )
        along_z[c] = derivatives.reshape(rows, planes, size)


def edge_terms(left, right):
    size = left.shape[1]
    even = lanes(left.shape) % 2 == 0
    left = pltpu.roll(left, 2, 1)
    right = pltpu.roll(right, size - 2, 1)
    to_last = jnp.where(even, -right, 8.0 * pltpu.roll(right, 1, 1) - right)
    to_first = jnp.where(even, left - 8.0 * pltpu.roll(left, size - 1, 1), left)
    return to_last, to_first


def z_derivatives(own_z, to_last, to_first, t, y, rows):
    size = own_z.shape[3]
    lane = lanes((TILE, size))
    edge = (lane < 2) | (lane >= size - 2)
    at = pl.ds(t * TILE, TILE)
    along_z = []
    for c in range(3):
        k = c * rows + y
        terms = jnp.where(lane < 2 * k + 2, to_last[at, :], to_first[at, :])
        terms = pltpu.roll(terms, (2 * size - 2 - 2 * k) % size, 1)
        along_z.append(own_z[c, y, at, :] + jnp.where(edge, terms, 0.0))
    return along_z


def finish(spin, stretch, bend_x, bend_y, z):
    turn_x, turn_y = bend_x - z[0], bend_y - z[1]
    shear_x, shear_y = bend_x + z[0], bend_y + z[1]
    enstrophy = spin + turn_x * turn_x + turn_y * turn_y
    strain = stretch + 2.0 * (z[2] * z[2]) + (shear_x * shear_x + shear_y * shear_y)
    return enstrophy * (1.0 / 288.0), strain * (1.0 / 288.0)


def store_results(results, out, index, pieces, half, t, planes, size):
    tile = slice(t * TILE, (t + 1) * TILE)
    lower = slice(planes + t * TILE, planes + (t + 1) * TILE)
    for f in range(2):
        out[f, index, tile, :] = results[f]
        high, low = split(results[f])
        pieces[f, tile, half * size : (half + 1) * size] = high
        pieces[f, lower, half * size : (half + 1) * size] = low


def beside_face(rows, planes, fields, own_z, halo, lower, to_last, to_first, t):
    at = pl.ds(t * TILE, TILE)
    within = pl.ds(2 + t * TILE, TILE)
    first = jnp.where(lower, 0, rows - 2)

    def window(c):
        own = [fields[c, jnp.where(lower, 0, rows - 4) + i, within, :] for i in range(4)]
        ends = [halo[i][c][at, :] for i in range(2)]
        before = [jnp.where(lower, ends[i], own[i]) for i in range(2)]
        centre = [jnp.where(lower, own[i], own[i + 2]) for i in range(2)]
        after = [jnp.where(lower, own[i + 2], ends[i]) for i in range(2)]
        return before + centre + after

    windows = [window(c) for c in range(3)]
    for i in range(2):
        y = first + i
        z = z_derivatives(own_z, to_last, to_first, t, y, rows)
        along_x = [derivative(*[fields[c, y, pl.ds(2 + t * TILE + k, TILE), :] for k in (-2, -1, 1, 2)]) for c in range(3)]
        along_y = [derivative(*[windows[c][2 + i + k] for k in (-2, -1, 1, 2)]) for c in range(3)]
        turn = along_x[1] - along_y[0]
        shear = along_x[1] + along_y[0]
        stretch = 2.0 * (along_x[0] * along_x[0] + along_y[1] * along_y[1]) + shear * shear
        yield i, finish(turn * turn, stretch, along_x[2], along_y[2], z)


def interior_kernel(
    rows, planes, fields, own_z, spin, stretch, bend_x, bend_y, near, left, right, out, total, to_last, to_first, pieces
):
    size = own_z.shape[3]
    odd = lax.axis_index("gy") % 2 == 1
    to_last[...], to_first[...] = edge_terms(left[...], right[...])
    for pair in range(rows // 2 - 1):
        buffer = pieces.at[pair % 2]
        for t in range(planes // TILE):
            if pair < rows // 2 - 2:
                for half in range(2):
                    index = 2 * pair + half
                    z = z_derivatives(own_z, to_last, to_first, t, index + 2, rows)
                    planar = [ref[index, t * TILE : (t + 1) * TILE, :] for ref in (spin, stretch, bend_x, bend_y)]
                    store_results(finish(*planar, z), out, index, buffer, half, t, planes, size)
            else:
                for half, results in beside_face(rows, planes, fields, own_z, [[near.at[i, c] for c in range(3)] for i in range(2)], odd, to_last, to_first, t):
                    store_results(results, out, 2 * pair + half, buffer, half, t, planes, size)
        for f in range(2):
            product = square(buffer[f])
            total[f] = product if pair == 0 else total[f] + product


def border_kernel(
    rows, planes, fields, own_z, far, to_last, to_first, part, velocity, out, keep, give, message, pieces
):
    size = fields.shape[3]
    odd = lax.axis_index("gy") % 2 == 1
    halo = [[far.at[pl.ds((3 * i + c) * planes, planes)] for c in range(3)] for i in range(2)]
    for t in range(planes // TILE):
        for half, results in beside_face(rows, planes, fields, own_z, halo, ~odd, to_last, to_first, t):
            store_results(results, out, half, pieces, half, t, planes, size)
    grams = [gram_of(part[f] + square(pieces[f])) for f in range(2)] + [velocity[c] for c in range(3)]
    message[0:planes, :] = pack_pair(grams[0], grams[1])
    message[planes : 2 * planes, :] = pack_pair(grams[2], grams[3])
    message[2 * planes : 5 * planes // 2, :] = fold(grams[4])
    for i, gram in enumerate(grams):
        message[5 * planes // 2 + i : 5 * planes // 2 + i + 1, :] = diagonal(gram)
    used = 5 * planes // 2 + 5
    message[used:, :] = jnp.zeros((message.shape[0] - used, planes), jnp.float32)
    mine, other = half_starts(keep.shape[0])
    keep[...] = message[pl.ds(mine, keep.shape[0]), :]
    give[...] = message[pl.ds(other, keep.shape[0]), :]


def assemble_kernel(rows, planes, f, inner, border, out):
    odd = lax.axis_index("gy") % 2 == 1

    def plane_of(y, at):
        if 2 <= y < rows - 2:
            return inner[f, y - 2, at, :]
        layer = y % (rows - 2)
        beside_near = odd if y < 2 else ~odd
        return jnp.where(beside_near, inner[f, rows - 4 + layer, at, :], border[f, layer, at, :])

    @pl.loop(0, planes // 8)
    def _(t):
        at = pl.ds(pl.multiple_of(t * 8, 8), 8)
        for base in range(0, rows, 8):
            block = jnp.stack([plane_of(y, at) for y in range(base, base + 8)], axis=0)
            out[at, base : base + 8, :] = jnp.swapaxes(block, 0, 1)


def splat(tile, j):
    return jnp.broadcast_to(tile[j : j + 1, :], tile.shape)

def spread_column(tile, at):
    return jnp.broadcast_to(tile[:, at : at + 1], tile.shape)


def thirds_of(values):
    high = values.astype(jnp.bfloat16).astype(jnp.float32)
    rest = values - high
    middle = rest.astype(jnp.bfloat16).astype(jnp.float32)
    return high, middle, rest - middle


def eliminate(rows, first, width):
    count, size = rows[0].shape
    sub = lax.broadcasted_iota(jnp.int32, (count, size), 0)
    lane = lax.broadcasted_iota(jnp.int32, (count, size), 1)
    head = width // count
    tall = len(rows)
    made = [[spread_column(rows[t], first + j) for j in range(width)] for t in range(tall)]
    spread = [[made[t][j] for t in range(tall)] for j in range(width)]
    rows = list(rows)
    results = [jnp.zeros((count, size), jnp.float32)] * head
    entries = {}
    pivot = splat(spread[0][0], 0)
    for j in range(width):
        t0, s0 = divmod(j, count)
        inverse = 1.0 / pivot
        for m in range(j + 1, width):
            entries[j, m] = splat(spread[j][m // count], m % count)
        if j + 1 < width:
            t1, s1 = divmod(j + 1, count)
            following = splat(spread[j + 1][t1], s1) - (entries[j, j + 1] * entries[j, j + 1]) * inverse
        row = splat(rows[t0], s0)
        results[t0] = jnp.where(sub == s0, row * lax.rsqrt(pivot), results[t0])
        for t in range(t0, tall):
            scaled = spread[j][t] * inverse
            for m in range(j + 1, width):
                spread[m][t] = spread[m][t] - scaled * entries[j, m]
            rows[t] = rows[t] - scaled * row
        if j + 1 < width:
            pivot = following
    results = [jnp.where(lane >= first + t * count + sub, results[t], 0.0) for t in range(head)]
    return results, rows[head:]


def factor_tiles(tiles, widths):
    count = tiles[0].shape[0]
    tiles = list(tiles)
    out = []
    first = 0
    for i, width in enumerate(widths):
        top, after = first // count, (first + width) // count
        end = after + sum(widths[i + 1 : i + 3]) // count
        results, tiles[after:end] = eliminate(tiles[top:end], first, width)
        out += results
        if end < len(tiles):
            high, middle, low = thirds_of(jnp.concatenate(results, axis=0))
            one = jnp.concatenate([high, high, middle, high, low, middle], axis=0).astype(jnp.bfloat16)
            two = jnp.concatenate([high, middle, high, low, high, middle], axis=0).astype(jnp.bfloat16)
            update = lax.dot_general(one, two, (((0,), (0,)), ((), ())), preferred_element_type=jnp.float32)
            for t in range(end, len(tiles)):
                tiles[t] = tiles[t] - update[t * count : (t + 1) * count, :]
        first += width
    return out


def factor_kernel(cells, planes, kept, given, factor, message):
    mine, other = half_starts(kept.shape[0])
    message[pl.ds(mine, kept.shape[0]), :] = kept[...]
    message[pl.ds(other, kept.shape[0]), :] = given[...]
    row, col = halves(planes)
    eye = row == col
    diagonals = message[5 * planes // 2 : 5 * planes // 2 + 8, :]
    squares = jnp.broadcast_to(jnp.sum(diagonals, axis=1, keepdims=True), diagonals.shape)
    scales = 1.0 / (5.0 * cells * (squares / (planes * cells) + 1e-06))
    scaled = diagonals * scales
    scale = [scales[i : i + 1, :] for i in range(5)]

    def pair(packed, first):
        return jnp.where(row > col, packed * scale[first], packed * scale[first + 1])

    folded = unfold(message[2 * planes : 5 * planes // 2, :])
    triangles = jnp.where(eye, 0.0, pair(message[0:planes, :], 0) + pair(message[planes : 2 * planes, :], 2))
    triangles = triangles + folded * scale[4]
    cross = triangles + triangles.T + jnp.where(eye, jnp.sum(scaled[0:5], axis=0, keepdims=True), 0.0)
    narrow = planes // 64 * 2
    widths = [8] * narrow + [16] * (planes // 16 - narrow // 2)
    upper = factor_tiles([cross[t : t + 8, :] for t in range(0, planes, 8)], widths)
    factor[...] = jnp.concatenate(upper, axis=0).T


def cost(microseconds):
    return pl.CostEstimate(flops=0, bytes_accessed=int(microseconds * 3.69e6), transcendentals=0)


AXES = ("gy", "gz")


def exchange(values, even, odd):
    count_z = lax.axis_size("gz")
    count = lax.axis_size("gy") * count_z
    return lax.ppermute(values, AXES, [(i, i ^ (odd if i // count_z % 2 else even)) for i in range(count)])


def rounds():
    count_y, count_z = lax.axis_size("gy"), lax.axis_size("gz")
    assert count_y & (count_y - 1) == 0 and count_z & (count_z - 1) == 0
    bits = [count_z << i for i in range(1, count_y.bit_length() - 1)] + [1 << i for i in range(count_z.bit_length() - 1)]
    groups = [bits[i : i + 2] for i in range(0, len(bits), 2)]
    return [[group[0]] if len(group) == 1 else [group[0], group[1], group[0] ^ group[1]] for group in groups]


def add_terms(terms):
    while len(terms) > 1:
        terms = [terms[i] + terms[i + 1] for i in range(0, len(terms), 2)]
    return terms[0]


def f32(*shape):
    return jax.ShapeDtypeStruct(shape, jnp.float32)


def per_device(fields):
    planes = fields.shape[1] - 4
    rows, cols = fields.shape[2], fields.shape[3]
    count_y, count_z = lax.axis_size("gy"), lax.axis_size("gz")

    far = pl.pallas_call(
        functools.partial(far_kernel, rows, planes),
        out_shape=f32(6 * planes + 8, cols),
        in_specs=[pl.BlockSpec(memory_space=pl.ANY)],
        out_specs=VMEM,
        scratch_shapes=[pltpu.SemaphoreType.DMA((2, 3))],
        compiler_params=params(),
        cost_estimate=cost(1),
        name="far_face",
    )(pltpu.with_memory_space_constraint(fields, pltpu.HBM))
    fields, far = lax.optimization_barrier((fields, far))
    far = lax.ppermute(far, "gy", [(i, (i + 1 if i % 2 else i - 1) % count_y) for i in range(count_y)])
    turned, near, behind, ahead = pl.pallas_call(
        functools.partial(faces_kernel, rows, planes),
        out_shape=(
            pltpu.VMEM((3, rows, planes + 4, cols), jnp.float32),
            f32(2, 3, planes, cols),
            f32(planes, cols),
            f32(planes, cols),
        ),
        in_specs=[VMEM],
        out_specs=(VMEM,) * 4,
        scratch_shapes=[pltpu.VMEM((planes + 4, cols), jnp.float32)] * 2,
        compiler_params=params(),
        cost_estimate=cost(2.5),
        name="faces",
    )(pltpu.with_memory_space_constraint(fields, pltpu.VMEM))
    near = lax.ppermute(near, "gy", [(i, i ^ 1) for i in range(count_y)])
    left = lax.ppermute(ahead, "gz", [(i, (i + 1) % count_z) for i in range(count_z)])
    right = lax.ppermute(behind, "gz", [(i, (i - 1) % count_z) for i in range(count_z)])

    inner_rows = [pltpu.VMEM((rows - 4, planes, cols), jnp.float32)] * 4
    velocity, own_z, *planar = pl.pallas_call(
        functools.partial(inner_kernel, rows, planes),
        out_shape=(f32(3, planes, planes), pltpu.VMEM((3, rows, planes, cols), jnp.float32), *inner_rows),
        in_specs=[VMEM],
        out_specs=(VMEM,) * 6,
        scratch_shapes=[
            pltpu.VMEM((rows, planes, 3 * cols), jnp.bfloat16),
            pltpu.VMEM((3 * cols, cols), jnp.bfloat16),
        ],
        compiler_params=params(),
        cost_estimate=cost(3),
        name="inner",
    )(turned)
    pieces = pltpu.VMEM((2, 2, 2 * planes, 2 * cols), jnp.bfloat16)
    inner, part, to_last, to_first = pl.pallas_call(
        functools.partial(interior_kernel, rows, planes),
        out_shape=(
            f32(2, rows - 2, planes, cols),
            f32(2, 2 * planes, 2 * planes),
            f32(planes, cols),
            f32(planes, cols),
        ),
        in_specs=[VMEM] * 9,
        out_specs=(VMEM,) * 4,
        scratch_shapes=[pieces],
        compiler_params=params(),
        cost_estimate=cost(0),
        name="interior",
    )(turned, own_z, *planar, near, left, right)
    half = -(-(5 * planes // 2 + 8) // 16) * 8
    message = pltpu.VMEM((2 * half, planes), jnp.float32)
    border, keep, give = pl.pallas_call(
        functools.partial(border_kernel, rows, planes),
        out_shape=(f32(2, 2, planes, cols), f32(half, planes), f32(half, planes)),
        in_specs=[VMEM] * 7,
        out_specs=(VMEM, VMEM, VMEM),
        scratch_shapes=[message, pltpu.VMEM((2, 2 * planes, 2 * cols), jnp.bfloat16)],
        compiler_params=params(),
        cost_estimate=cost(0.7),
        name="border",
    )(turned, own_z, far, to_last, to_first, part, velocity)
    enstrophy, strain_rate = [
        pl.pallas_call(
            functools.partial(assemble_kernel, rows, planes, f),
            out_shape=f32(planes, rows, cols),
            in_specs=[VMEM] * 2,
            out_specs=VMEM,
            compiler_params=params(),
            cost_estimate=cost(1),
            name="assemble",
        )(inner, border)
        for f in range(2)
    ]
    core = count_z
    kept = keep + exchange(give, core, core)
    masks = rounds()
    outputs = [enstrophy, strain_rate]
    for i, (even, odd) in enumerate(zip(masks, masks[::-1])):
        kept = add_terms([kept] + [exchange(kept, *pair) for pair in zip(even, odd)])
        if i < len(outputs):
            kept, outputs[i] = lax.optimization_barrier((kept, outputs[i]))
    enstrophy, strain_rate = outputs
    given = exchange(kept, core, core)
    cells = rows * cols * count_y * count_z
    factor = pl.pallas_call(
        functools.partial(factor_kernel, float(cells), planes),
        out_shape=f32(planes, planes),
        in_specs=[VMEM] * 2,
        out_specs=VMEM,
        scratch_shapes=[message],
        compiler_params=params(),
        cost_estimate=cost(6),
        name="factor",
    )(kept, given)
    return (enstrophy, strain_rate, factor)


def solution(mesh):
    return jax.shard_map(
        per_device,
        mesh=mesh,
        in_specs=(P(None, None, "gy", "gz"),),
        out_specs=(P(None, "gy", "gz"), P(None, "gy", "gz"), P()),
        check_vma=False,
    )
```

```python
import functools

import jax
import jax.numpy as jnp
from jax import lax
from jax.experimental import pallas as pl
from jax.experimental.pallas import tpu as pltpu
from jax.sharding import PartitionSpec as P

TILE = 16
VMEM = pl.BlockSpec(memory_space=pltpu.VMEM)
DIMS_NT = (((1,), (1,)), ((), ()))


def params(mebibytes=20):
    return pltpu.CompilerParams(vmem_limit_bytes=mebibytes * 1024 * 1024)


def lanes(shape):
    return lax.broadcasted_iota(jnp.int32, shape, 1)


def split(values):
    high = values.astype(jnp.bfloat16)
    low = (values - high.astype(jnp.float32)).astype(jnp.bfloat16)
    return high, low


def gram_of(product):
    size = product.shape[0] // 2
    same = product[:size, :size] + product[size:, size:]
    return same + (product[:size, size:] + product[size:, :size])


def square(pieces):
    return lax.dot_general(pieces, pieces, DIMS_NT, preferred_element_type=jnp.float32)


def halves(size):
    row = lax.broadcasted_iota(jnp.int32, (size, size), 0)
    col = lax.broadcasted_iota(jnp.int32, (size, size), 1)
    return row, col


def pack_pair(first, second):
    row, col = halves(first.shape[0])
    return jnp.where(row >= col, first, second)


def fold(matrix):
    half = matrix.shape[0] // 2
    row = lax.broadcasted_iota(jnp.int32, (half, 2 * half), 0)
    col = lax.broadcasted_iota(jnp.int32, (half, 2 * half), 1)
    first = pltpu.roll(matrix[:half, :], half, 1)
    last = matrix[half:, :]
    return jnp.where((col >= half) & (row >= col - half), first, last)


def unfold(folded):
    half = folded.shape[0]
    row = lax.broadcasted_iota(jnp.int32, folded.shape, 0)
    col = lax.broadcasted_iota(jnp.int32, folded.shape, 1)
    first = jnp.where(row > col, pltpu.roll(folded, half, 1), 0.0)
    last = jnp.where((col < half) | (col - half > row), folded, 0.0)
    return jnp.concatenate([first, last], axis=0)


def half_starts(length):
    core = lax.axis_index("gy") % 2
    return pl.multiple_of(core * length, 8), pl.multiple_of((1 - core) * length, 8)


def diagonal(matrix):
    row, col = halves(matrix.shape[0])
    return jnp.sum(jnp.where(row == col, matrix, 0.0), axis=0, keepdims=True)


def far_kernel(rows, planes, fields, far, arrived):
    first = lax.axis_index("gy") % 2 * (rows - 2)
    copies = []
    for layer in range(2):
        for c in range(3):
            source = fields.at[c, pl.ds(2, planes), first + layer, :]
            copies.append(pltpu.make_async_copy(source, far.at[pl.ds((3 * layer + c) * planes, planes)], arrived.at[layer, c]))
            copies[-1].start()
    far[6 * planes :, :] = jnp.zeros((far.shape[0] - 6 * planes, far.shape[1]), jnp.float32)
    for copy in copies:
        copy.wait()


def faces_kernel(rows, planes, fields, turned_fields, near, behind, ahead, tails, heads):
    odd = lax.axis_index("gy") % 2
    size = fields.shape[3]
    depth = planes + 4
    lane = lanes((8, size))
    near_row = (1 - odd) * (rows - 2)

    def turn(c, first):
        at = pl.ds(first, 8)
        tail = tails[at, :]
        head = heads[at, :]
        for base in range(0, rows, 8):
            block = jnp.swapaxes(fields[c, at, base : base + 8, :], 0, 1)
            for j in range(8):
                y = base + j
                k = c * rows + y
                turned_fields[c, y, at, :] = block[j]
                moved = pltpu.roll(block[j], (2 * k + 2) % size, 1)
                tail = jnp.where(lane >= 2 * k, moved, tail)
                head = jnp.where(lane >= 2 * k + 2, moved, head)
        tails[at, :] = tail
        heads[at, :] = head

    for c in range(3):

        @pl.loop(0, depth // 8, unroll=16)
        def _(t):
            turn(c, pl.multiple_of(t * 8, 8))

        if depth % 8:
            turn(c, depth - 8)
        for layer in range(2):
            near[layer, c] = turned_fields[c, near_row + layer, 2 : planes + 2, :]
    ahead[...] = tails[2 : planes + 2, :]
    behind[...] = heads[2 : planes + 2, :]


def derivative(minus_two, minus_one, plus_one, plus_two):
    return 8.0 * (plus_one - minus_one) - (plus_two - minus_two)


def inner_kernel(rows, planes, fields, grams, along_z, spin, stretch, bend_x, bend_y, thirds, band):
    size = fields.shape[3]
    row = lax.broadcasted_iota(jnp.int32, (3 * size, size), 0) % size
    col = lax.broadcasted_iota(jnp.int32, (3 * size, size), 1)
    far_side = jnp.where(row == col - 2, 1.0, jnp.where(row == col + 2, -1.0, 0.0))
    near_side = jnp.where(row == col - 1, -8.0, jnp.where(row == col + 1, 8.0, 0.0))
    band[...] = (far_side + near_side).astype(jnp.bfloat16)

    def planar(index, t):
        y = index + 2
        at = pl.ds(t * TILE, TILE)
        x, y = [
            [
                derivative(*[fields[c, y + k * step, pl.ds(2 + t * TILE + k * (1 - step), TILE), :] for k in (-2, -1, 1, 2)])
                for c in range(3)
            ]
            for step in (0, 1)
        ]
        turn = x[1] - y[0]
        shear = x[1] + y[0]
        spin[index, at, :] = turn * turn
        stretch[index, at, :] = 2.0 * (x[0] * x[0] + y[1] * y[1]) + shear * shear
        bend_x[index, at, :] = x[2]
        bend_y[index, at, :] = y[2]

    tiles = [(index, t) for index in range(rows - 4) for t in range(planes // TILE)]
    done = 0
    for c in range(3):
        total = None
        for y in range(rows):
            for t in range(planes // TILE):
                cells = fields[c, y, 2 + t * TILE : 2 + (t + 1) * TILE, :]
                high = cells.astype(jnp.bfloat16)
                rest = cells - high.astype(jnp.float32)
                middle = rest.astype(jnp.bfloat16)
                low = (rest - middle.astype(jnp.float32)).astype(jnp.bfloat16)
                for part, piece in enumerate((high, middle, low)):
                    thirds[y, t * TILE : (t + 1) * TILE, part * size : (part + 1) * size] = piece
            if y % 2 == 1:
                parts = [
                    jnp.concatenate([thirds[y - 1, :, at : at + size], thirds[y, :, at : at + size]], axis=1)
                    for at in (0, size)
                ]
                product = square(jnp.concatenate(parts, axis=0))
                total = product if y == 1 else total + product
            upto = len(tiles) * (c * rows + y + 1) // (3 * rows)
            for tile in tiles[done:upto]:
                planar(*tile)
            done = upto
        grams[c] = gram_of(total)
        derivatives = jnp.dot(
            thirds[...].reshape(rows * planes, 3 * size), band[...], preferred_element_type=jnp.float32
        )
        along_z[c] = derivatives.reshape(rows, planes, size)


def edge_terms(left, right):
    size = left.shape[1]
    even = lanes(left.shape) % 2 == 0
    left = pltpu.roll(left, 2, 1)
    right = pltpu.roll(right, size - 2, 1)
    to_last = jnp.where(even, -right, 8.0 * pltpu.roll(right, 1, 1) - right)
    to_first = jnp.where(even, left - 8.0 * pltpu.roll(left, size - 1, 1), left)
    return to_last, to_first


def z_derivatives(own_z, to_last, to_first, t, y, rows):
    size = own_z.shape[3]
    lane = lanes((TILE, size))
    edge = (lane < 2) | (lane >= size - 2)
    at = pl.ds(t * TILE, TILE)
    along_z = []
    for c in range(3):
        k = c * rows + y
        terms = jnp.where(lane < 2 * k + 2, to_last[at, :], to_first[at, :])
        terms = pltpu.roll(terms, (2 * size - 2 - 2 * k) % size, 1)
        along_z.append(own_z[c, y, at, :] + jnp.where(edge, terms, 0.0))
    return along_z


def finish(spin, stretch, bend_x, bend_y, z):
    turn_x, turn_y = bend_x - z[0], bend_y - z[1]
    shear_x, shear_y = bend_x + z[0], bend_y + z[1]
    enstrophy = spin + turn_x * turn_x + turn_y * turn_y
    strain = stretch + 2.0 * (z[2] * z[2]) + (shear_x * shear_x + shear_y * shear_y)
    return enstrophy * (1.0 / 288.0), strain * (1.0 / 288.0)


def store_results(results, out, index, pieces, half, t, planes, size):
    tile = slice(t * TILE, (t + 1) * TILE)
    lower = slice(planes + t * TILE, planes + (t + 1) * TILE)
    for f in range(2):
        out[f, index, tile, :] = results[f]
        high, low = split(results[f])
        pieces[f, tile, half * size : (half + 1) * size] = high
        pieces[f, lower, half * size : (half + 1) * size] = low


def x_derivatives(fields, t, y):
    return [derivative(*[fields[c, y, pl.ds(2 + t * TILE + k, TILE), :] for k in (-2, -1, 1, 2)]) for c in range(3)]


def beside_face(rows, fields, halo, lower, t, x_and_z):
    at = pl.ds(t * TILE, TILE)
    within = pl.ds(2 + t * TILE, TILE)
    first = jnp.where(lower, 0, rows - 2)

    def window(c):
        own = [fields[c, jnp.where(lower, 0, rows - 4) + i, within, :] for i in range(4)]
        ends = [halo[i][c][at, :] for i in range(2)]
        before = [jnp.where(lower, ends[i], own[i]) for i in range(2)]
        centre = [jnp.where(lower, own[i], own[i + 2]) for i in range(2)]
        after = [jnp.where(lower, own[i + 2], ends[i]) for i in range(2)]
        return before + centre + after

    windows = [window(c) for c in range(3)]
    for i in range(2):
        along_x, z = x_and_z(i, first + i)
        along_y = [derivative(*[windows[c][2 + i + k] for k in (-2, -1, 1, 2)]) for c in range(3)]
        turn = along_x[1] - along_y[0]
        shear = along_x[1] + along_y[0]
        stretch = 2.0 * (along_x[0] * along_x[0] + along_y[1] * along_y[1]) + shear * shear
        yield i, finish(turn * turn, stretch, along_x[2], along_y[2], z)


def interior_kernel(
    rows, planes, fields, own_z, spin, stretch, bend_x, bend_y, near, left, right, velocity,
    out, total, beside, packed, pieces, to_last, to_first
):
    size = own_z.shape[3]
    odd = lax.axis_index("gy") % 2 == 1
    to_last[...], to_first[...] = edge_terms(left[...], right[...])
    for pair in range(rows // 2 - 1):
        buffer = pieces.at[pair % 2]
        for t in range(planes // TILE):
            if pair < rows // 2 - 2:
                for half in range(2):
                    index = 2 * pair + half
                    z = z_derivatives(own_z, to_last, to_first, t, index + 2, rows)
                    planar = [ref[index, t * TILE : (t + 1) * TILE, :] for ref in (spin, stretch, bend_x, bend_y)]
                    store_results(finish(*planar, z), out, index, buffer, half, t, planes, size)
            else:
                halo = [[near.at[i, c] for c in range(3)] for i in range(2)]

                def x_and_z(i, y):
                    return x_derivatives(fields, t, y), z_derivatives(own_z, to_last, to_first, t, y, rows)

                for half, results in beside_face(rows, fields, halo, odd, t, x_and_z):
                    store_results(results, out, 2 * pair + half, buffer, half, t, planes, size)
                for i in range(2):
                    ready = x_and_z(i, jnp.where(odd, rows - 2, 0) + i)
                    for c in range(3):
                        beside[i, 0, c, t * TILE : (t + 1) * TILE, :] = ready[0][c]
                        beside[i, 1, c, t * TILE : (t + 1) * TILE, :] = ready[1][c]
        for f in range(2):
            product = square(buffer[f])
            total[f] = product if pair == 0 else total[f] + product
    packed[0:planes, :] = pack_pair(velocity[0], velocity[1])
    packed[planes : 3 * planes // 2, :] = fold(velocity[2])
    diagonals = [diagonal(velocity[c]) for c in range(3)]
    packed[3 * planes // 2 :, :] = jnp.concatenate(diagonals + [jnp.zeros((5, planes), jnp.float32)], axis=0)


def border_kernel(rows, planes, fields, far, beside, part, packed, out, keep, give, message, pieces):
    size = fields.shape[3]
    odd = lax.axis_index("gy") % 2 == 1
    halo = [[far.at[pl.ds((3 * i + c) * planes, planes)] for c in range(3)] for i in range(2)]
    for t in range(planes // TILE):

        def x_and_z(i, y):
            return [[beside[i, way, c, t * TILE : (t + 1) * TILE, :] for c in range(3)] for way in range(2)]

        for half, results in beside_face(rows, fields, halo, ~odd, t, x_and_z):
            store_results(results, out, half, pieces, half, t, planes, size)
    grams = [gram_of(part[f] + square(pieces[f])) for f in range(2)]
    message[0:planes, :] = pack_pair(grams[0], grams[1])
    message[planes : 5 * planes // 2, :] = packed[0 : 3 * planes // 2, :]
    used = 5 * planes // 2
    message[used : used + 2, :] = jnp.concatenate([diagonal(grams[0]), diagonal(grams[1])], axis=0)
    message[used + 2 : used + 8, :] = packed[3 * planes // 2 : 3 * planes // 2 + 6, :]
    if message.shape[0] > used + 8:
        message[used + 8 :, :] = jnp.zeros((message.shape[0] - used - 8, planes), jnp.float32)
    mine, other = half_starts(keep.shape[0])
    keep[...] = message[pl.ds(mine, keep.shape[0]), :]
    give[...] = message[pl.ds(other, keep.shape[0]), :]


def assemble_kernel(rows, planes, f, inner, border, out):
    odd = lax.axis_index("gy") % 2 == 1

    def plane_of(y, at):
        if 2 <= y < rows - 2:
            return inner[f, y - 2, at, :]
        layer = y % (rows - 2)
        beside_near = odd if y < 2 else ~odd
        return jnp.where(beside_near, inner[f, rows - 4 + layer, at, :], border[f, layer, at, :])

    @pl.loop(0, planes // 8)
    def _(t):
        at = pl.ds(pl.multiple_of(t * 8, 8), 8)
        for base in range(0, rows, 8):
            block = jnp.stack([plane_of(y, at) for y in range(base, base + 8)], axis=0)
            out[at, base : base + 8, :] = jnp.swapaxes(block, 0, 1)


def splat(tile, j):
    return jnp.broadcast_to(tile[j : j + 1, :], tile.shape)

def spread_column(tile, at):
    return jnp.broadcast_to(tile[:, at : at + 1], tile.shape)


def thirds_of(values):
    high = values.astype(jnp.bfloat16).astype(jnp.float32)
    rest = values - high
    middle = rest.astype(jnp.bfloat16).astype(jnp.float32)
    return high, middle, rest - middle


def eliminate(rows, first, width):
    count, size = rows[0].shape
    sub = lax.broadcasted_iota(jnp.int32, (count, size), 0)
    lane = lax.broadcasted_iota(jnp.int32, (count, size), 1)
    head = width // count
    tall = len(rows)
    made = [[spread_column(rows[t], first + j) for j in range(width)] for t in range(tall)]
    spread = [[made[t][j] for t in range(tall)] for j in range(width)]
    rows = list(rows)
    results = [jnp.zeros((count, size), jnp.float32)] * head
    entries = {}
    pivot = splat(spread[0][0], 0)
    for j in range(width):
        t0, s0 = divmod(j, count)
        inverse = 1.0 / pivot
        for m in range(j + 1, width):
            entries[j, m] = splat(spread[j][m // count], m % count)
        if j + 1 < width:
            t1, s1 = divmod(j + 1, count)
            following = splat(spread[j + 1][t1], s1) - (entries[j, j + 1] * entries[j, j + 1]) * inverse
        row = splat(rows[t0], s0)
        results[t0] = jnp.where(sub == s0, row * lax.rsqrt(pivot), results[t0])
        for t in range(t0, tall):
            scaled = spread[j][t] * inverse
            for m in range(j + 1, width):
                spread[m][t] = spread[m][t] - scaled * entries[j, m]
            rows[t] = rows[t] - scaled * row
        if j + 1 < width:
            pivot = following
    results = [jnp.where(lane >= first + t * count + sub, results[t], 0.0) for t in range(head)]
    return results, rows[head:]


def factor_tiles(tiles, widths):
    count = tiles[0].shape[0]
    tiles = list(tiles)
    out = []
    first = 0
    for i, width in enumerate(widths):
        top, after = first // count, (first + width) // count
        end = after + sum(widths[i + 1 : i + 3]) // count
        results, tiles[after:end] = eliminate(tiles[top:end], first, width)
        out += results
        if end < len(tiles):
            high, middle, low = thirds_of(jnp.concatenate(results, axis=0))
            one = jnp.concatenate([high, high, middle, high, low, middle], axis=0).astype(jnp.bfloat16)
            two = jnp.concatenate([high, middle, high, low, high, middle], axis=0).astype(jnp.bfloat16)
            update = lax.dot_general(one, two, (((0,), (0,)), ((), ())), preferred_element_type=jnp.float32)
            for t in range(end, len(tiles)):
                tiles[t] = tiles[t] - update[t * count : (t + 1) * count, :]
        first += width
    return out


def factor_kernel(cells, planes, kept, given, factor, message):
    mine, other = half_starts(kept.shape[0])
    message[pl.ds(mine, kept.shape[0]), :] = kept[...]
    message[pl.ds(other, kept.shape[0]), :] = given[...]
    row, col = halves(planes)
    eye = row == col
    diagonals = message[5 * planes // 2 : 5 * planes // 2 + 8, :]
    squares = jnp.broadcast_to(jnp.sum(diagonals, axis=1, keepdims=True), diagonals.shape)
    scales = 1.0 / (5.0 * cells * (squares / (planes * cells) + 1e-06))
    scaled = diagonals * scales
    scale = [scales[i : i + 1, :] for i in range(5)]

    def pair(packed, first):
        return jnp.where(row > col, packed * scale[first], packed * scale[first + 1])

    folded = unfold(message[2 * planes : 5 * planes // 2, :])
    triangles = jnp.where(eye, 0.0, pair(message[0:planes, :], 0) + pair(message[planes : 2 * planes, :], 2))
    triangles = triangles + folded * scale[4]
    cross = triangles + triangles.T + jnp.where(eye, jnp.sum(scaled[0:5], axis=0, keepdims=True), 0.0)
    narrow = planes // 64 * 2
    widths = [8] * narrow + [16] * (planes // 16 - narrow // 2)
    upper = factor_tiles([cross[t : t + 8, :] for t in range(0, planes, 8)], widths)
    factor[...] = jnp.concatenate(upper, axis=0).T


def cost(microseconds):
    return pl.CostEstimate(flops=0, bytes_accessed=int(microseconds * 3.69e6), transcendentals=0)


AXES = ("gy", "gz")


def exchange(values, even, odd):
    count_z = lax.axis_size("gz")
    count = lax.axis_size("gy") * count_z
    return lax.ppermute(values, AXES, [(i, i ^ (odd if i // count_z % 2 else even)) for i in range(count)])


def rounds():
    count_y, count_z = lax.axis_size("gy"), lax.axis_size("gz")
    assert count_y & (count_y - 1) == 0 and count_z & (count_z - 1) == 0
    bits = [count_z << i for i in range(1, count_y.bit_length() - 1)] + [1 << i for i in range(count_z.bit_length() - 1)]
    groups = [bits[i : i + 2] for i in range(0, len(bits), 2)]
    return [[group[0]] if len(group) == 1 else [group[0], group[1], group[0] ^ group[1]] for group in groups]


def add_terms(terms):
    while len(terms) > 1:
        terms = [terms[i] + terms[i + 1] for i in range(0, len(terms), 2)]
    return terms[0]


def f32(*shape):
    return jax.ShapeDtypeStruct(shape, jnp.float32)


def per_device(fields):
    planes = fields.shape[1] - 4
    rows, cols = fields.shape[2], fields.shape[3]
    count_y, count_z = lax.axis_size("gy"), lax.axis_size("gz")

    far = pl.pallas_call(
        functools.partial(far_kernel, rows, planes),
        out_shape=f32(6 * planes + 8, cols),
        in_specs=[pl.BlockSpec(memory_space=pl.ANY)],
        out_specs=VMEM,
        scratch_shapes=[pltpu.SemaphoreType.DMA((2, 3))],
        compiler_params=params(),
        cost_estimate=cost(1),
        name="far_face",
    )(pltpu.with_memory_space_constraint(fields, pltpu.HBM))
    fields, far = lax.optimization_barrier((fields, far))
    far = lax.ppermute(far, "gy", [(i, (i + 1 if i % 2 else i - 1) % count_y) for i in range(count_y)])
    turned, near, behind, ahead = pl.pallas_call(
        functools.partial(faces_kernel, rows, planes),
        out_shape=(
            pltpu.VMEM((3, rows, planes + 4, cols), jnp.float32),
            f32(2, 3, planes, cols),
            f32(planes, cols),
            f32(planes, cols),
        ),
        in_specs=[VMEM],
        out_specs=(VMEM,) * 4,
        scratch_shapes=[pltpu.VMEM((planes + 4, cols), jnp.float32)] * 2,
        compiler_params=params(),
        cost_estimate=cost(2.5),
        name="faces",
    )(pltpu.with_memory_space_constraint(fields, pltpu.VMEM))
    near = lax.ppermute(near, "gy", [(i, i ^ 1) for i in range(count_y)])
    left = lax.ppermute(ahead, "gz", [(i, (i + 1) % count_z) for i in range(count_z)])
    right = lax.ppermute(behind, "gz", [(i, (i - 1) % count_z) for i in range(count_z)])

    inner_rows = [pltpu.VMEM((rows - 4, planes, cols), jnp.float32)] * 4
    velocity, own_z, *planar = pl.pallas_call(
        functools.partial(inner_kernel, rows, planes),
        out_shape=(f32(3, planes, planes), pltpu.VMEM((3, rows, planes, cols), jnp.float32), *inner_rows),
        in_specs=[VMEM],
        out_specs=(VMEM,) * 6,
        scratch_shapes=[
            pltpu.VMEM((rows, planes, 3 * cols), jnp.bfloat16),
            pltpu.VMEM((3 * cols, cols), jnp.bfloat16),
        ],
        compiler_params=params(),
        cost_estimate=cost(3),
        name="inner",
    )(turned)
    pieces = pltpu.VMEM((2, 2, 2 * planes, 2 * cols), jnp.bfloat16)
    inner, part, beside, packed = pl.pallas_call(
        functools.partial(interior_kernel, rows, planes),
        out_shape=(
            f32(2, rows - 2, planes, cols),
            f32(2, 2 * planes, 2 * planes),
            pltpu.VMEM((2, 2, 3, planes, cols), jnp.float32),
            f32(3 * planes // 2 + 8, planes),
        ),
        in_specs=[VMEM] * 10,
        out_specs=(VMEM,) * 4,
        scratch_shapes=[pieces, pltpu.VMEM((planes, cols), jnp.float32), pltpu.VMEM((planes, cols), jnp.float32)],
        compiler_params=params(),
        cost_estimate=cost(0),
        name="interior",
    )(turned, own_z, *planar, near, left, right, velocity)
    half = -(-(5 * planes // 2 + 8) // 16) * 8
    message = pltpu.VMEM((2 * half, planes), jnp.float32)
    border, keep, give = pl.pallas_call(
        functools.partial(border_kernel, rows, planes),
        out_shape=(f32(2, 2, planes, cols), f32(half, planes), f32(half, planes)),
        in_specs=[VMEM] * 5,
        out_specs=(VMEM, VMEM, VMEM),
        scratch_shapes=[message, pltpu.VMEM((2, 2 * planes, 2 * cols), jnp.bfloat16)],
        compiler_params=params(),
        cost_estimate=cost(0.7),
        name="border",
    )(turned, far, beside, part, packed)
    enstrophy, strain_rate = [
        pl.pallas_call(
            functools.partial(assemble_kernel, rows, planes, f),
            out_shape=f32(planes, rows, cols),
            in_specs=[VMEM] * 2,
            out_specs=VMEM,
            compiler_params=params(),
            cost_estimate=cost(1),
            name="assemble",
        )(inner, border)
        for f in range(2)
    ]
    core = count_z
    kept = keep + exchange(give, core, core)
    masks = rounds()
    outputs = [enstrophy, strain_rate]
    for i, (even, odd) in enumerate(zip(masks, masks[::-1])):
        kept = add_terms([kept] + [exchange(kept, *pair) for pair in zip(even, odd)])
        if i < len(outputs):
            kept, outputs[i] = lax.optimization_barrier((kept, outputs[i]))
    enstrophy, strain_rate = outputs
    given = exchange(kept, core, core)
    cells = rows * cols * count_y * count_z
    factor = pl.pallas_call(
        functools.partial(factor_kernel, float(cells), planes),
        out_shape=f32(planes, planes),
        in_specs=[VMEM] * 2,
        out_specs=VMEM,
        scratch_shapes=[message],
        compiler_params=params(),
        cost_estimate=cost(6),
        name="factor",
    )(kept, given)
    return (enstrophy, strain_rate, factor)


def solution(mesh):
    return jax.shard_map(
        per_device,
        mesh=mesh,
        in_specs=(P(None, None, "gy", "gz"),),
        out_specs=(P(None, "gy", "gz"), P(None, "gy", "gz"), P()),
        check_vma=False,
    )
```

```python
import functools

import jax
import jax.numpy as jnp
from jax import lax
from jax.experimental import pallas as pl
from jax.experimental.pallas import tpu as pltpu
from jax.sharding import PartitionSpec as P

TILE = 16
VMEM = pl.BlockSpec(memory_space=pltpu.VMEM)
DIMS_NT = (((1,), (1,)), ((), ()))


def params(mebibytes=20):
    return pltpu.CompilerParams(vmem_limit_bytes=mebibytes * 1024 * 1024)


def lanes(shape):
    return lax.broadcasted_iota(jnp.int32, shape, 1)


def split(values):
    high = values.astype(jnp.bfloat16)
    low = (values - high.astype(jnp.float32)).astype(jnp.bfloat16)
    return high, low


def gram_of(product):
    size = product.shape[0] // 2
    same = product[:size, :size] + product[size:, size:]
    return same + (product[:size, size:] + product[size:, :size])


def square(pieces):
    return lax.dot_general(pieces, pieces, DIMS_NT, preferred_element_type=jnp.float32)


def halves(size):
    row = lax.broadcasted_iota(jnp.int32, (size, size), 0)
    col = lax.broadcasted_iota(jnp.int32, (size, size), 1)
    return row, col


def pack_pair(first, second):
    row, col = halves(first.shape[0])
    return jnp.where(row >= col, first, second)


def fold(matrix):
    half = matrix.shape[0] // 2
    row = lax.broadcasted_iota(jnp.int32, (half, 2 * half), 0)
    col = lax.broadcasted_iota(jnp.int32, (half, 2 * half), 1)
    first = pltpu.roll(matrix[:half, :], half, 1)
    last = matrix[half:, :]
    return jnp.where((col >= half) & (row >= col - half), first, last)


def unfold(folded):
    half = folded.shape[0]
    row = lax.broadcasted_iota(jnp.int32, folded.shape, 0)
    col = lax.broadcasted_iota(jnp.int32, folded.shape, 1)
    first = jnp.where(row > col, pltpu.roll(folded, half, 1), 0.0)
    last = jnp.where((col < half) | (col - half > row), folded, 0.0)
    return jnp.concatenate([first, last], axis=0)


def half_starts(length):
    core = lax.axis_index("gy") % 2
    return pl.multiple_of(core * length, 8), pl.multiple_of((1 - core) * length, 8)


def diagonal(matrix):
    row, col = halves(matrix.shape[0])
    return jnp.sum(jnp.where(row == col, matrix, 0.0), axis=0, keepdims=True)


def far_kernel(rows, planes, fields, far, arrived):
    first = lax.axis_index("gy") % 2 * (rows - 2)
    copies = []
    for layer in range(2):
        for c in range(3):
            source = fields.at[c, pl.ds(2, planes), first + layer, :]
            copies.append(pltpu.make_async_copy(source, far.at[pl.ds((3 * layer + c) * planes, planes)], arrived.at[layer, c]))
            copies[-1].start()
    far[6 * planes :, :] = jnp.zeros((far.shape[0] - 6 * planes, far.shape[1]), jnp.float32)
    for copy in copies:
        copy.wait()


def faces_kernel(rows, planes, fields, turned_fields, near, behind, ahead, tails, heads):
    odd = lax.axis_index("gy") % 2
    size = fields.shape[3]
    depth = planes + 4
    lane = lanes((8, size))
    near_row = (1 - odd) * (rows - 2)

    def turn(c, first):
        at = pl.ds(first, 8)
        tail = tails[at, :]
        head = heads[at, :]
        for base in range(0, rows, 8):
            block = jnp.swapaxes(fields[c, at, base : base + 8, :], 0, 1)
            for j in range(8):
                y = base + j
                k = c * rows + y
                turned_fields[c, y, at, :] = block[j]
                moved = pltpu.roll(block[j], (2 * k + 2) % size, 1)
                tail = jnp.where(lane >= 2 * k, moved, tail)
                head = jnp.where(lane >= 2 * k + 2, moved, head)
        tails[at, :] = tail
        heads[at, :] = head

    for c in range(3):

        @pl.loop(0, depth // 8, unroll=16)
        def _(t):
            turn(c, pl.multiple_of(t * 8, 8))

        if depth % 8:
            turn(c, depth - 8)
        for layer in range(2):
            near[layer, c] = turned_fields[c, near_row + layer, 2 : planes + 2, :]
    ahead[...] = tails[2 : planes + 2, :]
    behind[...] = heads[2 : planes + 2, :]


def derivative(minus_two, minus_one, plus_one, plus_two):
    return 8.0 * (plus_one - minus_one) - (plus_two - minus_two)


def inner_kernel(rows, planes, fields, grams, along_z, spin, stretch, bend_x, bend_y, thirds, band):
    size = fields.shape[3]
    row = lax.broadcasted_iota(jnp.int32, (3 * size, size), 0) % size
    col = lax.broadcasted_iota(jnp.int32, (3 * size, size), 1)
    far_side = jnp.where(row == col - 2, 1.0, jnp.where(row == col + 2, -1.0, 0.0))
    near_side = jnp.where(row == col - 1, -8.0, jnp.where(row == col + 1, 8.0, 0.0))
    band[...] = (far_side + near_side).astype(jnp.bfloat16)

    def planar(index, t):
        y = index + 2
        at = pl.ds(t * TILE, TILE)
        x, y = [
            [
                derivative(*[fields[c, y + k * step, pl.ds(2 + t * TILE + k * (1 - step), TILE), :] for k in (-2, -1, 1, 2)])
                for c in range(3)
            ]
            for step in (0, 1)
        ]
        turn = x[1] - y[0]
        shear = x[1] + y[0]
        spin[index, at, :] = turn * turn
        stretch[index, at, :] = 2.0 * (x[0] * x[0] + y[1] * y[1]) + shear * shear
        bend_x[index, at, :] = x[2]
        bend_y[index, at, :] = y[2]

    tiles = [(index, t) for index in range(rows - 4) for t in range(planes // TILE)]
    done = 0
    for c in range(3):
        total = None
        for y in range(rows):
            for t in range(planes // TILE):
                cells = fields[c, y, 2 + t * TILE : 2 + (t + 1) * TILE, :]
                high = cells.astype(jnp.bfloat16)
                rest = cells - high.astype(jnp.float32)
                middle = rest.astype(jnp.bfloat16)
                low = (rest - middle.astype(jnp.float32)).astype(jnp.bfloat16)
                for part, piece in enumerate((high, middle, low)):
                    thirds[y, t * TILE : (t + 1) * TILE, part * size : (part + 1) * size] = piece
            if y % 2 == 1:
                parts = [
                    jnp.concatenate([thirds[y - 1, :, at : at + size], thirds[y, :, at : at + size]], axis=1)
                    for at in (0, size)
                ]
                product = square(jnp.concatenate(parts, axis=0))
                total = product if y == 1 else total + product
            upto = len(tiles) * (c * rows + y + 1) // (3 * rows)
            for tile in tiles[done:upto]:
                planar(*tile)
            done = upto
        grams[c] = gram_of(total)
        derivatives = jnp.dot(
            thirds[...].reshape(rows * planes, 3 * size), band[...], preferred_element_type=jnp.float32
        )
        along_z[c] = derivatives.reshape(rows, planes, size)


def edge_terms(left, right):
    size = left.shape[1]
    even = lanes(left.shape) % 2 == 0
    left = pltpu.roll(left, 2, 1)
    right = pltpu.roll(right, size - 2, 1)
    to_last = jnp.where(even, -right, 8.0 * pltpu.roll(right, 1, 1) - right)
    to_first = jnp.where(even, left - 8.0 * pltpu.roll(left, size - 1, 1), left)
    return to_last, to_first


def z_derivatives(own_z, to_last, to_first, t, y, rows):
    size = own_z.shape[3]
    lane = lanes((TILE, size))
    edge = (lane < 2) | (lane >= size - 2)
    at = pl.ds(t * TILE, TILE)
    along_z = []
    for c in range(3):
        k = c * rows + y
        terms = jnp.where(lane < 2 * k + 2, to_last[at, :], to_first[at, :])
        terms = pltpu.roll(terms, (2 * size - 2 - 2 * k) % size, 1)
        along_z.append(own_z[c, y, at, :] + jnp.where(edge, terms, 0.0))
    return along_z


def finish(spin, stretch, bend_x, bend_y, z):
    turn_x, turn_y = bend_x - z[0], bend_y - z[1]
    shear_x, shear_y = bend_x + z[0], bend_y + z[1]
    enstrophy = spin + turn_x * turn_x + turn_y * turn_y
    strain = stretch + 2.0 * (z[2] * z[2]) + (shear_x * shear_x + shear_y * shear_y)
    return enstrophy * (1.0 / 288.0), strain * (1.0 / 288.0)


def store_results(results, out, index, pieces, half, t, planes, size):
    tile = slice(t * TILE, (t + 1) * TILE)
    lower = slice(planes + t * TILE, planes + (t + 1) * TILE)
    for f in range(2):
        out[f, index, tile, :] = results[f]
        high, low = split(results[f])
        pieces[f, tile, half * size : (half + 1) * size] = high
        pieces[f, lower, half * size : (half + 1) * size] = low


def x_derivatives(fields, t, y):
    return [derivative(*[fields[c, y, pl.ds(2 + t * TILE + k, TILE), :] for k in (-2, -1, 1, 2)]) for c in range(3)]


def beside_face(rows, fields, halo, lower, t, x_and_z):
    at = pl.ds(t * TILE, TILE)
    within = pl.ds(2 + t * TILE, TILE)
    first = jnp.where(lower, 0, rows - 2)

    def window(c):
        own = [fields[c, jnp.where(lower, 0, rows - 4) + i, within, :] for i in range(4)]
        ends = [halo[i][c][at, :] for i in range(2)]
        before = [jnp.where(lower, ends[i], own[i]) for i in range(2)]
        centre = [jnp.where(lower, own[i], own[i + 2]) for i in range(2)]
        after = [jnp.where(lower, own[i + 2], ends[i]) for i in range(2)]
        return before + centre + after

    windows = [window(c) for c in range(3)]
    for i in range(2):
        along_x, z = x_and_z(i, first + i)
        along_y = [derivative(*[windows[c][2 + i + k] for k in (-2, -1, 1, 2)]) for c in range(3)]
        turn = along_x[1] - along_y[0]
        shear = along_x[1] + along_y[0]
        stretch = 2.0 * (along_x[0] * along_x[0] + along_y[1] * along_y[1]) + shear * shear
        yield i, finish(turn * turn, stretch, along_x[2], along_y[2], z)


def interior_kernel(
    rows, planes, fields, own_z, spin, stretch, bend_x, bend_y, near, left, right, velocity,
    out, total, beside, packed, pieces, to_last, to_first
):
    size = own_z.shape[3]
    odd = lax.axis_index("gy") % 2 == 1
    to_last[...], to_first[...] = edge_terms(left[...], right[...])
    for pair in range(rows // 2 - 1):
        buffer = pieces.at[pair % 2]
        for t in range(planes // TILE):
            if pair < rows // 2 - 2:
                for half in range(2):
                    index = 2 * pair + half
                    z = z_derivatives(own_z, to_last, to_first, t, index + 2, rows)
                    planar = [ref[index, t * TILE : (t + 1) * TILE, :] for ref in (spin, stretch, bend_x, bend_y)]
                    store_results(finish(*planar, z), out, index, buffer, half, t, planes, size)
            else:
                halo = [[near.at[i, c] for c in range(3)] for i in range(2)]

                def x_and_z(i, y):
                    return x_derivatives(fields, t, y), z_derivatives(own_z, to_last, to_first, t, y, rows)

                for half, results in beside_face(rows, fields, halo, odd, t, x_and_z):
                    store_results(results, out, 2 * pair + half, buffer, half, t, planes, size)
                for i in range(2):
                    ready = x_and_z(i, jnp.where(odd, rows - 2, 0) + i)
                    for c in range(3):
                        beside[i, 0, c, t * TILE : (t + 1) * TILE, :] = ready[0][c]
                        beside[i, 1, c, t * TILE : (t + 1) * TILE, :] = ready[1][c]
        for f in range(2):
            product = square(buffer[f])
            total[f] = product if pair == 0 else total[f] + product
    packed[0:planes, :] = pack_pair(velocity[0], velocity[1])
    packed[planes : 3 * planes // 2, :] = fold(velocity[2])
    diagonals = [diagonal(velocity[c]) for c in range(3)]
    packed[3 * planes // 2 :, :] = jnp.concatenate(diagonals + [jnp.zeros((5, planes), jnp.float32)], axis=0)


def border_kernel(rows, planes, fields, far, beside, part, packed, out, keep, give, message, pieces):
    size = fields.shape[3]
    odd = lax.axis_index("gy") % 2 == 1
    halo = [[far.at[pl.ds((3 * i + c) * planes, planes)] for c in range(3)] for i in range(2)]
    for t in range(planes // TILE):

        def x_and_z(i, y):
            return [[beside[i, way, c, t * TILE : (t + 1) * TILE, :] for c in range(3)] for way in range(2)]

        for half, results in beside_face(rows, fields, halo, ~odd, t, x_and_z):
            store_results(results, out, half, pieces, half, t, planes, size)
    grams = [gram_of(part[f] + square(pieces[f])) for f in range(2)]
    message[0:planes, :] = pack_pair(grams[0], grams[1])
    message[planes : 5 * planes // 2, :] = packed[0 : 3 * planes // 2, :]
    used = 5 * planes // 2
    message[used : used + 2, :] = jnp.concatenate([diagonal(grams[0]), diagonal(grams[1])], axis=0)
    message[used + 2 : used + 8, :] = packed[3 * planes // 2 : 3 * planes // 2 + 6, :]
    if message.shape[0] > used + 8:
        message[used + 8 :, :] = jnp.zeros((message.shape[0] - used - 8, planes), jnp.float32)
    mine, other = half_starts(keep.shape[0])
    keep[...] = message[pl.ds(mine, keep.shape[0]), :]
    give[...] = message[pl.ds(other, keep.shape[0]), :]


def assemble_kernel(rows, planes, f, inner, border, out):
    odd = lax.axis_index("gy") % 2 == 1

    def plane_of(y, at):
        if 2 <= y < rows - 2:
            return inner[f, y - 2, at, :]
        layer = y % (rows - 2)
        beside_near = odd if y < 2 else ~odd
        return jnp.where(beside_near, inner[f, rows - 4 + layer, at, :], border[f, layer, at, :])

    @pl.loop(0, planes // 8)
    def _(t):
        at = pl.ds(pl.multiple_of(t * 8, 8), 8)
        for base in range(0, rows, 8):
            block = jnp.stack([plane_of(y, at) for y in range(base, base + 8)], axis=0)
            out[at, base : base + 8, :] = jnp.swapaxes(block, 0, 1)


def splat(tile, j):
    return jnp.broadcast_to(tile[j : j + 1, :], tile.shape)

def spread_column(tile, at):
    return jnp.broadcast_to(tile[:, at : at + 1], tile.shape)


def thirds_of(values):
    high = values.astype(jnp.bfloat16).astype(jnp.float32)
    rest = values - high
    middle = rest.astype(jnp.bfloat16).astype(jnp.float32)
    return high, middle, rest - middle


def eliminate(rows, first, width):
    count, size = rows[0].shape
    sub = lax.broadcasted_iota(jnp.int32, (count, size), 0)
    lane = lax.broadcasted_iota(jnp.int32, (count, size), 1)
    head = width // count
    tall = len(rows)
    made = [[spread_column(rows[t], first + j) for j in range(width)] for t in range(tall)]
    spread = [[made[t][j] for t in range(tall)] for j in range(width)]
    rows = list(rows)
    results = [jnp.zeros((count, size), jnp.float32)] * head
    entries = {}
    pivot = splat(spread[0][0], 0)
    for j in range(width):
        t0, s0 = divmod(j, count)
        inverse = 1.0 / pivot
        for m in range(j + 1, width):
            entries[j, m] = splat(spread[j][m // count], m % count)
        if j + 1 < width:
            t1, s1 = divmod(j + 1, count)
            following = splat(spread[j + 1][t1], s1) - (entries[j, j + 1] * entries[j, j + 1]) * inverse
        row = splat(rows[t0], s0)
        results[t0] = jnp.where(sub == s0, row * lax.rsqrt(pivot), results[t0])
        for t in range(t0, tall):
            scaled = spread[j][t] * inverse
            for m in range(j + 1, width):
                spread[m][t] = spread[m][t] - scaled * entries[j, m]
            rows[t] = rows[t] - scaled * row
        if j + 1 < width:
            pivot = following
    results = [jnp.where(lane >= first + t * count + sub, results[t], 0.0) for t in range(head)]
    return results, rows[head:]


def factor_tiles(tiles, widths):
    count = tiles[0].shape[0]
    tiles = list(tiles)
    out = []
    first = 0
    for i, width in enumerate(widths):
        top, after = first // count, (first + width) // count
        end = after + sum(widths[i + 1 : i + 3]) // count
        results, tiles[after:end] = eliminate(tiles[top:end], first, width)
        out += results
        if end < len(tiles):
            high, middle, low = thirds_of(jnp.concatenate(results, axis=0))
            one = jnp.concatenate([high, high, middle, high, low, middle], axis=0).astype(jnp.bfloat16)
            two = jnp.concatenate([high, middle, high, low, high, middle], axis=0).astype(jnp.bfloat16)
            update = lax.dot_general(one, two, (((0,), (0,)), ((), ())), preferred_element_type=jnp.float32)
            for t in range(end, len(tiles)):
                tiles[t] = tiles[t] - update[t * count : (t + 1) * count, :]
        first += width
    return out


def factor_kernel(cells, planes, kept, given, factor, message):
    mine, other = half_starts(kept.shape[0])
    message[pl.ds(mine, kept.shape[0]), :] = kept[...]
    message[pl.ds(other, kept.shape[0]), :] = given[...]
    row, col = halves(planes)
    eye = row == col
    diagonals = message[5 * planes // 2 : 5 * planes // 2 + 8, :]
    squares = jnp.broadcast_to(jnp.sum(diagonals, axis=1, keepdims=True), diagonals.shape)
    scales = 1.0 / (5.0 * cells * (squares / (planes * cells) + 1e-06))
    scaled = diagonals * scales
    scale = [scales[i : i + 1, :] for i in range(5)]

    def pair(packed, first):
        return jnp.where(row > col, packed * scale[first], packed * scale[first + 1])

    folded = unfold(message[2 * planes : 5 * planes // 2, :])
    triangles = jnp.where(eye, 0.0, pair(message[0:planes, :], 0) + pair(message[planes : 2 * planes, :], 2))
    triangles = triangles + folded * scale[4]
    cross = triangles + triangles.T + jnp.where(eye, jnp.sum(scaled[0:5], axis=0, keepdims=True), 0.0)
    narrow = planes // 128 * 2
    widths = [8] * narrow + [16] * (planes // 16 - narrow // 2)
    upper = factor_tiles([cross[t : t + 8, :] for t in range(0, planes, 8)], widths)
    factor[...] = jnp.concatenate(upper, axis=0).T


def cost(microseconds):
    return pl.CostEstimate(flops=0, bytes_accessed=int(microseconds * 3.69e6), transcendentals=0)


AXES = ("gy", "gz")


def exchange(values, even, odd):
    count_z = lax.axis_size("gz")
    count = lax.axis_size("gy") * count_z
    return lax.ppermute(values, AXES, [(i, i ^ (odd if i // count_z % 2 else even)) for i in range(count)])


def rounds():
    count_y, count_z = lax.axis_size("gy"), lax.axis_size("gz")
    assert count_y & (count_y - 1) == 0 and count_z & (count_z - 1) == 0
    bits = [count_z << i for i in range(1, count_y.bit_length() - 1)] + [1 << i for i in range(count_z.bit_length() - 1)]
    groups = [bits[i : i + 2] for i in range(0, len(bits), 2)]
    return [[group[0]] if len(group) == 1 else [group[0], group[1], group[0] ^ group[1]] for group in groups]


def add_terms(terms):
    while len(terms) > 1:
        terms = [terms[i] + terms[i + 1] for i in range(0, len(terms), 2)]
    return terms[0]


def f32(*shape):
    return jax.ShapeDtypeStruct(shape, jnp.float32)


def per_device(fields):
    planes = fields.shape[1] - 4
    rows, cols = fields.shape[2], fields.shape[3]
    count_y, count_z = lax.axis_size("gy"), lax.axis_size("gz")

    far = pl.pallas_call(
        functools.partial(far_kernel, rows, planes),
        out_shape=f32(6 * planes + 8, cols),
        in_specs=[pl.BlockSpec(memory_space=pl.ANY)],
        out_specs=VMEM,
        scratch_shapes=[pltpu.SemaphoreType.DMA((2, 3))],
        compiler_params=params(),
        cost_estimate=cost(1),
        name="far_face",
    )(pltpu.with_memory_space_constraint(fields, pltpu.HBM))
    fields, far = lax.optimization_barrier((fields, far))
    far = lax.ppermute(far, "gy", [(i, (i + 1 if i % 2 else i - 1) % count_y) for i in range(count_y)])
    turned, near, behind, ahead = pl.pallas_call(
        functools.partial(faces_kernel, rows, planes),
        out_shape=(
            pltpu.VMEM((3, rows, planes + 4, cols), jnp.float32),
            f32(2, 3, planes, cols),
            f32(planes, cols),
            f32(planes, cols),
        ),
        in_specs=[VMEM],
        out_specs=(VMEM,) * 4,
        scratch_shapes=[pltpu.VMEM((planes + 4, cols), jnp.float32)] * 2,
        compiler_params=params(),
        cost_estimate=cost(2.5),
        name="faces",
    )(pltpu.with_memory_space_constraint(fields, pltpu.VMEM))
    near = lax.ppermute(near, "gy", [(i, i ^ 1) for i in range(count_y)])
    left = lax.ppermute(ahead, "gz", [(i, (i + 1) % count_z) for i in range(count_z)])
    right = lax.ppermute(behind, "gz", [(i, (i - 1) % count_z) for i in range(count_z)])

    inner_rows = [pltpu.VMEM((rows - 4, planes, cols), jnp.float32)] * 4
    velocity, own_z, *planar = pl.pallas_call(
        functools.partial(inner_kernel, rows, planes),
        out_shape=(f32(3, planes, planes), pltpu.VMEM((3, rows, planes, cols), jnp.float32), *inner_rows),
        in_specs=[VMEM],
        out_specs=(VMEM,) * 6,
        scratch_shapes=[
            pltpu.VMEM((rows, planes, 3 * cols), jnp.bfloat16),
            pltpu.VMEM((3 * cols, cols), jnp.bfloat16),
        ],
        compiler_params=params(),
        cost_estimate=cost(3),
        name="inner",
    )(turned)
    pieces = pltpu.VMEM((2, 2, 2 * planes, 2 * cols), jnp.bfloat16)
    inner, part, beside, packed = pl.pallas_call(
        functools.partial(interior_kernel, rows, planes),
        out_shape=(
            f32(2, rows - 2, planes, cols),
            f32(2, 2 * planes, 2 * planes),
            pltpu.VMEM((2, 2, 3, planes, cols), jnp.float32),
            f32(3 * planes // 2 + 8, planes),
        ),
        in_specs=[VMEM] * 10,
        out_specs=(VMEM,) * 4,
        scratch_shapes=[pieces, pltpu.VMEM((planes, cols), jnp.float32), pltpu.VMEM((planes, cols), jnp.float32)],
        compiler_params=params(),
        cost_estimate=cost(0),
        name="interior",
    )(turned, own_z, *planar, near, left, right, velocity)
    half = -(-(5 * planes // 2 + 8) // 16) * 8
    message = pltpu.VMEM((2 * half, planes), jnp.float32)
    border, keep, give = pl.pallas_call(
        functools.partial(border_kernel, rows, planes),
        out_shape=(f32(2, 2, planes, cols), f32(half, planes), f32(half, planes)),
        in_specs=[VMEM] * 5,
        out_specs=(VMEM, VMEM, VMEM),
        scratch_shapes=[message, pltpu.VMEM((2, 2 * planes, 2 * cols), jnp.bfloat16)],
        compiler_params=params(),
        cost_estimate=cost(0.7),
        name="border",
    )(turned, far, beside, part, packed)
    enstrophy, strain_rate = [
        pl.pallas_call(
            functools.partial(assemble_kernel, rows, planes, f),
            out_shape=f32(planes, rows, cols),
            in_specs=[VMEM] * 2,
            out_specs=VMEM,
            compiler_params=params(),
            cost_estimate=cost(1),
            name="assemble",
        )(inner, border)
        for f in range(2)
    ]
    core = count_z
    kept = keep + exchange(give, core, core)
    masks = rounds()
    outputs = [enstrophy, strain_rate]
    for i, (even, odd) in enumerate(zip(masks, masks[::-1])):
        kept = add_terms([kept] + [exchange(kept, *pair) for pair in zip(even, odd)])
        if i < len(outputs):
            kept, outputs[i] = lax.optimization_barrier((kept, outputs[i]))
    enstrophy, strain_rate = outputs
    given = exchange(kept, core, core)
    cells = rows * cols * count_y * count_z
    factor = pl.pallas_call(
        functools.partial(factor_kernel, float(cells), planes),
        out_shape=f32(planes, planes),
        in_specs=[VMEM] * 2,
        out_specs=VMEM,
        scratch_shapes=[message],
        compiler_params=params(),
        cost_estimate=cost(6),
        name="factor",
    )(kept, given)
    return (enstrophy, strain_rate, factor)


def solution(mesh):
    return jax.shard_map(
        per_device,
        mesh=mesh,
        in_specs=(P(None, None, "gy", "gz"),),
        out_specs=(P(None, "gy", "gz"), P(None, "gy", "gz"), P()),
        check_vma=False,
    )
```
